32 devices in a mesh: seq: 8 (over z, y), exp: 4 (over x, core).
Axes of the slice: x: 2, y: 2, z: 4, core: 2. Of those that a mesh axis runs over, the one named last changes fastest.
Arguments:
- residual: bfloat16 [1024, 6144], P('exp', 'seq'), may hold values from -8 to 8
- query: bfloat16 [1024, 8192], P('seq', 'exp'), may hold values from -6 to 6
- key_in: bfloat16 [1024, 8192], P('seq', 'exp'), may hold values from -6 to 6
- value_in: bfloat16 [1024, 8192], P('seq', 'exp'), may hold values from -0.75 to 0.75
- gate_in: bfloat16 [1024, 8192], P('seq', 'exp'), may hold values from -6 to 6
- log_decay: float32 [1024, 64], P('seq', 'exp'), may hold values from -2 to 0
- state_in: float32 [64, 128, 128], P('exp'), may hold values from -12 to 12
- attn_gain: float32 [8192], P('exp'), may hold values from 0.1 to 1.9
- w_out: bfloat16 [8192, 6144], P('exp', 'seq'), may hold values from -0.0625 to 0.0625
- moe_gain: float32 [6144], P('seq'), may hold values from 0.1 to 1.9
- router: float32 [6144, 32], P('seq'), may hold values from -0.078125 to 0.078125
- w_gate: bfloat16 [4, 9216, 6144], P('exp', 'seq'), may hold values from -0.078125 to 0.078125
- w_up: bfloat16 [4, 9216, 6144], P('exp', 'seq'), may hold values from -0.078125 to 0.078125
- w_down: bfloat16 [4, 9216, 6144], P('exp', None, 'seq'), may hold values from -0.09375 to 0.09375
- expert_ids: int32 [1024, 2], P('exp'), may hold values from 0 to 31, all different within a row; in each aligned block of 256 rows (0 to 255, 256 to 511, ...) at most 20 rows name the same one
- keep_counts: int32 [32], replicated, may hold values from 16 to 79
Outputs:
- layer_out: bfloat16 [1024, 6144], P('exp', 'seq')
- final_state: float32 [64, 128, 128], P('exp', 'seq')
The draws below stay inside these ranges and needn't reach their ends.
Inputs may be any that keep to these rules, and one draw needn't show every extreme that they name: `expert_ids`: each row names 2 different experts. Among the rows of one device no expert is named more than 20 times, a bound that some block reaches.
All inputs are finite; a program needn't handle non-finite values.
Results may differ from the reference program's by a relative error of at most 0.014.
Values may be sent and summed in bfloat16 or wider, within the bound.
No kernel may reach another device: no remote copies, remote signals or barrier semaphores. Data moves between devices by JAX's collectives and lax.ppermute only.
A program may use at most 128 MiB of HBM per device.

```python
import math
import jax
import jax.numpy as jnp
import numpy as np
from jax import lax

D = 6144
HEAD_TOTAL = 64
HD = 128
FF = 9216
EXPERTS = 32
TOP = 2
TOK_DEV = 128
TOKEN_TOTAL = 1024
BLOCK = 256
WINDOW = 4
CAP = 20
N_EXP = 4


def draw_residual(key, part):
    random_subkeys = jax.random.split(key, 3)
    column_pos = jnp.arange(D, dtype=jnp.float32) / D
    column_scale = jnp.exp(column_pos * math.log(3.0)) * jnp.exp(jax.random.uniform(random_subkeys[1], (D,), jnp.float32, -0.6, 0.6))
    base_draw = jax.random.normal(random_subkeys[0], (TOKEN_TOTAL, D), jnp.float32)
    row_scale = jnp.exp(jax.random.uniform(random_subkeys[2], (TOKEN_TOTAL, 1), jnp.float32, -0.35, 0.35))
    values = base_draw * row_scale
    return jnp.clip(values * column_scale * 0.4, -8.0, 8.0).astype(jnp.bfloat16)


def draw_log_decay(key, part):
    random_subkeys = jax.random.split(key, 7)
    is_fast = jax.random.bernoulli(random_subkeys[0], 0.5, (1, HEAD_TOTAL))
    slow_rate = jnp.exp(jax.random.uniform(random_subkeys[1], (1, HEAD_TOTAL), jnp.float32, math.log(0.03), math.log(0.3))) / TOKEN_TOTAL
    fast_rate = jax.random.uniform(random_subkeys[2], (1, HEAD_TOTAL), jnp.float32, 1.0 / 50.0, 1.0 / 30.0)
    baseline_decay_rate = jnp.where(is_fast, fast_rate, slow_rate)
    blocks = TOKEN_TOTAL // TOK_DEV
    block_multiplier = jnp.exp(jax.random.uniform(random_subkeys[3], (blocks, 1, HEAD_TOTAL), jnp.float32, -math.log(2.0), math.log(2.0)))
    block_multiplier = jnp.broadcast_to(block_multiplier, (blocks, TOK_DEV, HEAD_TOTAL)).reshape(TOKEN_TOTAL, HEAD_TOTAL)
    random_perturbation = jnp.exp(jax.random.uniform(random_subkeys[4], (TOKEN_TOTAL, HEAD_TOTAL), jnp.float32, -math.log(1.4), math.log(1.4)))
    spike_positions = jax.random.randint(random_subkeys[5], (2, HEAD_TOTAL), 0, TOKEN_TOTAL)
    spike_strength = jax.random.uniform(random_subkeys[6], (2, HEAD_TOTAL), jnp.float32, math.log(0.5), math.log(0.8))
    spike_flags = (jnp.arange(TOKEN_TOTAL)[:, None, None] == spike_positions[None, :, :]).astype(jnp.float32)
    spike_events = jnp.sum(spike_flags * spike_strength[None], axis=1)
    return -baseline_decay_rate * block_multiplier * random_perturbation + spike_events


def place_ends(drawn, own_key, smallest, largest):
    spot = [jax.random.randint(jax.random.fold_in(own_key, axis), (), 0, length) for axis, length in enumerate(drawn.shape)]
    longest = drawn.shape.index(max(drawn.shape))
    next_to = spot[:longest] + [(spot[longest] + 1) % drawn.shape[longest]] + spot[longest + 1:]
    return drawn.at[tuple(spot)].set(smallest).at[tuple(next_to)].set(largest)


def spiked(array, stream_key, source, target, shards_of, factor):
    def block_of(position):
        return (jnp.arange(array.shape[position]) // (array.shape[position] // shards_of)).reshape((-1,) + (1,) * (array.ndim - 1 - position))

    near = jax.random.permutation(stream_key, shards_of)[block_of(target)]
    far = (block_of(target) + shards_of // 2) % shards_of
    return jnp.where((block_of(source) == near) | (block_of(source) == far), factor * array, array)


def shard_levels(rng, dims, pieces, low, largest):
    loudness = 1.0
    for axis_at, blocks in pieces:
        steps = jax.random.uniform(jax.random.fold_in(jax.random.fold_in(rng, 6), axis_at), (blocks,), jnp.float32, low / len(pieces), largest / len(pieces))
        loudness = loudness * jnp.repeat(jnp.exp(steps), dims[axis_at] // blocks).reshape((-1,) + (1,) * (len(dims) - 1 - axis_at))
    return loudness


def deal_out(stream_key, own, number, rows, number_of, top, reach, lean):
    ranking = jax.random.permutation(stream_key, number_of)
    packed, ordinary = portions_of(number_of, rows * top, reach, lean, True), portions_of(number_of, rows * top, reach, lean, False)
    places = jnp.arange(number_of)

    def named(sizes, turn):
        used = int((sizes > 0).sum())
        fixed = max(1, used // 4)
        moved = fixed + (places - fixed + turn * (used - fixed)) % max(1, number_of - fixed)
        return jnp.zeros((number_of,), jnp.int32).at[ranking[jnp.where(places < fixed, places, moved)]].set(jnp.asarray(sizes, jnp.int32))

    sizes = jnp.where(number % 4 == 0, named(packed, number // 4), named(ordinary, number - number // 4 - 1))
    mixed = jax.random.permutation(jax.random.fold_in(own, 3), number_of)
    donor, taker = mixed[0:number_of // 2 * 2:2], mixed[1:number_of // 2 * 2:2]
    slack = jnp.minimum(sizes[donor] - 1, reach - sizes[taker]) // 2
    slack = jnp.where((donor == ranking[0]) | (taker == ranking[0]) | (sizes[taker] == 0), 0, jnp.maximum(slack, 0))
    moved = jax.random.randint(jax.random.fold_in(own, 4), (number_of // 2,), 0, 1 << 20) % (slack + 1)
    sizes = sizes.at[donor].add(-moved).at[taker].add(moved)
    labels = jnp.searchsorted(jnp.cumsum(sizes), jnp.arange(rows * top), side="right").astype(jnp.int32)
    listing = labels.reshape(top, rows).T
    listing = listing[jax.random.permutation(jax.random.fold_in(own, 1), rows)]
    turn = jax.random.randint(jax.random.fold_in(own, 2), (rows, 1), 0, top)
    return jnp.take_along_axis(listing, (jnp.arange(top)[None, :] + turn) % top, axis=1)


def portions_of(amount, total, bound, lean, full):
    weights = [(1 << 20) // math.isqrt(grade ** lean) + 1 for grade in range(1, amount + 1)]
    largest = bound if full else min(bound, max(-(-total // amount), total * weights[0] // sum(weights)))
    least = 1 if total - largest >= amount - 1 else 0
    given, spare = [largest] + [least] * (amount - 1), total - largest - least * (amount - 1)
    while spare > 0:
        candidates = [i for i in range(1, amount) if given[i] < largest] or [i for i in range(1, amount) if given[i] < bound]
        mass, remaining = sum([weights[i] for i in candidates]), spare
        for i in candidates:
            addition = min(bound - given[i], max(1, remaining * weights[i] // mass), spare)
            given[i] = given[i] + addition
            spare = spare - addition
    return np.array(given)


def gaussian(key, dims, deviation, bound, cuts=(), kind=jnp.bfloat16):
    values = deviation * jax.random.normal(key, dims, jnp.float32)
    if cuts:
        values = values * shard_levels(key, dims, cuts, -0.22, 0.18)
    return jnp.clip(values, -bound, bound).astype(kind)


def bell_draw_with(rng, dims, scale, bound, shards, heavy, held_as=jnp.bfloat16):
    result = scale * jax.random.normal(rng, dims, jnp.float32)
    if shards:
        result = result * shard_levels(rng, dims, shards, -0.22, 0.18)
    return jnp.clip(spiked(result, jax.random.fold_in(rng, 3), *heavy), -bound, bound).astype(held_as)


def setup_inputs(seed: int = 0) -> dict:
    seeds = jax.random.split(jax.random.key(seed), 17)
    residual = draw_residual(jax.random.fold_in(seeds[16], 71), 0)
    query = gaussian(seeds[1], (TOKEN_TOTAL, HEAD_TOTAL * HD), 1.0, 6.0, ((0, 8), (1, 4)))
    key_in = gaussian(seeds[2], (TOKEN_TOTAL, HEAD_TOTAL * HD), 1.0, 6.0, ((0, 8), (1, 4)))
    value_in = gaussian(seeds[3], (TOKEN_TOTAL, HEAD_TOTAL * HD), 0.125, 0.75, ((0, 8), (1, 4)))
    gate_in = gaussian(seeds[4], (TOKEN_TOTAL, HEAD_TOTAL * HD), 1.0, 6.0, ((0, 8), (1, 4)))
    log_decay = draw_log_decay(jax.random.fold_in(seeds[16], 71), 0)
    state_in = gaussian(seeds[6], (HEAD_TOTAL, HD, HD), 2.0, 12.0, ((0, 4),), jnp.float32)
    attn_gain = jnp.clip(1.0 + 0.18 * jax.random.normal(seeds[7], (HEAD_TOTAL * HD,), jnp.float32), 0.1, 1.9)
    w_out = gaussian(seeds[8], (HEAD_TOTAL * HD, D), (HEAD_TOTAL * HD) ** -0.5, 0.0625, ((0, 4), (1, 8)))
    moe_gain = jnp.clip(1.0 + 0.18 * jax.random.normal(seeds[9], (D,), jnp.float32), 0.1, 1.9)
    router = gaussian(seeds[10], (D, EXPERTS), D ** -0.5, 0.078125, ((0, 8),), jnp.float32)
    w_gate = gaussian(seeds[11], (WINDOW, FF, D), D ** -0.5, 0.078125, ((0, 4), (1, 8)))
    w_up = gaussian(seeds[12], (WINDOW, FF, D), D ** -0.5, 0.078125, ((0, 4), (1, 8)))
    w_down = bell_draw_with(seeds[13], (WINDOW, FF, D), FF ** -0.5, 0.09375, ((0, 4), (2, 8)), (1, 2, 8, 2.0))
    expert_ids_keys = jax.random.split(jax.random.fold_in(seeds[14], 1), TOKEN_TOTAL // BLOCK)
    expert_ids_turns = jax.random.permutation(jax.random.fold_in(seeds[14], 3), TOKEN_TOTAL // BLOCK)
    expert_ids = jax.vmap(lambda own, number: deal_out(jax.random.fold_in(seeds[14], 2), own, number, BLOCK, EXPERTS, TOP, CAP, 1))(expert_ids_keys, expert_ids_turns).reshape((TOKEN_TOTAL, TOP))
    keep_counts = place_ends(jax.random.randint(seeds[15], (EXPERTS,), TOKEN_TOTAL * TOP // (4 * EXPERTS), 5 * TOKEN_TOTAL * TOP // (4 * EXPERTS)), jax.random.fold_in(seeds[15], 1), TOKEN_TOTAL * TOP // (4 * EXPERTS), (5 * TOKEN_TOTAL * TOP // (4 * EXPERTS)) - 1).astype(jnp.int32)
    return dict(residual=residual, query=query, key_in=key_in, value_in=value_in, gate_in=gate_in, log_decay=log_decay, state_in=state_in, attn_gain=attn_gain, w_out=w_out, moe_gain=moe_gain, router=router, w_gate=w_gate, w_up=w_up, w_down=w_down, expert_ids=expert_ids, keep_counts=keep_counts)


epsilon = 1e-05
highest = lax.Precision.HIGHEST

def block_terms(act_query, act_key, val_rows, log_rows):
    running_log = jnp.cumsum(log_rows, axis=0)
    block_log = running_log[-1]
    length = log_rows.shape[0]
    causal_mask = (jnp.arange(length)[:, None] >= jnp.arange(length)[None, :])[None]
    flipped = jnp.transpose(running_log)
    log_gap = flipped[:, :, None] - flipped[:, None, :]
    decay_rows = jnp.where(causal_mask, jnp.exp(jnp.where(causal_mask, log_gap, 0.0)), 0.0)
    scores = jnp.einsum('thd,shd->hts', act_query, act_key, precision=highest)
    local_part = jnp.einsum('hts,shd->thd', scores * decay_rows, val_rows, precision=highest)
    tail_decay = jnp.exp(block_log[None, :] - running_log)
    update = jnp.einsum('shd,she->hde', act_key * tail_decay[:, :, None], val_rows, precision=highest)
    return (local_part, running_log, block_log, update)

def from_state(act_query, running_log, state_carry):
    return jnp.einsum('thd,hde->the', act_query * jnp.exp(running_log)[:, :, None], state_carry, precision=highest)

def reference(residual, query, key_in, value_in, gate_in, log_decay, state_in, attn_gain, w_out, moe_gain, router, w_gate, w_up, w_down, expert_ids, keep_counts):
    act_query = jax.nn.silu(query.astype(jnp.float32)).reshape(TOKEN_TOTAL, HEAD_TOTAL, HD)
    act_key = jax.nn.silu(key_in.astype(jnp.float32)).reshape(TOKEN_TOTAL, HEAD_TOTAL, HD)
    val_rows = value_in.astype(jnp.float32).reshape(TOKEN_TOTAL, HEAD_TOTAL, HD)
    blocks = TOKEN_TOTAL // TOK_DEV

    def block_step(state_carry, portions):
        query_block, key_block, value_block, log_block = portions
        local_part, running_log, block_log, update = block_terms(query_block, key_block, value_block, log_block)
        outputs = local_part + from_state(query_block, running_log, state_carry)
        state_next = jnp.exp(block_log)[:, None, None] * state_carry + update
        return (state_next, outputs)
    last_state, outputs = lax.scan(block_step, state_in, (act_query.reshape(blocks, TOK_DEV, HEAD_TOTAL, HD), act_key.reshape(blocks, TOK_DEV, HEAD_TOTAL, HD), val_rows.reshape(blocks, TOK_DEV, HEAD_TOTAL, HD), log_decay.reshape(blocks, TOK_DEV, HEAD_TOTAL)))
    outputs = outputs.reshape(TOKEN_TOTAL, HEAD_TOTAL, HD)
    square_mean = lax.optimization_barrier(jnp.mean(outputs * outputs, axis=2, keepdims=True))
    normed = outputs * lax.rsqrt(square_mean + epsilon) * attn_gain.reshape(HEAD_TOTAL, HD)
    heads_mixed = (normed.reshape(TOKEN_TOTAL, HEAD_TOTAL * HD) * jax.nn.sigmoid(gate_in.astype(jnp.float32))).astype(jnp.bfloat16)
    after_attn = residual.astype(jnp.float32) + jnp.dot(heads_mixed, w_out, preferred_element_type=jnp.float32)
    model_mean = lax.optimization_barrier(jnp.mean(after_attn * after_attn, axis=1, keepdims=True))
    scaled = after_attn * lax.rsqrt(model_mean + epsilon) * moe_gain
    routed_in = scaled.astype(jnp.bfloat16)
    logits = jnp.dot(scaled, router, precision=highest)
    chosen = jnp.take_along_axis(logits, expert_ids, axis=1)
    gate_probs = jnp.stack([jax.nn.sigmoid(chosen[:, 0] - chosen[:, 1]), jax.nn.sigmoid(chosen[:, 1] - chosen[:, 0])], axis=1)
    flat_ids = expert_ids.reshape(TOKEN_TOTAL * TOP)
    onehot = (flat_ids[:, None] == jnp.arange(WINDOW, dtype=jnp.int32)[None, :]).astype(jnp.int32)
    global_rank = lax.optimization_barrier(jnp.sum((jnp.cumsum(onehot, axis=0) - onehot) * onehot, axis=1)).astype(jnp.int32)
    grouped = onehot.reshape(N_EXP, BLOCK * TOP, WINDOW)
    local_rank = lax.optimization_barrier(jnp.sum(((jnp.cumsum(grouped, axis=1) - grouped) * grouped).reshape(TOKEN_TOTAL * TOP, WINDOW), axis=1)).astype(jnp.int32)
    in_window = flat_ids < WINDOW
    safe_ids = jnp.where(in_window, flat_ids, 0).astype(jnp.int32)
    is_kept = in_window & (global_rank < keep_counts[safe_ids])
    order = jnp.arange(TOKEN_TOTAL * TOP, dtype=jnp.int32)
    slot_index = (order // (BLOCK * TOP) * CAP + local_rank).astype(jnp.int32)
    target = jnp.where(in_window, flat_ids, WINDOW).astype(jnp.int32)
    slot_tokens = jnp.zeros((WINDOW, N_EXP * CAP), jnp.int32).at[target, slot_index].set((order // TOP).astype(jnp.int32), mode='drop')

    def expert(portions):
        gate_rows, up_rows, down_rows, token_rows = portions
        chosen_rows = routed_in[token_rows]
        gate_val = jnp.dot(chosen_rows, gate_rows.T, preferred_element_type=jnp.float32)
        up_val = jnp.dot(chosen_rows, up_rows.T, preferred_element_type=jnp.float32)
        hidden = (jax.nn.silu(gate_val) * up_val).astype(jnp.bfloat16)
        return jnp.dot(hidden, down_rows, preferred_element_type=jnp.float32).astype(jnp.bfloat16)
    expert_out = lax.map(expert, (w_gate, w_up, w_down, slot_tokens))
    flat_out = expert_out.reshape(WINDOW * N_EXP * CAP, D)
    flat_index = jnp.where(is_kept, safe_ids * (N_EXP * CAP) + slot_index, 0).astype(jnp.int32)
    picked = flat_out[flat_index].astype(jnp.float32).reshape(TOKEN_TOTAL, TOP, D)
    weight = jnp.where(is_kept.reshape(TOKEN_TOTAL, TOP), gate_probs, 0.0)
    expert_sum = lax.optimization_barrier(jnp.sum(picked * weight[:, :, None], axis=1))
    return ((after_attn + expert_sum).astype(jnp.bfloat16), last_state)
```

```python
import functools
import jax
import jax.numpy as jnp
from jax import lax
from jax.experimental import pallas as pl
from jax.experimental.pallas import tpu as pltpu
from jax.sharding import PartitionSpec as P

EPS = 1e-05
F32 = jnp.float32
BF16 = jnp.bfloat16
I32 = jnp.int32
HIGHEST = lax.Precision.HIGHEST
NT = (((1,), (1,)), ((), ()))
TN = (((0,), (0,)), ((), ()))
NN = (((1,), (0,)), ((), ()))


def mm(a, b, dims=NN, precision=None):
    return lax.dot_general(a, b, dims, precision=precision, preferred_element_type=F32)


def sigmoid(v):
    return 1.0 / (1.0 + jnp.exp(-v))


def bit_reversed(p, bits):
    r = 0
    for b in range(bits):
        r = r * 2 + ((p >> b) & 1)
    return r


def whole(shape):
    return pl.BlockSpec(tuple(shape), lambda i, s: (0,) * len(shape))


def call(kernel, place, operands, outs, scratch=(), flops=0, limit=40):
    arrays, specs, moved = [], [], 0
    for item in operands:
        array, spec = item if isinstance(item, tuple) else (item, whole(item.shape))
        arrays.append(array)
        specs.append(spec)
        moved += array.size * array.dtype.itemsize
    moved += sum(o.size * o.dtype.itemsize for o in outs)
    return pl.pallas_call(
        kernel,
        out_shape=list(outs),
        grid_spec=pltpu.PrefetchScalarGridSpec(
            num_scalar_prefetch=1,
            grid=(1,),
            in_specs=specs,
            out_specs=[whole(o.shape) for o in outs],
            scratch_shapes=list(scratch),
        ),
        compiler_params=pltpu.CompilerParams(vmem_limit_bytes=limit * 1024 * 1024),
        cost_estimate=pl.CostEstimate(flops=flops, bytes_accessed=moved, transcendentals=0),
    )(place, *arrays)


def sds(shape, dtype):
    return jax.ShapeDtypeStruct(tuple(shape), dtype)


def pieces(x):
    hi = x.astype(BF16)
    rest = x - hi.astype(F32)
    mid = rest.astype(BF16)
    return hi, mid, (rest - mid.astype(F32)).astype(BF16)


def pack_kernel(s, k, v, q, g, kv, qg):
    kv[0] = k[...]
    kv[1] = v[...]
    qg[0] = q[...]
    qg[1] = g[...]


def update_kernel(nz, ny, heads, hd, s, *refs):
    z, y = s[0], s[1]
    n = ny - 1
    k_own, v_own = refs[0], refs[1]
    kv = refs[2 : 2 + n]
    logs = refs[2 + n : 2 + n + ny]
    outs = refs[2 + n + ny : 2 + n + ny + nz]
    c_row, c_col, log_all, state, tail = refs[2 + n + ny + nz :]
    tok = k_own.shape[0]
    total_tok = tok * ny
    share = hd // nz
    for d in range(ny):
        at = pl.multiple_of(lax.rem(y + ny - d, ny) * tok, tok)
        log_all[:, pl.ds(at, tok)] = logs[d][...]
    rows = lax.broadcasted_iota(I32, (total_tok, total_tok), 0)
    cols = lax.broadcasted_iota(I32, (total_tok, total_tok), 1)
    c_row[...] = mm(log_all[...], (rows <= cols).astype(F32), precision=HIGHEST)
    c_col[...] = mm((rows >= cols).astype(F32), log_all[...], NT, precision=HIGHEST)
    total = c_row[:, total_tok - 1 : total_tok]
    for h in range(heads):
        add = None
        for d in range(ny):
            at = pl.multiple_of(lax.rem(y + ny - d, ny) * tok, tok)
            lanes = slice(h * hd, (h + 1) * hd)
            key = (k_own[:, lanes] if d == 0 else kv[d - 1][0, :, lanes]).astype(F32)
            val = v_own[:, lanes] if d == 0 else kv[d - 1][1, :, lanes]
            decay = jnp.exp(total[h : h + 1, :] - c_col[pl.ds(at, tok), h : h + 1])
            weighted = (key * sigmoid(key) * decay).astype(BF16)
            part = mm(weighted, val, TN)
            add = part if add is None else add + part
        state[h] = add.astype(BF16)
    tail[...] = jnp.zeros_like(tail)
    hi, mid, lo = pieces(total)
    lane = lax.broadcasted_iota(I32, (heads, hd), 1)
    tail[0:heads, :] = jnp.where(
        lane == 0,
        hi.astype(F32),
        jnp.where(lane == 1, mid.astype(F32), jnp.where(lane == 2, lo.astype(F32), 0.0)),
    )
    for d in range(nz):
        at = pl.multiple_of(lax.rem(z + d, nz) * share, share)
        for h in range(heads):
            outs[d][h * share : (h + 1) * share, :] = state[h, pl.ds(at, share), :]
        outs[d][heads * share :, :] = tail[...].astype(BF16)


def prefix_kernel(nz, heads, hd, s, *refs):
    z = s[0]
    parts = refs[:nz]
    start = refs[nz]
    outs = refs[nz + 1 : 2 * nz + 1]
    final, held, entering, run = refs[2 * nz + 1 :]
    share = hd // nz
    for d in range(nz):
        held[lax.rem(z + nz - d, nz)] = parts[d][...]
    run[...] = start[...]
    for p in range(nz):
        logs = jnp.sum(held[p, heads * share :, :].astype(F32), axis=1, keepdims=True)
        keep = jnp.exp(logs)
        for h in range(heads):
            rows = slice(h * share, (h + 1) * share)
            now = run[h]
            entering[p, rows, :] = now.astype(BF16)
            run[h] = keep[h : h + 1, :] * now + held[p, rows, :].astype(F32)
    final[...] = run[...]
    for d in range(nz):
        outs[d][...] = entering[lax.rem(z + d, nz)]


def attention_kernel(nz, ny, heads, hd, s, *refs):
    z, y = s[0], s[1]
    n = ny - 1
    own = refs[:4]
    kv = refs[4 : 4 + n]
    qg = refs[4 + n : 4 + 2 * n]
    states = refs[4 + 2 * n : 4 + 2 * n + nz]
    c_row, c_col, gain, ids, tok_ids, out, chosen, qs, ks, vs, gs, state = refs[4 + 2 * n + nz :]
    tok = own[0].shape[0]
    total_tok = tok * ny
    share = hd // nz
    for d in range(ny):
        at = pl.ds(pl.multiple_of(lax.rem(y + ny - d, ny) * tok, tok), tok)
        ks[at, :] = own[0][...] if d == 0 else kv[d - 1][0]
        vs[at, :] = own[1][...] if d == 0 else kv[d - 1][1]
        qs[at, :] = own[2][...] if d == 0 else qg[d - 1][0]
        gs[at, :] = own[3][...] if d == 0 else qg[d - 1][1]
    for d in range(nz):
        at = pl.ds(pl.multiple_of(lax.rem(z + nz - d, nz) * share, share), share)
        for h in range(heads):
            state[h, at, :] = states[d][h * share : (h + 1) * share, :]
    rows = lax.broadcasted_iota(I32, (total_tok, total_tok), 0)
    cols = lax.broadcasted_iota(I32, (total_tok, total_tok), 1)
    causal = rows >= cols
    for h in range(heads):
        lanes = slice(h * hd, (h + 1) * hd)
        query = qs[:, lanes].astype(F32)
        query = query * sigmoid(query)
        key = ks[:, lanes].astype(F32)
        key = (key * sigmoid(key)).astype(BF16)
        col = c_col[:, h : h + 1]
        gap = jnp.where(causal, col - c_row[h : h + 1, :], 0.0)
        decay = jnp.where(causal, jnp.exp(gap), 0.0)
        scores = mm(query.astype(BF16), key, NT) * decay
        att = mm(scores.astype(BF16), vs[:, lanes])
        att = att + mm((query * jnp.exp(col)).astype(BF16), state[h])
        square = jnp.mean(att * att, axis=1, keepdims=True)
        gate = sigmoid(gs[:, lanes].astype(F32))
        out[:, lanes] = (att * lax.rsqrt(square + EPS) * gain[:, lanes] * gate).astype(BF16)
    pick = (ids[...] == tok_ids[0:1, :]) | (ids[...] == tok_ids[1:2, :])
    chosen[...] = mm(pick.astype(F32).astype(BF16), out[...]).astype(BF16)


def project_chosen_kernel(nz, ny, s, *refs):
    count = nz * ny
    blocks = refs[:count]
    weights = refs[count : count + ny]
    row_ids, col_ids, tok_ids, residual, keep, send, stacked = refs[count + ny :]
    rows = blocks[0].shape[0]
    total = None
    for dy in range(ny):
        for dz in range(nz):
            stacked[dz * rows : (dz + 1) * rows, :] = blocks[dy * nz + dz][...]
        part = mm(stacked[...], weights[dy][...])
        total = part if total is None else total + part
    order = (row_ids[...] == col_ids[...]).astype(F32).astype(BF16)
    mine = (row_ids[...] == tok_ids[0:1, :]) | (row_ids[...] == tok_ids[1:2, :])
    result = mm(order, total.astype(BF16)) + mm(mine.astype(F32).astype(BF16), residual[...])
    half = keep.shape[0]
    keep[...] = result[:half, :]
    send[...] = result[half:, :].astype(BF16)


def project_kernel(nz, ny, s, *refs):
    z, j = s[0], s[2]
    bits = nz.bit_length() - 1
    count = nz * ny
    blocks = refs[:count]
    weights = refs[count : count + ny]
    keep, send, stacked, sem = refs[count + ny :]
    rows = blocks[0].shape[0]
    copies = []
    for dy in range(ny):
        for dz in range(nz):
            copies.append(
                pltpu.make_async_copy(
                    blocks[dy * nz + dz], stacked.at[dy, dz], sem.at[dy * nz + dz]
                )
            )
            copies[-1].start()
    for c in copies:
        c.wait()
    for p in range(nz):
        block = lax.bitwise_xor(jnp.int32(bit_reversed(p, bits)), j)
        dz = lax.rem(z + nz - block, nz)
        total = None
        for dy in range(ny):
            part = mm(stacked[dy, dz], weights[dy][...])
            total = part if total is None else total + part
        if p < nz // 2:
            keep[p] = total.astype(BF16)
        else:
            send[p - nz // 2] = total.astype(BF16)


def rows_kernel(s, keep, received, gain, router, sign, out):
    width = gain.shape[1]
    rows = keep[...] + received[...].astype(F32)
    square = jnp.sum(rows * rows, axis=1, keepdims=True)
    scaled = rows * gain[...]
    logits = mm(scaled, router[...], precision=HIGHEST)
    gap = jnp.sum(logits * sign[...], axis=1, keepdims=True)
    out[:, :width] = scaled.astype(BF16)
    lane = lax.broadcasted_iota(I32, (rows.shape[0], 128), 1)
    stats = jnp.zeros((rows.shape[0], 128), F32)
    for at, value in ((0, square), (3, gap)):
        for k, piece in enumerate(pieces(value)):
            stats = jnp.where(lane == at + k, piece.astype(F32), stats)
    out[:, width:] = stats.astype(BF16)


def up_kernel(nz, ny, places, first, last, features, s, *refs):
    z, y = s[0], s[1]
    count = len(places)
    blocks = refs[:count]
    refs = refs[count:]
    before = () if first else refs[:3]
    refs = refs[0 if first else 3 :]
    w_gate, w_up = refs[:2]
    outs = refs[2 : 4 if last else 5]
    gate_buf, up_buf, sem = refs[4 if last else 5 :]
    width = gate_buf.shape[2]
    copies = []
    for n, (dz, dy) in enumerate(places):
        source = lax.rem(z + nz - dz, nz) * ny + lax.rem(y + ny - dy, ny)
        at = pl.ds(pl.multiple_of(source * width, 128), width)
        copies.append(
            (
                pltpu.make_async_copy(w_gate.at[0, :, at], gate_buf.at[n], sem.at[0, n]),
                pltpu.make_async_copy(w_up.at[0, :, at], up_buf.at[n], sem.at[1, n]),
            )
        )
        for c in copies[-1]:
            c.start()
    gate, up, stats = (None, None, None) if first else (b[...] for b in before)
    for n in range(count):
        rows = blocks[n][:, :width]
        part = blocks[n][:, width:].astype(F32)
        stats = part if stats is None else stats + part
        copies[n][0].wait()
        part = mm(rows, gate_buf[n], NT)
        gate = part if gate is None else gate + part
        copies[n][1].wait()
        part = mm(rows, up_buf[n], NT)
        up = part if up is None else up + part
    if not last:
        outs[0][...] = gate
        outs[1][...] = up
        outs[2][...] = stats
        return
    square = stats[:, 0:1] + stats[:, 1:2] + stats[:, 2:3]
    gap = stats[:, 3:4] + stats[:, 4:5] + stats[:, 5:6]
    inverse = lax.rsqrt(square / features + EPS)
    gate = gate * inverse
    outs[0][...] = (gate * sigmoid(gate) * (up * inverse)).astype(BF16)
    outs[1][...] = jnp.broadcast_to(sigmoid(gap * inverse), outs[1].shape)


def down_kernel(nz, ny, places, first, last, s, *refs):
    z, y = s[0], s[1]
    count = len(places)
    blocks = refs[:count]
    refs = refs[count:]
    before = None if first else refs[0]
    refs = refs[0 if first else 1 :]
    w_down = refs[0]
    refs = refs[1:]
    if last:
        weight, out_ids, row_ids = refs[:3]
        refs = refs[3:]
    outs, buf, sem = refs[:-2], refs[-2], refs[-1]
    depth = buf.shape[1]
    copies = []
    for n, (dz, dy) in enumerate(places):
        source = lax.rem(z + nz - dz, nz) * ny + lax.rem(y + ny - dy, ny)
        at = pl.ds(pl.multiple_of(source * depth, depth), depth)
        copies.append(pltpu.make_async_copy(w_down.at[0, at, :], buf.at[n], sem.at[n]))
        copies[-1].start()
    total = None if first else before[...]
    for n in range(count):
        copies[n].wait()
        part = mm(blocks[n][...], buf[n])
        total = part if total is None else total + part
    if not last:
        outs[0][...] = total
        return
    result = (total * weight[:, 0:1]).astype(BF16)
    for r, out in enumerate(outs):
        rows = out.shape[0]
        pick = out_ids[r * rows : (r + 1) * rows, :] == row_ids[...]
        out[...] = mm(pick.astype(F32).astype(BF16), result).astype(BF16)


def combine_kernel(count, s, *refs):
    returned = refs[:count]
    keep, received, residual, tok_ids, ret_ids, out, stacked = refs[count:]
    rows = returned[0].shape[0]
    for n in range(count):
        stacked[n * rows : (n + 1) * rows, :] = returned[n][...]
    pick = (tok_ids[:, 0:1] == ret_ids[...]) | (tok_ids[:, 1:2] == ret_ids[...])
    total = residual[...].astype(F32) + (keep[...].astype(F32) + received[...].astype(F32))
    total = total + mm(pick.astype(F32).astype(BF16), stacked[...])
    out[...] = total.astype(BF16)


def local(
    residual,
    query,
    key_in,
    value_in,
    gate_in,
    log_decay,
    state_in,
    attn_gain,
    w_out,
    moe_gain,
    router,
    w_gate,
    w_up,
    w_down,
    expert_ids,
    keep_counts,
):
    nz = lax.axis_size("exp")
    ny = lax.axis_size("seq") // nz
    bits = nz.bit_length() - 1
    i = lax.axis_index("seq").astype(I32)
    j = lax.axis_index("exp").astype(I32)
    z, y = i // ny, i % ny
    place = jnp.stack([z, y, j])

    tok, head_width = query.shape
    head_count, hd = state_in.shape[0], state_in.shape[2]
    heads = head_count // ny
    width = heads * hd
    block, cols = residual.shape
    features = w_gate.shape[2]
    units = w_gate.shape[1]
    experts = router.shape[1]
    cap = 5 * block * nz // (2 * nz * experts)
    slots = nz * cap

    def z_turn(a, d):
        pairs = [(p * ny + q, (p + d) % nz * ny + q) for p in range(nz) for q in range(ny)]
        return lax.ppermute(a, "seq", pairs)

    def y_turn(a, d):
        pairs = [(p * ny + q, p * ny + (q + d) % ny) for p in range(nz) for q in range(ny)]
        return lax.ppermute(a, "seq", pairs)

    def swap(a, r):
        return lax.ppermute(a, "exp", [(p, p ^ r) for p in range(nz)])

    z_order = sorted(range(1, nz), key=lambda d: (min(d, nz - d), d))

    def gather(a):
        held = {(0, 0): a}
        for d in range(1, ny):
            held[0, d] = y_turn(a, d)
        for d in z_order:
            held[d, 0] = z_turn(a, d)
        for d in z_order:
            for e in range(1, ny):
                held[d, e] = y_turn(held[d, 0], e)
        return held

    ids = jnp.transpose(expert_ids)[None]
    for b in range(bits):
        ids = jnp.concatenate([ids, swap(ids, 1 << b)], axis=0)
    ids = jnp.stack([lax.dynamic_index_in_dim(ids, p ^ j, 0, False) for p in range(nz)])
    window = jnp.arange(nz, dtype=I32)
    named = (ids[None, :, 0] == window[:, None, None]) | (ids[None, :, 1] == window[:, None, None])
    strict = (jnp.arange(block)[:, None] < jnp.arange(block)[None, :]).astype(BF16)
    rank = jnp.einsum(
        "ebt,ts->ebs", named.astype(BF16), strict, preferred_element_type=F32
    ).astype(I32)
    counts = jnp.sum(named.astype(I32), axis=2)
    earlier = jnp.sum(
        jnp.where(window[:, None] < window[None, :], 1, 0)[None] * counts[:, :, None], axis=1
    )
    kept = named & (rank + earlier[:, :, None] < keep_counts[:nz][:, None, None])
    code = jnp.where(
        kept, (window[:, None, None] * nz + window[None, :, None]) * cap + rank, -1
    )
    code_a = jnp.max(code, axis=0)
    code_b = jnp.max(jnp.where(code == code_a[None], -1, code), axis=0)
    codes = jnp.stack([code_a, code_b], axis=1)
    codes_z = lax.dynamic_index_in_dim(codes, z, 0, False)
    codes_j = lax.dynamic_index_in_dim(codes, j, 0, False)
    slot = jnp.arange(cap, dtype=I32)

    def number(e, p):
        return (e * nz + p)[..., None] * cap + slot

    back = (z - window) % nz
    col_ids = number(window[None, :], back[:, None]).reshape(nz * slots)
    turned = jnp.array([bit_reversed(p, bits) for p in range(nz)], I32) ^ j
    row_ids = number(turned[:, None], window[None, :]).reshape(nz * slots, 1)
    own_rows = number(j, window).reshape(slots)
    pad = -cap % 16
    ret_rows = slot.shape[0] + pad
    padded = functools.partial(jnp.pad, pad_width=((0, 0), (0, pad)), constant_values=-2)
    out_ids = padded(number(j, window ^ j)).reshape(nz * ret_rows, 1)
    ret_ids = padded(number(window ^ j, j)).reshape(1, nz * ret_rows)
    holds = (own_rows[:, None, None] == code_a[None]) | (own_rows[:, None, None] == code_b[None])
    other = jnp.sum(jnp.where(holds, (ids[:, 0] + ids[:, 1])[None], 0), axis=(1, 2)) - j
    every = jnp.arange(experts, dtype=I32)[None, :]
    sign = (every == j).astype(F32) - (every == other[:, None]).astype(F32)

    here = pl.BlockSpec((tok, width), lambda n, s: (0, s[1]))
    logs_t = jnp.transpose(log_decay)
    logs = [lax.dynamic_slice_in_dim(logs_t, y * heads, heads, 0)]
    kvs, qgs = [], []
    for d in range(1, ny):
        there = pl.BlockSpec((tok, width), lambda n, s, d=d: (0, lax.rem(s[1] + d, ny)))
        kv, qg = call(
            pack_kernel,
            place,
            [(key_in, there), (value_in, there), (query, there), (gate_in, there)],
            [sds((2, tok, width), BF16)] * 2,
        )
        to = (y + d) % ny
        logs.append(y_turn(lax.dynamic_slice_in_dim(logs_t, to * heads, heads, 0), d))
        kvs.append(y_turn(kv, d))
        qgs.append(y_turn(qg, d))
    share = hd // nz
    long = tok * ny
    *parts, c_row, c_col = call(
        functools.partial(update_kernel, nz, ny, heads, hd),
        place,
        [(key_in, here), (value_in, here), *kvs, *logs],
        [sds((heads * share + 16, hd), BF16)] * nz
        + [sds((heads, long), F32), sds((long, heads), F32)],
        [
            pltpu.VMEM((heads, long), F32),
            pltpu.VMEM((heads, hd, hd), BF16),
            pltpu.VMEM((16, hd), F32),
        ],
        flops=2 * long * hd * hd * heads,
    )
    parts = [parts[0]] + [z_turn(parts[d], d) for d in range(1, nz)]
    *entering, last_rows = call(
        functools.partial(prefix_kernel, nz, heads, hd),
        place,
        [*parts, (state_in, pl.BlockSpec((heads, share, hd), lambda n, s: (s[1], s[0], 0)))],
        [sds((heads * share, hd), BF16)] * nz + [sds((heads, share, hd), F32)],
        [
            pltpu.VMEM((nz, heads * share + 16, hd), BF16),
            pltpu.VMEM((nz, heads * share, hd), BF16),
            pltpu.VMEM((heads, share, hd), F32),
        ],
    )
    entering = [entering[0]] + [z_turn(entering[d], d) for d in range(1, nz)]
    mixed, chosen = call(
        functools.partial(attention_kernel, nz, ny, heads, hd),
        place,
        [
            (key_in, here),
            (value_in, here),
            (query, here),
            (gate_in, here),
            *kvs,
            *qgs,
            *entering,
            c_row,
            c_col,
            (attn_gain[None], pl.BlockSpec((1, width), lambda n, s: (0, s[1]))),
            col_ids[:slots, None],
            codes_z,
        ],
        [sds((long, width), BF16), sds((slots, width), BF16)],
        [pltpu.VMEM((long, width), BF16)] * 4 + [pltpu.VMEM((heads, hd, hd), BF16)],
        flops=4 * long * long * width,
    )
    rows = share // ny
    final_rows = jnp.zeros((head_count, rows, hd), F32)
    for d in range(ny):
        sent = lax.dynamic_slice_in_dim(last_rows, (y + d) % ny * rows, rows, 1)
        got = sent if d == 0 else y_turn(sent, d)
        final_rows = lax.dynamic_update_slice_in_dim(
            final_rows, got, (y - d) % ny * heads, 0
        )

    picked = gather(chosen)
    places = [(dz, dy) for dy in range(ny) for dz in range(nz)]
    w_parts = [
        (w_out, pl.BlockSpec((width, cols), lambda n, s, d=d: (lax.rem(s[1] + ny - d, ny), 0)))
        for d in range(ny)
    ]
    keep, send = call(
        functools.partial(project_chosen_kernel, nz, ny),
        place,
        [picked[p] for p in places]
        + w_parts
        + [row_ids, col_ids[None], codes_j, residual],
        [sds((nz * slots // 2, cols), F32), sds((nz * slots // 2, cols), BF16)],
        [pltpu.VMEM((nz * slots, width), BF16)],
        flops=2 * nz * slots * head_width * cols,
    )
    for b in range(bits):
        received = swap(send, 1 << b)
        if b < bits - 1:
            half = keep.shape[0] // 2
            send = (keep[half:] + received[half:].astype(F32)).astype(BF16)
            keep = keep[:half] + received[:half].astype(F32)
    (rows_out,) = call(
        rows_kernel,
        place,
        [keep, received, moe_gain[None], router, sign],
        [sds((slots, cols + 128), BF16)],
    )

    everything = gather(mixed)
    keep_all, send_all = call(
        functools.partial(project_kernel, nz, ny),
        place,
        [(everything[p], pl.BlockSpec(memory_space=pl.ANY)) for p in places] + w_parts,
        [sds((nz // 2, block, cols), BF16)] * 2,
        [pltpu.VMEM((ny, nz, long, width), BF16), pltpu.SemaphoreType.DMA((nz * ny,))],
        flops=2 * nz * long * head_width * cols,
    )
    for b in range(bits):
        received_all = swap(send_all, 1 << b)
        if b < bits - 1:
            half = keep_all.shape[0] // 2
            both = keep_all.astype(F32) + received_all.astype(F32)
            send_all, keep_all = both[half:].astype(BF16), both[:half].astype(BF16)

    groups = [[(0, d) for d in range(ny)], [(d, 0) for d in z_order]]
    groups.append([(d, e) for d in z_order for e in range(1, ny)])
    arrived = gather(rows_out)
    state = []
    if cols % 128:
        order = jnp.stack([(z - dz) % nz * ny + (y - dy) % ny for dz, dy in places])
        at = jnp.argsort(order)
        rows_all = jnp.take(jnp.stack([arrived[p] for p in places]), at, axis=0)
        stats = jnp.sum(rows_all[:, :, cols:].astype(F32), axis=0)
        rows_all = jnp.swapaxes(rows_all[:, :, :cols], 0, 1).reshape(slots, features)
        inverse = lax.rsqrt(jnp.sum(stats[:, :3], axis=1) / features + EPS)[:, None]
        gate = mm(rows_all, w_gate[0], NT) * inverse
        hidden = (gate * sigmoid(gate) * (mm(rows_all, w_up[0], NT) * inverse)).astype(BF16)
        weight = sigmoid(jnp.sum(stats[:, 3:6], axis=1)[:, None] * inverse)
        state = [hidden, jnp.broadcast_to(weight, (slots, 128))]
    for n, group in enumerate(groups if cols % 128 == 0 else ()):
        last = n == len(groups) - 1
        hbm = pl.BlockSpec(memory_space=pl.ANY)
        outs = [sds((slots, units), F32)] * 2 + [sds((slots, 128), F32)]
        if last:
            outs = [sds((slots, units), BF16), sds((slots, 128), F32)]
        state = call(
            functools.partial(up_kernel, nz, ny, group, n == 0, last, features),
            place,
            [arrived[p] for p in group] + list(state) + [(w_gate, hbm), (w_up, hbm)],
            outs,
            [pltpu.VMEM((len(group), units, cols), BF16)] * 2
            + [pltpu.SemaphoreType.DMA((2, len(group)))],
            flops=4 * len(group) * slots * units * cols,
        )
    hidden, weight = state
    arrived = gather(hidden)
    state = []
    for n, group in enumerate(groups):
        last = n == len(groups) - 1
        outs = [sds((slots, cols), F32)]
        if last:
            outs = [sds((ret_rows, cols), BF16)] * nz
        state = call(
            functools.partial(down_kernel, nz, ny, group, n == 0, last),
            place,
            [arrived[p] for p in group]
            + list(state)
            + [(w_down, pl.BlockSpec(memory_space=pl.ANY))]
            + ([weight, out_ids, own_rows[None]] if last else []),
            outs,
            [
                pltpu.VMEM((len(group), units, cols), BF16),
                pltpu.SemaphoreType.DMA((len(group),)),
            ],
            flops=2 * len(group) * slots * units * cols,
        )
    returned = [state[0]] + [swap(state[r], r) for r in range(1, nz)]
    (layer_out,) = call(
        functools.partial(combine_kernel, nz),
        place,
        returned
        + [keep_all[0], received_all[0], residual, jnp.transpose(codes_j), ret_ids],
        [sds((block, cols), BF16)],
        [pltpu.VMEM((nz * ret_rows, cols), BF16)],
    )
    return layer_out, final_rows


def solution(mesh):
    in_specs = (
        P("exp", "seq"),
        P("seq", "exp"),
        P("seq", "exp"),
        P("seq", "exp"),
        P("seq", "exp"),
        P("seq", "exp"),
        P("exp", None, None),
        P("exp"),
        P("exp", "seq"),
        P("seq"),
        P("seq", None),
        P("exp", "seq", None),
        P("exp", "seq", None),
        P("exp", None, "seq"),
        P("exp", None),
        P(),
    )
    out_specs = (P("exp", "seq"), P("exp", "seq", None))
    return jax.shard_map(local, mesh=mesh, in_specs=in_specs, out_specs=out_specs, check_vma=False)
```

```python
import functools
import jax
import jax.numpy as jnp
import numpy as np
from jax import lax
from jax.experimental import pallas as pl
from jax.experimental.pallas import tpu as pltpu
from jax.sharding import PartitionSpec as P

EPS = 1e-05
F32 = jnp.float32
BF16 = jnp.bfloat16
I32 = jnp.int32
HIGHEST = lax.Precision.HIGHEST
NT = (((1,), (1,)), ((), ()))
TN = (((0,), (0,)), ((), ()))
NN = (((1,), (0,)), ((), ()))


def mm(a, b, dims=NN, precision=None):
    return lax.dot_general(a, b, dims, precision=precision, preferred_element_type=F32)


def sigmoid(v):
    return 1.0 / (1.0 + jnp.exp(-v))


def bit_reversed(p, bits):
    r = 0
    for b in range(bits):
        r = r * 2 + ((p >> b) & 1)
    return r


def whole(shape):
    return pl.BlockSpec(tuple(shape), lambda i, s: (0,) * len(shape))


def call(kernel, place, operands, outs, scratch=(), flops=0, limit=40, out_any=False):
    arrays, specs, moved = [], [], 0
    for item in operands:
        array, spec = item if isinstance(item, tuple) else (item, whole(item.shape))
        arrays.append(array)
        specs.append(spec)
        moved += array.size * array.dtype.itemsize
    moved += sum(o.size * o.dtype.itemsize for o in outs)
    return pl.pallas_call(
        kernel,
        out_shape=list(outs),
        grid_spec=pltpu.PrefetchScalarGridSpec(
            num_scalar_prefetch=1,
            grid=(1,),
            in_specs=specs,
            out_specs=[
                pl.BlockSpec(memory_space=pl.ANY) if out_any else whole(o.shape) for o in outs
            ],
            scratch_shapes=list(scratch),
        ),
        compiler_params=pltpu.CompilerParams(vmem_limit_bytes=limit * 1024 * 1024),
        cost_estimate=pl.CostEstimate(flops=flops, bytes_accessed=moved, transcendentals=0),
    )(place, *arrays)


def hbm(array):
    return (array, pl.BlockSpec(memory_space=pltpu.HBM))


def anywhere(array):
    return (array, pl.BlockSpec(memory_space=pl.ANY))


def run_copies(pairs, sem):
    copies = [pltpu.make_async_copy(a, b, sem.at[n]) for n, (a, b) in enumerate(pairs)]
    for c in copies:
        c.start()
    return copies


def one_hot(mask):
    return mask.astype(F32).astype(BF16)


def turned_back(z, back, nz):
    return jnp.where(z < back, z - back + nz, z - back)


def sds(shape, dtype):
    return jax.ShapeDtypeStruct(tuple(shape), dtype)


def pieces(x):
    hi = x.astype(BF16)
    rest = x - hi.astype(F32)
    mid = rest.astype(BF16)
    return hi, mid, (rest - mid.astype(F32)).astype(BF16)


def routing_kernel(nz, cap, own_rows, s, *refs):
    keep = refs[0]
    given = refs[1 : nz + 1]
    base, codes, sign, ids = refs[nz + 1 :]
    j = s[2]
    block = given[0].shape[1]
    for r in range(nz):
        ids[lax.bitwise_xor(j, r)] = given[r][...]
    rows = lax.broadcasted_iota(I32, (block, block), 0)
    cols = lax.broadcasted_iota(I32, (block, block), 1)
    strict = one_hot(rows < cols)
    own = base[...] + j * (nz * cap)
    earlier = [jnp.zeros((1, 1), I32) for _ in range(nz)]
    other = jnp.zeros((own_rows, 1), I32)
    place = lax.broadcasted_iota(I32, (16, block), 0)
    for b in range(nz):
        first, second = ids[b, 0:1, :], ids[b, 1:2, :]
        named = ((place == first) | (place == second)) & (place < nz)
        ranks = mm(one_hot(named), strict).astype(I32)
        slots = []
        for e in range(nz):
            hit = (first == e) | (second == e)
            rank = ranks[e : e + 1, :]
            kept = hit & (rank + earlier[e] < keep[e])
            slots.append(jnp.where(kept, (e * nz + b) * cap + rank, -1))
            earlier[e] = earlier[e] + jnp.sum(hit.astype(I32), axis=1, keepdims=True)
        top = functools.reduce(jnp.maximum, slots)
        rest = functools.reduce(jnp.maximum, [jnp.where(c == top, -1, c) for c in slots])
        codes[b, 0:1, :] = top
        codes[b, 1:2, :] = rest
        holds = (own == top) | (own == rest)
        other = other + jnp.sum(jnp.where(holds, first + second, 0), axis=1, keepdims=True)
    every = lax.broadcasted_iota(I32, sign.shape, 1)
    sign[...] = (every == j).astype(F32) - (every == other - j).astype(F32)


def pack_kernel(away, ny, width, s, a, b, out, sem):
    at = pl.multiple_of(lax.rem(s[1] + away, ny) * width, 128)
    for c in run_copies([(x.at[:, pl.ds(at, width)], out.at[n]) for n, x in enumerate((a, b))], sem):
        c.wait()


def update_kernel(nz, ny, heads, hd, s, *refs):
    z, y = s[0], s[1]
    n = ny - 1
    k_arg, v_arg = refs[0], refs[1]
    kv = refs[2 : 2 + n]
    logs = refs[2 + n : 2 + n + ny]
    outs = refs[2 + n + ny : 2 + n + ny + nz]
    c_row, c_col, log_all, state, tail, own, sem = refs[2 + n + ny + nz :]
    tok = k_arg.shape[0]
    total_tok = tok * ny
    share = hd // nz
    mine = pl.ds(pl.multiple_of(y * heads * hd, 128), heads * hd)
    copies = run_copies([(x.at[:, mine], own.at[m]) for m, x in enumerate((k_arg, v_arg))], sem)
    for d in range(ny):
        at = pl.multiple_of(lax.rem(y + ny - d, ny) * tok, tok)
        log_all[:, pl.ds(at, tok)] = logs[d][pl.ds(y * heads, heads), :]
    rows = lax.broadcasted_iota(I32, (total_tok, total_tok), 0)
    cols = lax.broadcasted_iota(I32, (total_tok, total_tok), 1)
    c_row[...] = mm(log_all[...], (rows <= cols).astype(F32), precision=HIGHEST)
    c_col[...] = mm((rows >= cols).astype(F32), log_all[...], NT, precision=HIGHEST)
    total = c_row[:, total_tok - 1 : total_tok]
    for c in copies:
        c.wait()
    for h in range(heads):
        add = None
        for d in range(ny):
            at = pl.multiple_of(lax.rem(y + ny - d, ny) * tok, tok)
            lanes = slice(h * hd, (h + 1) * hd)
            pair = own if d == 0 else kv[d - 1]
            key = pair[0, :, lanes].astype(F32)
            decay = jnp.exp(total[h : h + 1, :] - c_col[pl.ds(at, tok), h : h + 1])
            weighted = (key * sigmoid(key) * decay).astype(BF16)
            part = mm(weighted, pair[1, :, lanes], TN)
            add = part if add is None else add + part
        state[h] = add.astype(BF16)
    tail[...] = jnp.zeros_like(tail)
    hi, mid, lo = pieces(total)
    lane = lax.broadcasted_iota(I32, (heads, hd), 1)
    tail[0:heads, :] = jnp.where(
        lane == 0,
        hi.astype(F32),
        jnp.where(lane == 1, mid.astype(F32), jnp.where(lane == 2, lo.astype(F32), 0.0)),
    )
    for d in range(nz):
        at = pl.multiple_of(lax.rem(z + d, nz) * share, share)
        for h in range(heads):
            outs[d][h * share : (h + 1) * share, :] = state[h, pl.ds(at, share), :]
        outs[d][heads * share :, :] = tail[...].astype(BF16)


def prefix_kernel(nz, heads, hd, s, *refs):
    z, y = s[0], s[1]
    parts = refs[:nz]
    start = refs[nz]
    outs = refs[nz + 1 : 2 * nz + 1]
    final, held, entering, run, sem = refs[2 * nz + 1 :]
    share = hd // nz
    source = start.at[
        pl.ds(y * heads, heads), pl.ds(pl.multiple_of(z * share, share), share), :
    ]
    copies = run_copies([(source, run)], sem)
    for d in range(nz):
        held[lax.rem(z + nz - d, nz)] = parts[d][...]
    copies[0].wait()
    for p in range(nz):
        logs = jnp.sum(held[p, heads * share :, :].astype(F32), axis=1, keepdims=True)
        keep = jnp.exp(logs)
        for h in range(heads):
            rows = slice(h * share, (h + 1) * share)
            now = run[h]
            entering[p, rows, :] = now.astype(BF16)
            run[h] = keep[h : h + 1, :] * now + held[p, rows, :].astype(F32)
    final[...] = run[...]
    for d in range(nz):
        outs[d][...] = entering[lax.rem(z + d, nz)]


def attention_kernel(nz, ny, heads, hd, s, *refs):
    z, y = s[0], s[1]
    n = ny - 1
    args = refs[:4]
    kv = refs[4 : 4 + n]
    qg = refs[4 + n : 4 + 2 * n]
    states = refs[4 + 2 * n : 4 + 2 * n + nz]
    c_row, c_col, gain, out, ks, vs, qs, gs, state, sem = refs[4 + 2 * n + nz :]
    tok = args[0].shape[0]
    total_tok = tok * ny
    share = hd // nz
    mine = pl.ds(pl.multiple_of(y * heads * hd, 128), heads * hd)
    moves = []
    for d in range(ny):
        at = pl.ds(pl.multiple_of(lax.rem(y + ny - d, ny) * tok, tok), tok)
        for m, to in enumerate((ks, vs, qs, gs)):
            if d == 0:
                source = args[m].at[:, mine]
            else:
                source = (kv if m < 2 else qg)[d - 1].at[m % 2]
            moves.append((source, to.at[at, :]))
    copies = run_copies(moves, sem)
    for d in range(nz):
        at = pl.ds(pl.multiple_of(lax.rem(z + nz - d, nz) * share, share), share)
        for h in range(heads):
            state[h, at, :] = states[d][h * share : (h + 1) * share, :]
    rows = lax.broadcasted_iota(I32, (total_tok, total_tok), 0)
    cols = lax.broadcasted_iota(I32, (total_tok, total_tok), 1)
    causal = rows >= cols
    for c in copies:
        c.wait()
    for h in range(heads):
        lanes = slice(h * hd, (h + 1) * hd)
        query = qs[:, lanes].astype(F32)
        query = query * sigmoid(query)
        key = ks[:, lanes].astype(F32)
        key = (key * sigmoid(key)).astype(BF16)
        col = c_col[:, h : h + 1]
        gap = jnp.where(causal, col - c_row[h : h + 1, :], 0.0)
        decay = jnp.where(causal, jnp.exp(gap), 0.0)
        scores = mm(query.astype(BF16), key, NT) * decay
        att = mm(scores.astype(BF16), vs[:, lanes])
        att = att + mm((query * jnp.exp(col)).astype(BF16), state[h])
        square = jnp.mean(att * att, axis=1, keepdims=True)
        gate = sigmoid(gs[:, lanes].astype(F32))
        out[:, lanes] = (att * lax.rsqrt(square + EPS) * gain[:, lanes] * gate).astype(BF16)


def project_kernel(nz, ny, cap, dzs, last, s, *refs):
    z, j = s[0], s[2]
    bits = nz.bit_length() - 1
    parts = [len(p) for p in dzs.values()]
    count = sum(parts) * ny
    blocks = refs[:count]
    weights = refs[count : count + ny]
    r_ids, b_ids, codes = refs[count + ny : count + ny + 3]
    refs = refs[count + ny + 3 :]
    if last:
        done, sums, residual = refs[:3]
        keep, send, keep_all, send_all, stacked, own, sem = refs[3:]
    else:
        done, sums, stacked, sem = refs
    rows = stacked.shape[2]
    moves = []
    at = 0
    for dy in range(ny):
        for n, (dz, pieces_of) in enumerate(dzs.items()):
            first = 0
            for _ in pieces_of:
                size = blocks[at].shape[0]
                moves.append((blocks[at], stacked.at[dy, n, pl.ds(first, size)]))
                first += size
                at += 1
    if last:
        moves.append((residual, own))
    copies = run_copies(moves, sem)
    ids = lax.bitwise_xor(r_ids[...], j) * (nz * cap) + b_ids[...]
    pick = lambda b: one_hot((ids == codes[b, 0:1, :]) | (ids == codes[b, 1:2, :]))
    total_rows = sums[...] if last else None
    for c in copies:
        c.wait()
    projected = {}
    for n, dz in enumerate(dzs):
        total = None
        for dy in range(ny):
            part = mm(stacked[dy, n], weights[dy][...])
            total = part if total is None else total + part
        projected[dz] = total.astype(BF16)
        part = mm(pick(lax.rem(z + nz - dz, nz)), projected[dz])
        total_rows = part if total_rows is None else total_rows + part
    if not last:
        for n, dz in enumerate(dzs):
            done[n] = projected[dz]
        sums[...] = total_rows
        return
    total_rows = total_rows + mm(pick(j), own[...])
    half = keep.shape[0]
    keep[...] = total_rows[:half, :]
    send[...] = total_rows[half:, :].astype(BF16)
    before = [dz for dz in range(nz) if dz not in dzs]
    for p in range(nz):
        block = lax.bitwise_xor(jnp.int32(bit_reversed(p, bits)), j)
        away = lax.rem(z + nz - block, nz)
        to = keep_all.at[p] if p < nz // 2 else send_all.at[p - nz // 2]
        for dz in range(nz):

            @pl.when(away == dz)
            def _(dz=dz):
                to[...] = projected[dz] if dz in dzs else done[before.index(dz)]


def rows_kernel(s, keep, received, gain, router_t, sign, out):
    width = gain.shape[1]
    rows = keep[...] + received[...].astype(F32)
    square = jnp.sum(rows * rows, axis=1, keepdims=True)
    scaled = rows * gain[...]
    logits = mm(scaled, router_t[...], NT, precision=HIGHEST)
    gap = jnp.sum(logits * sign[...], axis=1, keepdims=True)
    out[:, :width] = scaled.astype(BF16)
    lane = lax.broadcasted_iota(I32, (rows.shape[0], 128), 1)
    stats = jnp.zeros((rows.shape[0], 128), F32)
    for at, value in ((0, square), (3, gap)):
        for k, piece in enumerate(pieces(value)):
            stats = jnp.where(lane == at + k, piece.astype(F32), stats)
    out[:, width:] = stats.astype(BF16)


def up_kernel(nz, ny, places, first, last, features, s, *refs):
    z, y = s[0], s[1]
    count = len(places)
    blocks = refs[:count]
    refs = refs[count:]
    before = () if first else refs[:3]
    refs = refs[0 if first else 3 :]
    w_gate, w_up = refs[:2]
    outs = refs[2 : 4 if last else 5]
    gate_buf, up_buf, sem = refs[4 if last else 5 :]
    width = gate_buf.shape[2]
    copies = []
    for n, (dz, dy) in enumerate(places):
        source = lax.rem(z + nz - dz, nz) * ny + lax.rem(y + ny - dy, ny)
        at = pl.ds(pl.multiple_of(source * width, 128), width)
        copies.append(
            (
                pltpu.make_async_copy(w_gate.at[0, :, at], gate_buf.at[n], sem.at[0, n]),
                pltpu.make_async_copy(w_up.at[0, :, at], up_buf.at[n], sem.at[1, n]),
            )
        )
        for c in copies[-1]:
            c.start()
    gate, up, stats = (None, None, None) if first else (b[...] for b in before)
    for n in range(count):
        rows = blocks[n][:, :width]
        part = blocks[n][:, width:].astype(F32)
        stats = part if stats is None else stats + part
        copies[n][0].wait()
        part = mm(rows, gate_buf[n], NT)
        gate = part if gate is None else gate + part
        copies[n][1].wait()
        part = mm(rows, up_buf[n], NT)
        up = part if up is None else up + part
    if not last:
        outs[0][...] = gate
        outs[1][...] = up
        outs[2][...] = stats
        return
    square = stats[:, 0:1] + stats[:, 1:2] + stats[:, 2:3]
    gap = stats[:, 3:4] + stats[:, 4:5] + stats[:, 5:6]
    inverse = lax.rsqrt(square / features + EPS)
    gate = gate * inverse
    outs[0][...] = (gate * sigmoid(gate) * (up * inverse)).astype(BF16)
    outs[1][...] = jnp.broadcast_to(sigmoid(gap * inverse), outs[1].shape)


def down_kernel(nz, ny, cap, places, first, last, s, *refs):
    z, y, j = s[0], s[1], s[2]
    count = len(places)
    blocks = refs[:count]
    refs = refs[count:]
    before = None if first else refs[0]
    refs = refs[0 if first else 1 :]
    w_down = refs[0]
    refs = refs[1:]
    if last:
        weight, out_base, row_base = refs[:3]
        refs = refs[3:]
    outs, buf, sem = refs[:-2], refs[-2], refs[-1]
    depth = buf.shape[1]
    copies = []
    for n, (dz, dy) in enumerate(places):
        source = lax.rem(z + nz - dz, nz) * ny + lax.rem(y + ny - dy, ny)
        at = pl.ds(pl.multiple_of(source * depth, depth), depth)
        copies.append(pltpu.make_async_copy(w_down.at[0, at, :], buf.at[n], sem.at[n]))
        copies[-1].start()
    total = None if first else before[...]
    for n in range(count):
        copies[n].wait()
        part = mm(blocks[n][...], buf[n])
        total = part if total is None else total + part
    if not last:
        outs[0][...] = total
        return
    result = (total * weight[:, 0:1]).astype(BF16)
    for r, out in enumerate(outs):
        wanted = out_base[...] + lax.bitwise_xor(j, r) * cap
        out[...] = mm(one_hot(wanted == row_base[...]), result).astype(BF16)


def combine_kernel(nz, cap, s, *refs):
    j = s[2]
    returned = refs[:nz]
    keep, received, residual, codes, ret_r, ret_base, out, stacked, own, sem = refs[nz:]
    copies = run_copies([(residual, own)], sem)
    rows = returned[0].shape[0]
    for n in range(nz):
        stacked[n * rows : (n + 1) * rows, :] = returned[n][...]
    ids = lax.bitwise_xor(ret_r[...], j) * (nz * cap) + ret_base[...] + j * cap
    pick = (ids == codes[j, 0:1, :]) | (ids == codes[j, 1:2, :])
    added = mm(one_hot(pick), stacked[...], TN)
    copies[0].wait()
    total = own[...].astype(F32) + (keep[...].astype(F32) + received[...].astype(F32))
    out[...] = (total + added).astype(BF16)


def local(
    residual,
    query,
    key_in,
    value_in,
    gate_in,
    log_decay,
    state_in,
    attn_gain,
    w_out,
    moe_gain,
    router,
    w_gate,
    w_up,
    w_down,
    expert_ids,
    keep_counts,
):
    nz = lax.axis_size("exp")
    ny = lax.axis_size("seq") // nz
    bits = nz.bit_length() - 1
    i = lax.axis_index("seq").astype(I32)
    j = lax.axis_index("exp").astype(I32)
    z, y = i // ny, i % ny
    place = jnp.stack([z, y, j])

    tok, head_width = query.shape
    head_count, hd = state_in.shape[0], state_in.shape[2]
    heads = head_count // ny
    width = heads * hd
    block, cols = residual.shape
    features = w_gate.shape[2]
    units = w_gate.shape[1]
    experts = router.shape[1]
    cap = 5 * block * nz // (2 * nz * experts)
    slots = nz * cap

    def z_turn(a, d):
        pairs = [(p * ny + q, (p + d) % nz * ny + q) for p in range(nz) for q in range(ny)]
        return lax.ppermute(a, "seq", pairs)

    def y_turn(a, d):
        pairs = [(p * ny + q, p * ny + (q + d) % ny) for p in range(nz) for q in range(ny)]
        return lax.ppermute(a, "seq", pairs)

    def swap(a, r):
        return lax.ppermute(a, "exp", [(p, p ^ r) for p in range(nz)])

    z_order = sorted(range(1, nz), key=lambda d: (min(d, nz - d), d))
    near = [d for d in z_order if min(d, nz - d) == 1]
    distant = [d for d in z_order if d not in near]
    places = [(dz, dy) for dy in range(ny) for dz in range(nz)]

    def behind(values, events):
        return list(lax.optimization_barrier((tuple(values), tuple(events)))[0])

    def gather(a):
        held = {(0, 0): a}
        for d in range(1, ny):
            held[0, d] = y_turn(a, d)
        for d in z_order:
            held[d, 0] = z_turn(a, d)
        for d in z_order:
            for e in range(1, ny):
                held[d, e] = y_turn(held[d, 0], e)
        return held

    slot = np.arange(cap)
    row_r = np.repeat([bit_reversed(p, bits) for p in range(nz)], slots).astype(np.int32)[:, None]
    row_base = np.tile((np.arange(nz)[:, None] * cap + slot).reshape(slots), nz)
    row_base = row_base.astype(np.int32)[:, None]
    own_base = row_base[:slots]
    ret_rows = cap + -cap % 16
    padded = np.where(np.arange(ret_rows) < cap, np.arange(ret_rows), -(10**8)).astype(np.int32)
    ret_r = np.repeat(np.arange(nz), ret_rows).astype(np.int32)[:, None]
    ret_base = np.tile(padded, nz)[:, None]

    hand = [pltpu.SemaphoreType.DMA((2,))]
    logs_t = jnp.transpose(log_decay)
    logs, kvs, qgs = [logs_t], [], []
    for d in range(1, ny):
        pack = functools.partial(pack_kernel, d, ny, width)
        out = [sds((2, tok, width), BF16)]
        (kv,) = call(pack, place, [hbm(key_in), hbm(value_in)], out, hand, out_any=True)
        kvs.append(y_turn(kv, d))
        logs.append(y_turn(logs_t, d))
        (qg,) = call(pack, place, [hbm(query), hbm(gate_in)], out, hand, out_any=True)
        qgs.append(y_turn(qg, d))
    ids = jnp.transpose(expert_ids)
    codes, sign = call(
        functools.partial(routing_kernel, nz, cap, slots),
        place,
        [(keep_counts, pl.BlockSpec(memory_space=pltpu.SMEM))]
        + [ids]
        + [swap(ids, r) for r in range(1, nz)]
        + [own_base],
        [sds((nz, 2, block), I32), sds((slots, experts), F32)],
        [pltpu.VMEM((nz, 2, block), I32)],
    )
    attn_gain_2, moe_gain_2, router_t = attn_gain[None], moe_gain[None], jnp.transpose(router)
    kvs = behind(kvs, [codes, sign, attn_gain_2, moe_gain_2])
    share = hd // nz
    long = tok * ny
    *parts, c_row, c_col = call(
        functools.partial(update_kernel, nz, ny, heads, hd),
        place,
        [hbm(key_in), hbm(value_in), *kvs, *logs],
        [sds((heads * share + 16, hd), BF16)] * nz
        + [sds((heads, long), F32), sds((long, heads), F32)],
        [
            pltpu.VMEM((heads, long), F32),
            pltpu.VMEM((heads, hd, hd), BF16),
            pltpu.VMEM((16, hd), F32),
            pltpu.VMEM((2, tok, width), BF16),
            pltpu.SemaphoreType.DMA((2,)),
        ],
        flops=2 * long * hd * hd * heads,
    )
    parts = [parts[0]] + [z_turn(parts[d], d) for d in range(1, nz)]
    *entering, last_rows = call(
        functools.partial(prefix_kernel, nz, heads, hd),
        place,
        [*parts, hbm(state_in)],
        [sds((heads * share, hd), BF16)] * nz + [sds((heads, share, hd), F32)],
        [
            pltpu.VMEM((nz, heads * share + 16, hd), BF16),
            pltpu.VMEM((nz, heads * share, hd), BF16),
            pltpu.VMEM((heads, share, hd), F32),
            pltpu.SemaphoreType.DMA((1,)),
        ],
    )
    entering = [entering[0]] + [z_turn(entering[d], d) for d in range(1, nz)]
    (mixed,) = call(
        functools.partial(attention_kernel, nz, ny, heads, hd),
        place,
        [
            hbm(key_in),
            hbm(value_in),
            hbm(query),
            hbm(gate_in),
            *[anywhere(x) for x in kvs],
            *[anywhere(x) for x in qgs],
            *entering,
            c_row,
            c_col,
            (attn_gain_2, pl.BlockSpec((1, width), lambda n, s: (0, s[1]))),
        ],
        [sds((long, width), BF16)],
        [pltpu.VMEM((long, width), BF16)] * 4
        + [pltpu.VMEM((heads, hd, hd), BF16), pltpu.SemaphoreType.DMA((4 * ny,))],
        flops=4 * long * long * width,
    )

    def across(blocks):
        return [[y_turn(x, e) for x in blocks] for e in range(1, ny)]

    held = {0: [[mixed]] + across([mixed])}
    for d in near:
        held[d] = [[z_turn(mixed, d)]]
    free = behind([mixed], [held[d][0][0] for d in near])[0]
    for d in near:
        held[d] += across(held[d][0])
    halves = [free[: long // 2], free[long // 2 :]]
    for d in distant:
        held[d] = [[z_turn(x, d) for x in halves]]
    for d in distant:
        held[d] += across(held[d][0])
    w_parts = [
        (w_out, pl.BlockSpec((width, cols), lambda n, s, d=d: (lax.rem(s[1] + ny - d, ny), 0)))
        for d in range(ny)
    ]
    given = []
    for group in ([0] + near, distant):
        last = group is distant
        dzs = {d: held[d][0] for d in group}
        blocks = [x for dy in range(ny) for d in group for x in held[d][dy]]
        half = nz * slots // 2
        outs = [sds((len(group), block, cols), BF16), sds((nz * slots, cols), F32)]
        if last:
            outs = [sds((half, cols), F32), sds((half, cols), BF16)]
            outs += [sds((nz // 2, block, cols), BF16)] * 2
        given = call(
            functools.partial(project_kernel, nz, ny, cap, dzs, last),
            place,
            [anywhere(x) for x in blocks]
            + w_parts
            + [row_r, row_base, codes]
            + list(given)
            + ([hbm(residual)] if last else []),
            outs,
            [pltpu.VMEM((ny, len(group), long, width), BF16)]
            + ([pltpu.VMEM((block, cols), BF16)] if last else [])
            + [pltpu.SemaphoreType.DMA((len(blocks) + 1,))],
            flops=2 * len(group) * long * head_width * cols,
        )
    keep, send, keep_all, send_all = given
    for b in range(bits):
        received = swap(send, 1 << b)
        if b < bits - 1:
            part = keep.shape[0] // 2
            send = (keep[part:] + received[part:].astype(F32)).astype(BF16)
            keep = keep[:part] + received[:part].astype(F32)
    (rows_out,) = call(
        rows_kernel,
        place,
        [keep, received, moe_gain_2, router_t, sign],
        [sds((slots, cols + 128), BF16)],
    )
    send_all = behind([send_all], [rows_out])[0]
    for b in range(bits):
        received_all = swap(send_all, 1 << b)
        if b < bits - 1:
            n = keep_all.shape[0] // 2
            both = keep_all.astype(F32) + received_all.astype(F32)
            send_all, keep_all = both[n:].astype(BF16), both[:n].astype(BF16)
    rows = share // ny
    last_rows = behind([last_rows], [rows_out])[0]
    final_rows = jnp.zeros((head_count, rows, hd), F32)
    for d in range(ny):
        sent = lax.dynamic_slice_in_dim(last_rows, (y + d) % ny * rows, rows, 1)
        got = sent if d == 0 else y_turn(sent, d)
        final_rows = lax.dynamic_update_slice_in_dim(
            final_rows, got, (y - d) % ny * heads, 0
        )

    groups = [[(0, d) for d in range(ny)], [(d, 0) for d in z_order]]
    groups.append([(d, e) for d in z_order for e in range(1, ny)])
    arrived = gather(rows_out)
    state = []
    if cols % 128:
        order = jnp.stack([(z - dz) % nz * ny + (y - dy) % ny for dz, dy in places])
        at = jnp.argsort(order)
        rows_all = jnp.take(jnp.stack([arrived[p] for p in places]), at, axis=0)
        stats = jnp.sum(rows_all[:, :, cols:].astype(F32), axis=0)
        rows_all = jnp.swapaxes(rows_all[:, :, :cols], 0, 1).reshape(slots, features)
        inverse = lax.rsqrt(jnp.sum(stats[:, :3], axis=1) / features + EPS)[:, None]
        gate = mm(rows_all, w_gate[0], NT) * inverse
        hidden = (gate * sigmoid(gate) * (mm(rows_all, w_up[0], NT) * inverse)).astype(BF16)
        weight = sigmoid(jnp.sum(stats[:, 3:6], axis=1)[:, None] * inverse)
        state = [hidden, jnp.broadcast_to(weight, (slots, 128))]
    for n, group in enumerate(groups if cols % 128 == 0 else ()):
        last = n == len(groups) - 1
        outs = [sds((slots, units), F32)] * 2 + [sds((slots, 128), F32)]
        if last:
            outs = [sds((slots, units), BF16), sds((slots, 128), F32)]
        state = call(
            functools.partial(up_kernel, nz, ny, group, n == 0, last, features),
            place,
            [arrived[p] for p in group] + list(state) + [anywhere(w_gate), anywhere(w_up)],
            outs,
            [pltpu.VMEM((len(group), units, cols), BF16)] * 2
            + [pltpu.SemaphoreType.DMA((2, len(group)))],
            flops=4 * len(group) * slots * units * cols,
        )
    hidden, weight = state
    arrived = gather(hidden)
    state = []
    for n, group in enumerate(groups):
        last = n == len(groups) - 1
        outs = [sds((slots, cols), F32)]
        if last:
            outs = [sds((ret_rows, cols), BF16)] * nz
        state = call(
            functools.partial(down_kernel, nz, ny, cap, group, n == 0, last),
            place,
            [arrived[p] for p in group]
            + list(state)
            + [anywhere(w_down)]
            + ([weight, padded[:, None], own_base.T] if last else []),
            outs,
            [
                pltpu.VMEM((len(group), units, cols), BF16),
                pltpu.SemaphoreType.DMA((len(group),)),
            ],
            flops=2 * len(group) * slots * units * cols,
        )
    returned = [state[0]] + [swap(state[r], r) for r in range(1, nz)]
    (layer_out,) = call(
        functools.partial(combine_kernel, nz, cap),
        place,
        returned + [keep_all[0], received_all[0], hbm(residual), codes, ret_r, ret_base],
        [sds((block, cols), BF16)],
        [
            pltpu.VMEM((nz * ret_rows, cols), BF16),
            pltpu.VMEM((block, cols), BF16),
            pltpu.SemaphoreType.DMA((1,)),
        ],
    )
    return layer_out, final_rows


def solution(mesh):
    in_specs = (
        P("exp", "seq"),
        P("seq", "exp"),
        P("seq", "exp"),
        P("seq", "exp"),
        P("seq", "exp"),
        P("seq", "exp"),
        P("exp", None, None),
        P("exp"),
        P("exp", "seq"),
        P("seq"),
        P("seq", None),
        P("exp", "seq", None),
        P("exp", "seq", None),
        P("exp", None, "seq"),
        P("exp", None),
        P(),
    )
    out_specs = (P("exp", "seq"), P("exp", "seq", None))
    return jax.shard_map(local, mesh=mesh, in_specs=in_specs, out_specs=out_specs, check_vma=False)
```

```python
import functools
import jax
import jax.numpy as jnp
import numpy as np
from jax import lax
from jax.experimental import pallas as pl
from jax.experimental.pallas import tpu as pltpu
from jax.sharding import PartitionSpec as P

EPS = 1e-05
F32 = jnp.float32
BF16 = jnp.bfloat16
I32 = jnp.int32
HIGHEST = lax.Precision.HIGHEST
NT = (((1,), (1,)), ((), ()))
TN = (((0,), (0,)), ((), ()))
NN = (((1,), (0,)), ((), ()))


def mm(a, b, dims=NN, precision=None):
    return lax.dot_general(a, b, dims, precision=precision, preferred_element_type=F32)


def sigmoid(v):
    return 1.0 / (1.0 + jnp.exp(-v))


def bit_reversed(p, bits):
    r = 0
    for b in range(bits):
        r = r * 2 + ((p >> b) & 1)
    return r


def whole(shape):
    return pl.BlockSpec(tuple(shape), lambda i, s: (0,) * len(shape))


def call(kernel, place, operands, outs, scratch=(), flops=0, limit=40):
    arrays, specs, moved = [], [], 0
    for item in operands:
        array, spec = item if isinstance(item, tuple) else (item, whole(item.shape))
        arrays.append(array)
        specs.append(spec)
        moved += array.size * array.dtype.itemsize
    moved += sum(o.size * o.dtype.itemsize for o in outs)
    return pl.pallas_call(
        kernel,
        out_shape=list(outs),
        grid_spec=pltpu.PrefetchScalarGridSpec(
            num_scalar_prefetch=1,
            grid=(1,),
            in_specs=specs,
            out_specs=[whole(o.shape) for o in outs],
            scratch_shapes=list(scratch),
        ),
        compiler_params=pltpu.CompilerParams(vmem_limit_bytes=limit * 1024 * 1024),
        cost_estimate=pl.CostEstimate(flops=flops, bytes_accessed=moved, transcendentals=0),
    )(place, *arrays)


def hbm(array):
    return (array, pl.BlockSpec(memory_space=pltpu.HBM))


def anywhere(array):
    return (array, pl.BlockSpec(memory_space=pl.ANY))


def run_copies(pairs, sem):
    copies = [pltpu.make_async_copy(a, b, sem.at[n]) for n, (a, b) in enumerate(pairs)]
    for c in copies:
        c.start()
    return copies


def one_hot(mask):
    return mask.astype(F32).astype(BF16)


def turned_back(z, back, nz):
    return jnp.where(z < back, z - back + nz, z - back)


def sds(shape, dtype):
    return jax.ShapeDtypeStruct(tuple(shape), dtype)


def pieces(x):
    hi = x.astype(BF16)
    rest = x - hi.astype(F32)
    mid = rest.astype(BF16)
    return hi, mid, (rest - mid.astype(F32)).astype(BF16)


def routing_kernel(nz, cap, own_rows, s, *refs):
    keep = refs[0]
    given = refs[1 : nz + 1]
    base, codes, sign, ids = refs[nz + 1 :]
    j = s[2]
    block = given[0].shape[1]
    for r in range(nz):
        ids[lax.bitwise_xor(j, r)] = given[r][...]
    rows = lax.broadcasted_iota(I32, (block, block), 0)
    cols = lax.broadcasted_iota(I32, (block, block), 1)
    strict = one_hot(rows < cols)
    own = base[...] + j * (nz * cap)
    earlier = [jnp.zeros((1, 1), I32) for _ in range(nz)]
    other = jnp.zeros((own_rows, 1), I32)
    place = lax.broadcasted_iota(I32, (16, block), 0)
    for b in range(nz):
        first, second = ids[b, 0:1, :], ids[b, 1:2, :]
        named = ((place == first) | (place == second)) & (place < nz)
        ranks = mm(one_hot(named), strict).astype(I32)
        slots = []
        for e in range(nz):
            hit = (first == e) | (second == e)
            rank = ranks[e : e + 1, :]
            kept = hit & (rank + earlier[e] < keep[e])
            slots.append(jnp.where(kept, (e * nz + b) * cap + rank, -1))
            earlier[e] = earlier[e] + jnp.sum(hit.astype(I32), axis=1, keepdims=True)
        top = functools.reduce(jnp.maximum, slots)
        rest = functools.reduce(jnp.maximum, [jnp.where(c == top, -1, c) for c in slots])
        codes[b, 0:1, :] = top
        codes[b, 1:2, :] = rest
        holds = (own == top) | (own == rest)
        other = other + jnp.sum(jnp.where(holds, first + second, 0), axis=1, keepdims=True)
    every = lax.broadcasted_iota(I32, sign.shape, 1)
    sign[...] = (every == j).astype(F32) - (every == other - j).astype(F32)


def pack_kernel(s, a, b, out):
    out[0] = a[...]
    out[1] = b[...]


def update_kernel(nz, ny, heads, hd, s, *refs):
    z, y = s[0], s[1]
    n = ny - 1
    k_arg, v_arg = refs[0], refs[1]
    kv = refs[2 : 2 + n]
    logs = refs[2 + n : 2 + n + ny]
    outs = refs[2 + n + ny : 2 + n + ny + nz]
    c_row, c_col, log_all, state, tail, own, sem = refs[2 + n + ny + nz :]
    tok = k_arg.shape[0]
    total_tok = tok * ny
    share = hd // nz
    mine = pl.ds(pl.multiple_of(y * heads * hd, 128), heads * hd)
    copies = run_copies([(x.at[:, mine], own.at[m]) for m, x in enumerate((k_arg, v_arg))], sem)
    for d in range(ny):
        at = pl.multiple_of(lax.rem(y + ny - d, ny) * tok, tok)
        log_all[:, pl.ds(at, tok)] = logs[d][pl.ds(y * heads, heads), :]
    rows = lax.broadcasted_iota(I32, (total_tok, total_tok), 0)
    cols = lax.broadcasted_iota(I32, (total_tok, total_tok), 1)
    c_row[...] = mm(log_all[...], (rows <= cols).astype(F32), precision=HIGHEST)
    c_col[...] = mm((rows >= cols).astype(F32), log_all[...], NT, precision=HIGHEST)
    total = c_row[:, total_tok - 1 : total_tok]
    for c in copies:
        c.wait()
    for h in range(heads):
        add = None
        for d in range(ny):
            at = pl.multiple_of(lax.rem(y + ny - d, ny) * tok, tok)
            lanes = slice(h * hd, (h + 1) * hd)
            pair = own if d == 0 else kv[d - 1]
            key = pair[0, :, lanes].astype(F32)
            decay = jnp.exp(total[h : h + 1, :] - c_col[pl.ds(at, tok), h : h + 1])
            weighted = (key * sigmoid(key) * decay).astype(BF16)
            part = mm(weighted, pair[1, :, lanes], TN)
            add = part if add is None else add + part
        state[h] = add.astype(BF16)
    tail[...] = jnp.zeros_like(tail)
    hi, mid, lo = pieces(total)
    lane = lax.broadcasted_iota(I32, (heads, hd), 1)
    tail[0:heads, :] = jnp.where(
        lane == 0,
        hi.astype(F32),
        jnp.where(lane == 1, mid.astype(F32), jnp.where(lane == 2, lo.astype(F32), 0.0)),
    )
    for d in range(nz):
        at = pl.multiple_of(lax.rem(z + d, nz) * share, share)
        for h in range(heads):
            outs[d][h * share : (h + 1) * share, :] = state[h, pl.ds(at, share), :]
        outs[d][heads * share :, :] = tail[...].astype(BF16)


def prefix_kernel(nz, heads, hd, s, *refs):
    z, y = s[0], s[1]
    parts = refs[:nz]
    start = refs[nz]
    outs = refs[nz + 1 : 2 * nz + 1]
    final, held, entering, run, sem = refs[2 * nz + 1 :]
    share = hd // nz
    source = start.at[
        pl.ds(y * heads, heads), pl.ds(pl.multiple_of(z * share, share), share), :
    ]
    copies = run_copies([(source, run)], sem)
    for d in range(nz):
        held[lax.rem(z + nz - d, nz)] = parts[d][...]
    copies[0].wait()
    for p in range(nz):
        logs = jnp.sum(held[p, heads * share :, :].astype(F32), axis=1, keepdims=True)
        keep = jnp.exp(logs)
        for h in range(heads):
            rows = slice(h * share, (h + 1) * share)
            now = run[h]
            entering[p, rows, :] = now.astype(BF16)
            run[h] = keep[h : h + 1, :] * now + held[p, rows, :].astype(F32)
    final[...] = run[...]
    for d in range(nz):
        outs[d][...] = entering[lax.rem(z + d, nz)]


def attention_kernel(nz, ny, heads, hd, s, *refs):
    z, y = s[0], s[1]
    n = ny - 1
    args = refs[:4]
    kv = refs[4 : 4 + n]
    qg = refs[4 + n : 4 + 2 * n]
    states = refs[4 + 2 * n : 4 + 2 * n + nz]
    c_row, c_col, gain, out, ks, vs, qs, gs, state, sem = refs[4 + 2 * n + nz :]
    tok = args[0].shape[0]
    total_tok = tok * ny
    share = hd // nz
    mine = pl.ds(pl.multiple_of(y * heads * hd, 128), heads * hd)
    moves = []
    for d in range(ny):
        at = pl.ds(pl.multiple_of(lax.rem(y + ny - d, ny) * tok, tok), tok)
        for m, to in enumerate((ks, vs, qs, gs)):
            if d == 0:
                source = args[m].at[:, mine]
            else:
                source = (kv if m < 2 else qg)[d - 1].at[m % 2]
            moves.append((source, to.at[at, :]))
    copies = run_copies(moves, sem)
    for d in range(nz):
        at = pl.ds(pl.multiple_of(lax.rem(z + nz - d, nz) * share, share), share)
        for h in range(heads):
            state[h, at, :] = states[d][h * share : (h + 1) * share, :]
    rows = lax.broadcasted_iota(I32, (total_tok, total_tok), 0)
    cols = lax.broadcasted_iota(I32, (total_tok, total_tok), 1)
    causal = rows >= cols
    for c in copies:
        c.wait()
    for h in range(heads):
        lanes = slice(h * hd, (h + 1) * hd)
        query = qs[:, lanes].astype(F32)
        query = query * sigmoid(query)
        key = ks[:, lanes].astype(F32)
        key = (key * sigmoid(key)).astype(BF16)
        col = c_col[:, h : h + 1]
        gap = jnp.where(causal, col - c_row[h : h + 1, :], 0.0)
        decay = jnp.where(causal, jnp.exp(gap), 0.0)
        scores = mm(query.astype(BF16), key, NT) * decay
        att = mm(scores.astype(BF16), vs[:, lanes])
        att = att + mm((query * jnp.exp(col)).astype(BF16), state[h])
        square = jnp.mean(att * att, axis=1, keepdims=True)
        gate = sigmoid(gs[:, lanes].astype(F32))
        out[:, lanes] = (att * lax.rsqrt(square + EPS) * gain[:, lanes] * gate).astype(BF16)


def project_kernel(nz, ny, cap, dzs, last, s, *refs):
    z, j = s[0], s[2]
    bits = nz.bit_length() - 1
    parts = [len(p) for p in dzs.values()]
    count = sum(parts) * ny
    blocks = refs[:count]
    weights = refs[count : count + ny]
    r_ids, b_ids, codes = refs[count + ny : count + ny + 3]
    refs = refs[count + ny + 3 :]
    if last:
        done, sums, residual = refs[:3]
        keep, send, keep_all, send_all, stacked, own, sem = refs[3:]
    else:
        done, sums, stacked, sem = refs
    rows = stacked.shape[2]
    moves = []
    at = 0
    for dy in range(ny):
        for n, (dz, pieces_of) in enumerate(dzs.items()):
            first = 0
            for _ in pieces_of:
                size = blocks[at].shape[0]
                moves.append((blocks[at], stacked.at[dy, n, pl.ds(first, size)]))
                first += size
                at += 1
    if last:
        moves.append((residual, own))
    copies = run_copies(moves, sem)
    ids = lax.bitwise_xor(r_ids[...], j) * (nz * cap) + b_ids[...]
    pick = lambda b: one_hot((ids == codes[b, 0:1, :]) | (ids == codes[b, 1:2, :]))
    total_rows = sums[...] if last else None
    for c in copies:
        c.wait()
    projected = {}
    for n, dz in enumerate(dzs):
        total = None
        for dy in range(ny):
            part = mm(stacked[dy, n], weights[dy][...])
            total = part if total is None else total + part
        projected[dz] = total.astype(BF16)
        part = mm(pick(lax.rem(z + nz - dz, nz)), projected[dz])
        total_rows = part if total_rows is None else total_rows + part
    if not last:
        for n, dz in enumerate(dzs):
            done[n] = projected[dz]
        sums[...] = total_rows
        return
    total_rows = total_rows + mm(pick(j), own[...])
    half = keep.shape[0]
    keep[...] = total_rows[:half, :]
    send[...] = total_rows[half:, :].astype(BF16)
    before = [dz for dz in range(nz) if dz not in dzs]
    for p in range(nz):
        block = lax.bitwise_xor(jnp.int32(bit_reversed(p, bits)), j)
        away = lax.rem(z + nz - block, nz)
        to = keep_all.at[p] if p < nz // 2 else send_all.at[p - nz // 2]
        for dz in range(nz):

            @pl.when(away == dz)
            def _(dz=dz):
                to[...] = projected[dz] if dz in dzs else done[before.index(dz)]


def rows_kernel(s, keep, received, gain, router_t, sign, out):
    width = gain.shape[1]
    rows = keep[...] + received[...].astype(F32)
    square = jnp.sum(rows * rows, axis=1, keepdims=True)
    scaled = rows * gain[...]
    logits = mm(scaled, router_t[...], NT, precision=HIGHEST)
    gap = jnp.sum(logits * sign[...], axis=1, keepdims=True)
    out[:, :width] = scaled.astype(BF16)
    lane = lax.broadcasted_iota(I32, (rows.shape[0], 128), 1)
    stats = jnp.zeros((rows.shape[0], 128), F32)
    for at, value in ((0, square), (3, gap)):
        for k, piece in enumerate(pieces(value)):
            stats = jnp.where(lane == at + k, piece.astype(F32), stats)
    out[:, width:] = stats.astype(BF16)


def up_kernel(nz, ny, places, first, last, features, s, *refs):
    z, y = s[0], s[1]
    count = len(places)
    blocks = refs[:count]
    refs = refs[count:]
    before = () if first else refs[:3]
    refs = refs[0 if first else 3 :]
    w_gate, w_up = refs[:2]
    outs = refs[2 : 4 if last else 5]
    gate_buf, up_buf, sem = refs[4 if last else 5 :]
    width = gate_buf.shape[2]
    copies = []
    for n, (dz, dy) in enumerate(places):
        source = lax.rem(z + nz - dz, nz) * ny + lax.rem(y + ny - dy, ny)
        at = pl.ds(pl.multiple_of(source * width, 128), width)
        copies.append(
            (
                pltpu.make_async_copy(w_gate.at[0, :, at], gate_buf.at[n], sem.at[0, n]),
                pltpu.make_async_copy(w_up.at[0, :, at], up_buf.at[n], sem.at[1, n]),
            )
        )
        for c in copies[-1] if n < 2 else ():
            c.start()
    gate, up, stats = (None, None, None) if first else (b[...] for b in before)
    for n in range(count):
        rows = blocks[n][:, :width]
        part = blocks[n][:, width:].astype(F32)
        stats = part if stats is None else stats + part
        copies[n][0].wait()
        if n + 2 < count:
            for c in copies[n + 2]:
                c.start()
        part = mm(rows, gate_buf[n], NT)
        gate = part if gate is None else gate + part
        copies[n][1].wait()
        part = mm(rows, up_buf[n], NT)
        up = part if up is None else up + part
    if not last:
        outs[0][...] = gate
        outs[1][...] = up
        outs[2][...] = stats
        return
    square = stats[:, 0:1] + stats[:, 1:2] + stats[:, 2:3]
    gap = stats[:, 3:4] + stats[:, 4:5] + stats[:, 5:6]
    inverse = lax.rsqrt(square / features + EPS)
    gate = gate * inverse
    outs[0][...] = (gate * sigmoid(gate) * (up * inverse)).astype(BF16)
    outs[1][...] = jnp.broadcast_to(sigmoid(gap * inverse), outs[1].shape)


def down_kernel(nz, ny, cap, places, first, last, s, *refs):
    z, y, j = s[0], s[1], s[2]
    count = len(places)
    blocks = refs[:count]
    refs = refs[count:]
    before = None if first else refs[0]
    refs = refs[0 if first else 1 :]
    w_down = refs[0]
    refs = refs[1:]
    if last:
        weight, out_base, row_base = refs[:3]
        refs = refs[3:]
    outs, buf, sem = refs[:-2], refs[-2], refs[-1]
    depth = buf.shape[1]
    copies = []
    for n, (dz, dy) in enumerate(places):
        source = lax.rem(z + nz - dz, nz) * ny + lax.rem(y + ny - dy, ny)
        at = pl.ds(pl.multiple_of(source * depth, depth), depth)
        copies.append(pltpu.make_async_copy(w_down.at[0, at, :], buf.at[n], sem.at[n]))
        if n < 3:
            copies[-1].start()
    total = None if first else before[...]
    for n in range(count):
        copies[n].wait()
        if n + 3 < count:
            copies[n + 3].start()
        part = mm(blocks[n][...], buf[n])
        total = part if total is None else total + part
    if not last:
        outs[0][...] = total
        return
    result = (total * weight[:, 0:1]).astype(BF16)
    for r, out in enumerate(outs):
        wanted = out_base[...] + lax.bitwise_xor(j, r) * cap
        out[...] = mm(one_hot(wanted == row_base[...]), result).astype(BF16)


def combine_kernel(nz, cap, s, *refs):
    j = s[2]
    returned = refs[:nz]
    keep, received, residual, codes, ret_r, ret_base, out, stacked, own, sem = refs[nz:]
    copies = run_copies([(residual, own)], sem)
    rows = returned[0].shape[0]
    for n in range(nz):
        stacked[n * rows : (n + 1) * rows, :] = returned[n][...]
    ids = lax.bitwise_xor(ret_r[...], j) * (nz * cap) + ret_base[...] + j * cap
    pick = (ids == codes[j, 0:1, :]) | (ids == codes[j, 1:2, :])
    added = mm(one_hot(pick), stacked[...], TN)
    copies[0].wait()
    total = own[...].astype(F32) + (keep[...].astype(F32) + received[...].astype(F32))
    out[...] = (total + added).astype(BF16)


def local(
    residual,
    query,
    key_in,
    value_in,
    gate_in,
    log_decay,
    state_in,
    attn_gain,
    w_out,
    moe_gain,
    router,
    w_gate,
    w_up,
    w_down,
    expert_ids,
    keep_counts,
):
    nz = lax.axis_size("exp")
    ny = lax.axis_size("seq") // nz
    bits = nz.bit_length() - 1
    i = lax.axis_index("seq").astype(I32)
    j = lax.axis_index("exp").astype(I32)
    z, y = i // ny, i % ny
    place = jnp.stack([z, y, j])

    tok, head_width = query.shape
    head_count, hd = state_in.shape[0], state_in.shape[2]
    heads = head_count // ny
    width = heads * hd
    block, cols = residual.shape
    features = w_gate.shape[2]
    units = w_gate.shape[1]
    experts = router.shape[1]
    cap = 5 * block * nz // (2 * nz * experts)
    slots = nz * cap

    def z_turn(a, d):
        pairs = [(p * ny + q, (p + d) % nz * ny + q) for p in range(nz) for q in range(ny)]
        return lax.ppermute(a, "seq", pairs)

    def y_turn(a, d):
        pairs = [(p * ny + q, p * ny + (q + d) % ny) for p in range(nz) for q in range(ny)]
        return lax.ppermute(a, "seq", pairs)

    def swap(a, r):
        return lax.ppermute(a, "exp", [(p, p ^ r) for p in range(nz)])

    z_order = sorted(range(1, nz), key=lambda d: (min(d, nz - d), d))
    near = [d for d in z_order if min(d, nz - d) == 1]
    distant = [d for d in z_order if d not in near]
    places = [(dz, dy) for dy in range(ny) for dz in range(nz)]

    def behind(values, events):
        return list(lax.optimization_barrier((tuple(values), tuple(events)))[0])

    def gather_z(a):
        held = {(0, 0): a}
        for d in range(1, ny):
            held[0, d] = y_turn(a, d)
        for d in z_order:
            held[d, 0] = z_turn(a, d)
        return held

    def gather_y(held, events):
        for d in z_order:
            x = held[d, 0] = behind([held[d, 0]], events)[0]
            for e in range(1, ny):
                held[d, e] = y_turn(x, e)

    def stages(run, a):
        arrived = gather_z(a)
        state = run(0, groups[0], arrived, [])
        gather_y(arrived, state)
        for n in (1, 2):
            state = run(n, groups[n], arrived, state)
        return state

    groups = [[(0, 0)], [(0, d) for d in range(1, ny)] + [(d, 0) for d in z_order]]
    groups.append([(d, e) for d in z_order for e in range(1, ny)])

    slot = np.arange(cap)
    row_r = np.repeat([bit_reversed(p, bits) for p in range(nz)], slots).astype(np.int32)[:, None]
    row_base = np.tile((np.arange(nz)[:, None] * cap + slot).reshape(slots), nz)
    row_base = row_base.astype(np.int32)[:, None]
    own_base = row_base[:slots]
    ret_rows = cap + -cap % 16
    padded = np.where(np.arange(ret_rows) < cap, np.arange(ret_rows), -(10**8)).astype(np.int32)
    ret_r = np.repeat(np.arange(nz), ret_rows).astype(np.int32)[:, None]
    ret_base = np.tile(padded, nz)[:, None]

    logs_t = jnp.transpose(log_decay)
    logs, kvs, qgs = [logs_t], [], []
    for d in range(1, ny):
        there = pl.BlockSpec((tok, width), lambda n, s, d=d: (0, lax.rem(s[1] + d, ny)))
        out = [sds((2, tok, width), BF16)]
        (kv,) = call(pack_kernel, place, [(key_in, there), (value_in, there)], out, limit=60)
        kvs.append(y_turn(kv, d))
        logs.append(y_turn(logs_t, d))
        qgs += call(pack_kernel, place, [(query, there), (gate_in, there)], out, limit=60)
    ids = jnp.transpose(expert_ids)
    codes, sign = call(
        functools.partial(routing_kernel, nz, cap, slots),
        place,
        [(keep_counts, pl.BlockSpec(memory_space=pltpu.SMEM))]
        + [ids]
        + [swap(ids, r) for r in range(1, nz)]
        + [own_base],
        [sds((nz, 2, block), I32), sds((slots, experts), F32)],
        [pltpu.VMEM((nz, 2, block), I32)],
    )
    attn_gain_2, moe_gain_2, router_t = attn_gain[None], moe_gain[None], jnp.transpose(router)
    prepared = [codes, sign, attn_gain_2, moe_gain_2]
    qgs = [y_turn(qg, d + 1) for d, qg in enumerate(behind(qgs, kvs + logs + prepared))]
    share = hd // nz
    long = tok * ny
    *parts, c_row, c_col = call(
        functools.partial(update_kernel, nz, ny, heads, hd),
        place,
        [hbm(key_in), hbm(value_in), *kvs, *logs],
        [sds((heads * share + 16, hd), BF16)] * nz
        + [sds((heads, long), F32), sds((long, heads), F32)],
        [
            pltpu.VMEM((heads, long), F32),
            pltpu.VMEM((heads, hd, hd), BF16),
            pltpu.VMEM((16, hd), F32),
            pltpu.VMEM((2, tok, width), BF16),
            pltpu.SemaphoreType.DMA((2,)),
        ],
        limit=40,
            flops=2 * long * hd * hd * heads,
    )
    parts = [parts[0]] + [z_turn(parts[d], d) for d in range(1, nz)]
    *entering, last_rows = call(
        functools.partial(prefix_kernel, nz, heads, hd),
        place,
        [*parts, hbm(state_in)],
        [sds((heads * share, hd), BF16)] * nz + [sds((heads, share, hd), F32)],
        [
            pltpu.VMEM((nz, heads * share + 16, hd), BF16),
            pltpu.VMEM((nz, heads * share, hd), BF16),
            pltpu.VMEM((heads, share, hd), F32),
            pltpu.SemaphoreType.DMA((1,)),
        ],
    )
    entering = [entering[0]] + [z_turn(entering[d], d) for d in range(1, nz)]
    (mixed,) = call(
        functools.partial(attention_kernel, nz, ny, heads, hd),
        place,
        [
            hbm(key_in),
            hbm(value_in),
            hbm(query),
            hbm(gate_in),
            *[anywhere(x) for x in kvs],
            *[anywhere(x) for x in qgs],
            *entering,
            c_row,
            c_col,
            (attn_gain_2, pl.BlockSpec((1, width), lambda n, s: (0, s[1]))),
        ],
        [sds((long, width), BF16)],
        [pltpu.VMEM((long, width), BF16)] * 4
        + [pltpu.VMEM((heads, hd, hd), BF16), pltpu.SemaphoreType.DMA((4 * ny,))],
        limit=40,
            flops=4 * long * long * width,
    )

    def across(blocks):
        return [[y_turn(x, e) for x in blocks] for e in range(1, ny)]

    held = {0: [[mixed]] + across([mixed])}
    for d in near:
        held[d] = [[z_turn(mixed, d)]]
    free = behind([mixed], [held[d][0][0] for d in near])[0]
    for d in near:
        held[d] += across(held[d][0])
    halves = [free[: long // 2], free[long // 2 :]]
    for d in distant:
        held[d] = [[z_turn(x, d) for x in halves]]
    for d in distant:
        held[d] += across(held[d][0])
    w_parts = [
        (w_out, pl.BlockSpec((width, cols), lambda n, s, d=d: (lax.rem(s[1] + ny - d, ny), 0)))
        for d in range(ny)
    ]
    given = []
    for group in ([0] + near, distant):
        last = group is distant
        dzs = {d: held[d][0] for d in group}
        blocks = [x for dy in range(ny) for d in group for x in held[d][dy]]
        half = nz * slots // 2
        outs = [sds((len(group), block, cols), BF16), sds((nz * slots, cols), F32)]
        if last:
            outs = [sds((half, cols), F32), sds((half, cols), BF16)]
            outs += [sds((nz // 2, block, cols), BF16)] * 2
        given = call(
            functools.partial(project_kernel, nz, ny, cap, dzs, last),
            place,
            [anywhere(x) for x in blocks]
            + w_parts
            + [row_r, row_base, codes]
            + list(given)
            + ([hbm(residual)] if last else []),
            outs,
            [pltpu.VMEM((ny, len(group), long, width), BF16)]
            + ([pltpu.VMEM((block, cols), BF16)] if last else [])
            + [pltpu.SemaphoreType.DMA((len(blocks) + 1,))],
            limit=40,
            flops=2 * len(group) * long * head_width * cols,
        )
    keep, send, keep_all, send_all = given
    for b in range(bits):
        received = swap(send, 1 << b)
        if b < bits - 1:
            part = keep.shape[0] // 2
            send = (keep[part:] + received[part:].astype(F32)).astype(BF16)
            keep = keep[:part] + received[:part].astype(F32)
    (rows_out,) = call(
        rows_kernel,
        place,
        [keep, received, moe_gain_2, router_t, sign],
        [sds((slots, cols + 128), BF16)],
    )
    send_all = behind([send_all], [rows_out])[0]
    for b in range(bits):
        received_all = swap(send_all, 1 << b)
        if b < bits - 1:
            n = keep_all.shape[0] // 2
            both = keep_all.astype(F32) + received_all.astype(F32)
            send_all, keep_all = both[n:].astype(BF16), both[:n].astype(BF16)
    rows = share // ny
    last_rows = behind([last_rows], [rows_out])[0]
    final_rows = jnp.zeros((head_count, rows, hd), F32)
    for d in range(ny):
        sent = lax.dynamic_slice_in_dim(last_rows, (y + d) % ny * rows, rows, 1)
        got = sent if d == 0 else y_turn(sent, d)
        final_rows = lax.dynamic_update_slice_in_dim(
            final_rows, got, (y - d) % ny * heads, 0
        )

    def up(n, group, arrived, state):
        last = n == len(groups) - 1
        outs = [sds((slots, units), F32)] * 2 + [sds((slots, 128), F32)]
        if last:
            outs = [sds((slots, units), BF16), sds((slots, 128), F32)]
        return call(
            functools.partial(up_kernel, nz, ny, group, n == 0, last, features),
            place,
            [arrived[p] for p in group] + list(state) + [anywhere(w_gate), anywhere(w_up)],
            outs,
            [pltpu.VMEM((len(group), units, cols), BF16)] * 2
            + [pltpu.SemaphoreType.DMA((2, len(group)))],
            limit=40,
            flops=4 * len(group) * slots * units * cols,
        )

    def down(n, group, arrived, state):
        last = n == len(groups) - 1
        outs = [sds((slots, cols), F32)]
        if last:
            outs = [sds((ret_rows, cols), BF16)] * nz
        return call(
            functools.partial(down_kernel, nz, ny, cap, group, n == 0, last),
            place,
            [arrived[p] for p in group]
            + list(state)
            + [anywhere(w_down)]
            + ([weight, padded[:, None], own_base.T] if last else []),
            outs,
            [
                pltpu.VMEM((len(group), units, cols), BF16),
                pltpu.SemaphoreType.DMA((len(group),)),
            ],
            limit=40,
            flops=2 * len(group) * slots * units * cols,
        )

    if cols % 128:
        arrived = gather_z(rows_out)
        gather_y(arrived, [])
        order = jnp.stack([(z - dz) % nz * ny + (y - dy) % ny for dz, dy in places])
        at = jnp.argsort(order)
        rows_all = jnp.take(jnp.stack([arrived[p] for p in places]), at, axis=0)
        stats = jnp.sum(rows_all[:, :, cols:].astype(F32), axis=0)
        rows_all = jnp.swapaxes(rows_all[:, :, :cols], 0, 1).reshape(slots, features)
        inverse = lax.rsqrt(jnp.sum(stats[:, :3], axis=1) / features + EPS)[:, None]
        gate = mm(rows_all, w_gate[0], NT) * inverse
        hidden = (gate * sigmoid(gate) * (mm(rows_all, w_up[0], NT) * inverse)).astype(BF16)
        weight = sigmoid(jnp.sum(stats[:, 3:6], axis=1)[:, None] * inverse)
        weight = jnp.broadcast_to(weight, (slots, 128))
    else:
        hidden, weight = stages(up, rows_out)
    state = stages(down, hidden)
    returned = [state[0]] + [swap(state[r], r) for r in range(1, nz)]
    (layer_out,) = call(
        functools.partial(combine_kernel, nz, cap),
        place,
        returned + [keep_all[0], received_all[0], hbm(residual), codes, ret_r, ret_base],
        [sds((block, cols), BF16)],
        [
            pltpu.VMEM((nz * ret_rows, cols), BF16),
            pltpu.VMEM((block, cols), BF16),
            pltpu.SemaphoreType.DMA((1,)),
        ],
    )
    return layer_out, final_rows


def solution(mesh):
    in_specs = (
        P("exp", "seq"),
        P("seq", "exp"),
        P("seq", "exp"),
        P("seq", "exp"),
        P("seq", "exp"),
        P("seq", "exp"),
        P("exp", None, None),
        P("exp"),
        P("exp", "seq"),
        P("seq"),
        P("seq", None),
        P("exp", "seq", None),
        P("exp", "seq", None),
        P("exp", None, "seq"),
        P("exp", None),
        P(),
    )
    out_specs = (P("exp", "seq"), P("exp", "seq", None))
    return jax.shard_map(local, mesh=mesh, in_specs=in_specs, out_specs=out_specs, check_vma=False)
```

```python
import functools
import jax
import jax.numpy as jnp
import numpy as np
from jax import lax
from jax.experimental import pallas as pl
from jax.experimental.pallas import tpu as pltpu
from jax.sharding import PartitionSpec as P

EPS = 1e-05
F32 = jnp.float32
BF16 = jnp.bfloat16
I32 = jnp.int32
HIGHEST = lax.Precision.HIGHEST
NT = (((1,), (1,)), ((), ()))
TN = (((0,), (0,)), ((), ()))
NN = (((1,), (0,)), ((), ()))


def mm(a, b, dims=NN, precision=None):
    return lax.dot_general(a, b, dims, precision=precision, preferred_element_type=F32)


def sigmoid(v):
    return 1.0 / (1.0 + jnp.exp(-v))


def bit_reversed(p, bits):
    r = 0
    for b in range(bits):
        r = r * 2 + ((p >> b) & 1)
    return r


def whole(shape):
    return pl.BlockSpec(tuple(shape), lambda i, s: (0,) * len(shape))


def call(kernel, place, operands, outs, scratch=(), flops=0, limit=40, held=0):
    arrays, specs, moved = [], [], 0
    for item in operands:
        array, spec = item if isinstance(item, tuple) else (item, whole(item.shape))
        arrays.append(array)
        specs.append(spec)
        moved += array.size * array.dtype.itemsize
    moved += sum(o.size * o.dtype.itemsize for o in outs)
    return pl.pallas_call(
        kernel,
        out_shape=list(outs),
        grid_spec=pltpu.PrefetchScalarGridSpec(
            num_scalar_prefetch=1,
            grid=(1,),
            in_specs=specs,
            out_specs=[
                pl.BlockSpec(memory_space=pltpu.VMEM) if n >= len(outs) - held else whole(o.shape)
                for n, o in enumerate(outs)
            ],
            scratch_shapes=list(scratch),
        ),
        compiler_params=pltpu.CompilerParams(vmem_limit_bytes=limit * 1024 * 1024),
        cost_estimate=pl.CostEstimate(flops=flops, bytes_accessed=moved, transcendentals=0),
    )(place, *arrays)


def hbm(array):
    return (array, pl.BlockSpec(memory_space=pltpu.HBM))


def anywhere(array):
    return (array, pl.BlockSpec(memory_space=pl.ANY))


def run_copies(pairs, sem):
    copies = [pltpu.make_async_copy(a, b, sem.at[n]) for n, (a, b) in enumerate(pairs)]
    for c in copies:
        c.start()
    return copies


def one_hot(mask):
    return mask.astype(F32).astype(BF16)


def turned_back(z, back, nz):
    return jnp.where(z < back, z - back + nz, z - back)


def sds(shape, dtype):
    return jax.ShapeDtypeStruct(tuple(shape), dtype)


def pieces(x):
    hi = x.astype(BF16)
    rest = x - hi.astype(F32)
    mid = rest.astype(BF16)
    return hi, mid, (rest - mid.astype(F32)).astype(BF16)


def routing_kernel(nz, cap, own_rows, s, *refs):
    keep = refs[0]
    given = refs[1 : nz + 1]
    base, codes, sign, ids = refs[nz + 1 :]
    j = s[2]
    block = given[0].shape[1]
    for r in range(nz):
        ids[lax.bitwise_xor(j, r)] = given[r][...]
    rows = lax.broadcasted_iota(I32, (block, block), 0)
    cols = lax.broadcasted_iota(I32, (block, block), 1)
    strict = one_hot(rows < cols)
    own = base[...] + j * (nz * cap)
    earlier = [jnp.zeros((1, 1), I32) for _ in range(nz)]
    other = jnp.zeros((own_rows, 1), I32)
    place = lax.broadcasted_iota(I32, (16, block), 0)
    for b in range(nz):
        first, second = ids[b, 0:1, :], ids[b, 1:2, :]
        named = ((place == first) | (place == second)) & (place < nz)
        ranks = mm(one_hot(named), strict).astype(I32)
        slots = []
        for e in range(nz):
            hit = (first == e) | (second == e)
            rank = ranks[e : e + 1, :]
            kept = hit & (rank + earlier[e] < keep[e])
            slots.append(jnp.where(kept, (e * nz + b) * cap + rank, -1))
            earlier[e] = earlier[e] + jnp.sum(hit.astype(I32), axis=1, keepdims=True)
        top = functools.reduce(jnp.maximum, slots)
        rest = functools.reduce(jnp.maximum, [jnp.where(c == top, -1, c) for c in slots])
        codes[b, 0:1, :] = top
        codes[b, 1:2, :] = rest
        holds = (own == top) | (own == rest)
        other = other + jnp.sum(jnp.where(holds, first + second, 0), axis=1, keepdims=True)
    every = lax.broadcasted_iota(I32, sign.shape, 1)
    sign[...] = (every == j).astype(F32) - (every == other - j).astype(F32)


def pack_kernel(s, a, b, out):
    out[0] = a[...]
    out[1] = b[...]


def update_kernel(nz, ny, heads, hd, s, *refs):
    z, y = s[0], s[1]
    n = ny - 1
    k_arg, v_arg = refs[0], refs[1]
    kv = refs[2 : 2 + n]
    logs = refs[2 + n : 2 + n + ny]
    outs = refs[2 + n + ny : 2 + n + ny + nz]
    c_row, c_col, log_all, state, tail, own, sem = refs[2 + n + ny + nz :]
    tok = k_arg.shape[0]
    total_tok = tok * ny
    share = hd // nz
    mine = pl.ds(pl.multiple_of(y * heads * hd, 128), heads * hd)
    copies = run_copies([(x.at[:, mine], own.at[m]) for m, x in enumerate((k_arg, v_arg))], sem)
    for d in range(ny):
        at = pl.multiple_of(lax.rem(y + ny - d, ny) * tok, tok)
        log_all[:, pl.ds(at, tok)] = logs[d][pl.ds(y * heads, heads), :]
    rows = lax.broadcasted_iota(I32, (total_tok, total_tok), 0)
    cols = lax.broadcasted_iota(I32, (total_tok, total_tok), 1)
    c_row[...] = mm(log_all[...], (rows <= cols).astype(F32), precision=HIGHEST)
    c_col[...] = mm((rows >= cols).astype(F32), log_all[...], NT, precision=HIGHEST)
    total = c_row[:, total_tok - 1 : total_tok]
    for c in copies:
        c.wait()
    for h in range(heads):
        add = None
        for d in range(ny):
            at = pl.multiple_of(lax.rem(y + ny - d, ny) * tok, tok)
            lanes = slice(h * hd, (h + 1) * hd)
            pair = own if d == 0 else kv[d - 1]
            key = pair[0, :, lanes].astype(F32)
            decay = jnp.exp(total[h : h + 1, :] - c_col[pl.ds(at, tok), h : h + 1])
            weighted = (key * sigmoid(key) * decay).astype(BF16)
            part = mm(weighted, pair[1, :, lanes], TN)
            add = part if add is None else add + part
        state[h] = add.astype(BF16)
    tail[...] = jnp.zeros_like(tail)
    hi, mid, lo = pieces(total)
    lane = lax.broadcasted_iota(I32, (heads, hd), 1)
    tail[0:heads, :] = jnp.where(
        lane == 0,
        hi.astype(F32),
        jnp.where(lane == 1, mid.astype(F32), jnp.where(lane == 2, lo.astype(F32), 0.0)),
    )
    for d in range(nz):
        at = pl.multiple_of(lax.rem(z + d, nz) * share, share)
        for h in range(heads):
            outs[d][h * share : (h + 1) * share, :] = state[h, pl.ds(at, share), :]
        outs[d][heads * share :, :] = tail[...].astype(BF16)


def prefix_kernel(nz, heads, hd, s, *refs):
    z, y = s[0], s[1]
    parts = refs[:nz]
    start = refs[nz]
    outs = refs[nz + 1 : 2 * nz + 1]
    final, held, entering, run, sem = refs[2 * nz + 1 :]
    share = hd // nz
    source = start.at[
        pl.ds(y * heads, heads), pl.ds(pl.multiple_of(z * share, share), share), :
    ]
    copies = run_copies([(source, run)], sem)
    for d in range(nz):
        held[lax.rem(z + nz - d, nz)] = parts[d][...]
    copies[0].wait()
    for p in range(nz):
        logs = jnp.sum(held[p, heads * share :, :].astype(F32), axis=1, keepdims=True)
        keep = jnp.exp(logs)
        for h in range(heads):
            rows = slice(h * share, (h + 1) * share)
            now = run[h]
            entering[p, rows, :] = now.astype(BF16)
            run[h] = keep[h : h + 1, :] * now + held[p, rows, :].astype(F32)
    final[...] = run[...]
    for d in range(nz):
        outs[d][...] = entering[lax.rem(z + d, nz)]


def attention_kernel(nz, ny, heads, hd, s, *refs):
    z, y = s[0], s[1]
    n = ny - 1
    args = refs[:4]
    kv = refs[4 : 4 + n]
    qg = refs[4 + n : 4 + 2 * n]
    states = refs[4 + 2 * n : 4 + 2 * n + nz]
    c_row, c_col, gain, out, ks, vs, qs, gs, state, sem = refs[4 + 2 * n + nz :]
    tok = args[0].shape[0]
    total_tok = tok * ny
    share = hd // nz
    mine = pl.ds(pl.multiple_of(y * heads * hd, 128), heads * hd)
    moves = []
    for d in range(ny):
        at = pl.ds(pl.multiple_of(lax.rem(y + ny - d, ny) * tok, tok), tok)
        for m, to in enumerate((ks, vs, qs, gs)):
            if d == 0:
                source = args[m].at[:, mine]
            else:
                source = (kv if m < 2 else qg)[d - 1].at[m % 2]
            moves.append((source, to.at[at, :]))
    copies = run_copies(moves, sem)
    for d in range(nz):
        at = pl.ds(pl.multiple_of(lax.rem(z + nz - d, nz) * share, share), share)
        for h in range(heads):
            state[h, at, :] = states[d][h * share : (h + 1) * share, :]
    rows = lax.broadcasted_iota(I32, (total_tok, total_tok), 0)
    cols = lax.broadcasted_iota(I32, (total_tok, total_tok), 1)
    causal = rows >= cols
    for c in copies:
        c.wait()
    for h in range(heads):
        lanes = slice(h * hd, (h + 1) * hd)
        query = qs[:, lanes].astype(F32)
        query = query * sigmoid(query)
        key = ks[:, lanes].astype(F32)
        key = (key * sigmoid(key)).astype(BF16)
        col = c_col[:, h : h + 1]
        gap = jnp.where(causal, col - c_row[h : h + 1, :], 0.0)
        decay = jnp.where(causal, jnp.exp(gap), 0.0)
        scores = mm(query.astype(BF16), key, NT) * decay
        att = mm(scores.astype(BF16), vs[:, lanes])
        att = att + mm((query * jnp.exp(col)).astype(BF16), state[h])
        square = jnp.mean(att * att, axis=1, keepdims=True)
        gate = sigmoid(gs[:, lanes].astype(F32))
        out[:, lanes] = (att * lax.rsqrt(square + EPS) * gain[:, lanes] * gate).astype(BF16)


def project_kernel(nz, ny, cap, dzs, last, s, *refs):
    z, j = s[0], s[2]
    bits = nz.bit_length() - 1
    parts = [len(p) for p in dzs.values()]
    count = sum(parts) * ny
    blocks = refs[:count]
    weights = refs[count : count + ny]
    r_ids, b_ids, codes = refs[count + ny : count + ny + 3]
    refs = refs[count + ny + 3 :]
    if last:
        done, sums, residual = refs[:3]
        keep, send, keep_all, send_all, stacked, own, sem = refs[3:]
    else:
        done, sums, stacked, sem = refs
    rows = stacked.shape[2]
    moves = []
    at = 0
    for dy in range(ny):
        for n, (dz, pieces_of) in enumerate(dzs.items()):
            first = 0
            for _ in pieces_of:
                size = blocks[at].shape[0]
                moves.append((blocks[at], stacked.at[dy, n, pl.ds(first, size)]))
                first += size
                at += 1
    if last:
        moves.append((residual, own))
    copies = run_copies(moves, sem)
    ids = lax.bitwise_xor(r_ids[...], j) * (nz * cap) + b_ids[...]
    pick = lambda b: one_hot((ids == codes[b, 0:1, :]) | (ids == codes[b, 1:2, :]))
    total_rows = sums[...] if last else None
    for c in copies:
        c.wait()
    projected = {}
    for n, dz in enumerate(dzs):
        total = None
        for dy in range(ny):
            part = mm(stacked[dy, n], weights[dy][...])
            total = part if total is None else total + part
        projected[dz] = total.astype(BF16)
        part = mm(pick(lax.rem(z + nz - dz, nz)), projected[dz])
        total_rows = part if total_rows is None else total_rows + part
    if not last:
        for n, dz in enumerate(dzs):
            done[n] = projected[dz]
        sums[...] = total_rows
        return
    total_rows = total_rows + mm(pick(j), own[...])
    half = keep.shape[0]
    keep[...] = total_rows[:half, :]
    send[...] = total_rows[half:, :].astype(BF16)
    before = [dz for dz in range(nz) if dz not in dzs]
    for p in range(nz):
        block = lax.bitwise_xor(jnp.int32(bit_reversed(p, bits)), j)
        away = lax.rem(z + nz - block, nz)
        to = keep_all.at[p] if p < nz // 2 else send_all.at[p - nz // 2]
        for dz in range(nz):

            @pl.when(away == dz)
            def _(dz=dz):
                to[...] = projected[dz] if dz in dzs else done[before.index(dz)]


def rows_kernel(s, keep, received, gain, router_t, sign, out):
    width = gain.shape[1]
    rows = keep[...] + received[...].astype(F32)
    square = jnp.sum(rows * rows, axis=1, keepdims=True)
    scaled = rows * gain[...]
    logits = mm(scaled, router_t[...], NT, precision=HIGHEST)
    gap = jnp.sum(logits * sign[...], axis=1, keepdims=True)
    out[:, :width] = scaled.astype(BF16)
    lane = lax.broadcasted_iota(I32, (rows.shape[0], 128), 1)
    stats = jnp.zeros((rows.shape[0], 128), F32)
    for at, value in ((0, square), (3, gap)):
        for k, piece in enumerate(pieces(value)):
            stats = jnp.where(lane == at + k, piece.astype(F32), stats)
    out[:, width:] = stats.astype(BF16)


def source_of(s, nz, ny, place):
    z = lax.rem(s[0] + nz - place[0], nz)
    return z * ny + lax.rem(s[1] + ny - place[1], ny)


def throttled(copies, n, depth):
    if n < 0:
        for c in copies[:depth]:
            c.start()
        return
    copies[n].wait()
    if n + depth < len(copies):
        copies[n + depth].start()


def up_kernel(nz, ny, places, ahead, first, last, features, s, *refs):
    count = len(places)
    blocks = refs[:count]
    refs = refs[count:]
    before = () if first else refs[:3]
    refs = refs[0 if first else 3 :]
    weights = refs[:2]
    refs = refs[2:]
    if last:
        outs, buffers, sem = refs[:2], refs[2:4], refs[4]
    elif ahead:
        outs, kept, buffers, sem = refs[:3], refs[3:5], refs[5:7], refs[7]
    else:
        outs, buffers, sem = refs[:3], refs[3:5], refs[5]
    width = blocks[0].shape[1] - 128

    copies = []
    if True:
        jobs = [(p, buffers, n) for n, p in enumerate(places)]
        jobs += [(p, kept, n) for n, p in enumerate(ahead)]
        for p, to, n in jobs:
            lanes = pl.ds(pl.multiple_of(source_of(s, nz, ny, p) * width, 128), width)
            for m in range(2):
                source = weights[m].at[0, :, lanes]
                copies.append(pltpu.make_async_copy(source, to[m].at[n], sem.at[len(copies)]))
        throttled(copies, -1, 4)
    gate, up, stats = (None, None, None) if first else (b[...] for b in before)
    for n in range(count):
        rows = blocks[n][:, :width]
        part = blocks[n][:, width:].astype(F32)
        stats = part if stats is None else stats + part
        if True:
            throttled(copies, 2 * n, 4)
        part = mm(rows, buffers[0][n], NT)
        gate = part if gate is None else gate + part
        if True:
            throttled(copies, 2 * n + 1, 4)
        part = mm(rows, buffers[1][n], NT)
        up = part if up is None else up + part
    if not last:
        outs[0][...] = gate
        outs[1][...] = up
        outs[2][...] = stats
        for n in range(2 * count, len(copies)):
            throttled(copies, n, 4)
        return
    square = stats[:, 0:1] + stats[:, 1:2] + stats[:, 2:3]
    gap = stats[:, 3:4] + stats[:, 4:5] + stats[:, 5:6]
    inverse = lax.rsqrt(square / features + EPS)
    gate = gate * inverse
    outs[0][...] = (gate * sigmoid(gate) * (up * inverse)).astype(BF16)
    outs[1][...] = jnp.broadcast_to(sigmoid(gap * inverse), outs[1].shape)


def down_kernel(nz, ny, cap, places, ahead, first, last, s, *refs):
    j = s[2]
    count = len(places)
    blocks = refs[:count]
    refs = refs[count:]
    before = None if first else refs[0]
    refs = refs[0 if first else 1 :]
    w_down = refs[0]
    refs = refs[1:]
    depth = blocks[0].shape[1]
    copies = []
    if last:
        weight, out_base, row_base = refs[:3]
        outs, buf = refs[3:], w_down
    else:
        outs = refs[:1]
        kept = refs[1] if ahead else None
        buf, sem = refs[-2:]
        jobs = [(p, buf, n) for n, p in enumerate(places)]
        jobs += [(p, kept, n) for n, p in enumerate(ahead)]
        for p, to, n in jobs:
            at = pl.ds(pl.multiple_of(source_of(s, nz, ny, p) * depth, depth), depth)
            source = w_down.at[0, at, :]
            copies.append(pltpu.make_async_copy(source, to.at[n], sem.at[len(copies)]))
        throttled(copies, -1, 3)
    total = None if first else before[...]
    for n in range(count):
        if not last:
            throttled(copies, n, 3)
        part = mm(blocks[n][...], buf[n])
        total = part if total is None else total + part
    if not last:
        outs[0][...] = total
        for n in range(count, len(copies)):
            throttled(copies, n, 3)
        return
    result = (total * weight[:, 0:1]).astype(BF16)
    for r, out in enumerate(outs):
        wanted = out_base[...] + lax.bitwise_xor(j, r) * cap
        out[...] = mm(one_hot(wanted == row_base[...]), result).astype(BF16)


def combine_kernel(nz, cap, s, *refs):
    j = s[2]
    returned = refs[:nz]
    keep, received, residual, codes, ret_r, ret_base, out, stacked, own, sem = refs[nz:]
    copies = run_copies([(residual, own)], sem)
    rows = returned[0].shape[0]
    for n in range(nz):
        stacked[n * rows : (n + 1) * rows, :] = returned[n][...]
    ids = lax.bitwise_xor(ret_r[...], j) * (nz * cap) + ret_base[...] + j * cap
    pick = (ids == codes[j, 0:1, :]) | (ids == codes[j, 1:2, :])
    added = mm(one_hot(pick), stacked[...], TN)
    copies[0].wait()
    total = own[...].astype(F32) + (keep[...].astype(F32) + received[...].astype(F32))
    out[...] = (total + added).astype(BF16)


def local(
    residual,
    query,
    key_in,
    value_in,
    gate_in,
    log_decay,
    state_in,
    attn_gain,
    w_out,
    moe_gain,
    router,
    w_gate,
    w_up,
    w_down,
    expert_ids,
    keep_counts,
):
    nz = lax.axis_size("exp")
    ny = lax.axis_size("seq") // nz
    bits = nz.bit_length() - 1
    i = lax.axis_index("seq").astype(I32)
    j = lax.axis_index("exp").astype(I32)
    z, y = i // ny, i % ny
    place = jnp.stack([z, y, j])

    tok, head_width = query.shape
    head_count, hd = state_in.shape[0], state_in.shape[2]
    heads = head_count // ny
    width = heads * hd
    block, cols = residual.shape
    features = w_gate.shape[2]
    units = w_gate.shape[1]
    experts = router.shape[1]
    cap = 5 * block * nz // (2 * nz * experts)
    slots = nz * cap

    def z_turn(a, d):
        pairs = [(p * ny + q, (p + d) % nz * ny + q) for p in range(nz) for q in range(ny)]
        return lax.ppermute(a, "seq", pairs)

    def y_turn(a, d):
        pairs = [(p * ny + q, p * ny + (q + d) % ny) for p in range(nz) for q in range(ny)]
        return lax.ppermute(a, "seq", pairs)

    def swap(a, r):
        return lax.ppermute(a, "exp", [(p, p ^ r) for p in range(nz)])

    z_order = sorted(range(1, nz), key=lambda d: (min(d, nz - d), d))
    near = [d for d in z_order if min(d, nz - d) == 1]
    distant = [d for d in z_order if d not in near]
    places = [(dz, dy) for dy in range(ny) for dz in range(nz)]

    def behind(values, events):
        return list(lax.optimization_barrier((tuple(values), tuple(events)))[0])

    def gather_z(a):
        held = {(0, 0): a}
        for d in range(1, ny):
            held[0, d] = y_turn(a, d)
        for d in z_order:
            held[d, 0] = z_turn(a, d)
        return held

    def gather_y(held, events):
        for d in z_order:
            x = held[d, 0] = behind([held[d, 0]], events)[0]
            for e in range(1, ny):
                held[d, e] = y_turn(x, e)

    def stages(run, a):
        arrived = gather_z(a)
        state = run(0, groups[0], arrived, [])
        gather_y(arrived, state)
        for n in (1, 2):
            state = run(n, groups[n], arrived, state)
        return state

    groups = [[(0, 0)], [(0, d) for d in range(1, ny)] + [(d, 0) for d in z_order]]
    groups.append([(d, e) for d in z_order for e in range(1, ny)])

    slot = np.arange(cap)
    row_r = np.repeat([bit_reversed(p, bits) for p in range(nz)], slots).astype(np.int32)[:, None]
    row_base = np.tile((np.arange(nz)[:, None] * cap + slot).reshape(slots), nz)
    row_base = row_base.astype(np.int32)[:, None]
    own_base = row_base[:slots]
    ret_rows = cap + -cap % 16
    padded = np.where(np.arange(ret_rows) < cap, np.arange(ret_rows), -(10**8)).astype(np.int32)
    ret_r = np.repeat(np.arange(nz), ret_rows).astype(np.int32)[:, None]
    ret_base = np.tile(padded, nz)[:, None]

    logs_t = jnp.transpose(log_decay)
    logs, kvs, qgs = [logs_t], [], []
    for d in range(1, ny):
        there = pl.BlockSpec((tok, width), lambda n, s, d=d: (0, lax.rem(s[1] + d, ny)))
        out = [sds((2, tok, width), BF16)]
        (kv,) = call(pack_kernel, place, [(key_in, there), (value_in, there)], out, limit=60)
        kvs.append(y_turn(kv, d))
        logs.append(y_turn(logs_t, d))
        qgs += call(pack_kernel, place, [(query, there), (gate_in, there)], out, limit=60)
    ids = jnp.transpose(expert_ids)
    codes, sign = call(
        functools.partial(routing_kernel, nz, cap, slots),
        place,
        [(keep_counts, pl.BlockSpec(memory_space=pltpu.SMEM))]
        + [ids]
        + [swap(ids, r) for r in range(1, nz)]
        + [own_base],
        [sds((nz, 2, block), I32), sds((slots, experts), F32)],
        [pltpu.VMEM((nz, 2, block), I32)],
    )
    attn_gain_2, moe_gain_2, router_t = attn_gain[None], moe_gain[None], jnp.transpose(router)
    prepared = [codes, sign, attn_gain_2, moe_gain_2]
    qgs = [y_turn(qg, d + 1) for d, qg in enumerate(behind(qgs, kvs + logs + prepared))]
    share = hd // nz
    long = tok * ny
    *parts, c_row, c_col = call(
        functools.partial(update_kernel, nz, ny, heads, hd),
        place,
        [hbm(key_in), hbm(value_in), *kvs, *logs],
        [sds((heads * share + 16, hd), BF16)] * nz
        + [sds((heads, long), F32), sds((long, heads), F32)],
        [
            pltpu.VMEM((heads, long), F32),
            pltpu.VMEM((heads, hd, hd), BF16),
            pltpu.VMEM((16, hd), F32),
            pltpu.VMEM((2, tok, width), BF16),
            pltpu.SemaphoreType.DMA((2,)),
        ],
        limit=40,
            flops=2 * long * hd * hd * heads,
    )
    parts = [parts[0]] + [z_turn(parts[d], d) for d in range(1, nz)]
    *entering, last_rows = call(
        functools.partial(prefix_kernel, nz, heads, hd),
        place,
        [*parts, hbm(state_in)],
        [sds((heads * share, hd), BF16)] * nz + [sds((heads, share, hd), F32)],
        [
            pltpu.VMEM((nz, heads * share + 16, hd), BF16),
            pltpu.VMEM((nz, heads * share, hd), BF16),
            pltpu.VMEM((heads, share, hd), F32),
            pltpu.SemaphoreType.DMA((1,)),
        ],
    )
    entering = [entering[0]] + [z_turn(entering[d], d) for d in range(1, nz)]
    (mixed,) = call(
        functools.partial(attention_kernel, nz, ny, heads, hd),
        place,
        [
            hbm(key_in),
            hbm(value_in),
            hbm(query),
            hbm(gate_in),
            *[anywhere(x) for x in kvs],
            *[anywhere(x) for x in qgs],
            *entering,
            c_row,
            c_col,
            (attn_gain_2, pl.BlockSpec((1, width), lambda n, s: (0, s[1]))),
        ],
        [sds((long, width), BF16)],
        [pltpu.VMEM((long, width), BF16)] * 4
        + [pltpu.VMEM((heads, hd, hd), BF16), pltpu.SemaphoreType.DMA((4 * ny,))],
        limit=40,
            flops=4 * long * long * width,
    )

    def across(blocks):
        return [[y_turn(x, e) for x in blocks] for e in range(1, ny)]

    held = {0: [[mixed]] + across([mixed])}
    for d in near:
        held[d] = [[z_turn(mixed, d)]]
    free = behind([mixed], [held[near[0]][0][0]])[0]
    for d in near:
        held[d] += across(held[d][0])
    halves = [free[: long // 2], free[long // 2 :]]
    for d in distant:
        held[d] = [[z_turn(x, d) for x in halves]]
    for d in distant:
        held[d] += across(held[d][0])
    w_parts = [
        (w_out, pl.BlockSpec((width, cols), lambda n, s, d=d: (lax.rem(s[1] + ny - d, ny), 0)))
        for d in range(ny)
    ]
    given = []
    for group in ([0] + near, distant):
        last = group is distant
        dzs = {d: held[d][0] for d in group}
        blocks = [x for dy in range(ny) for d in group for x in held[d][dy]]
        half = nz * slots // 2
        outs = [sds((len(group), block, cols), BF16), sds((nz * slots, cols), F32)]
        if last:
            outs = [sds((half, cols), F32), sds((half, cols), BF16)]
            outs += [sds((nz // 2, block, cols), BF16)] * 2
        given = call(
            functools.partial(project_kernel, nz, ny, cap, dzs, last),
            place,
            [anywhere(x) for x in blocks]
            + w_parts
            + [row_r, row_base, codes]
            + list(given)
            + ([hbm(residual)] if last else []),
            outs,
            [pltpu.VMEM((ny, len(group), long, width), BF16)]
            + ([pltpu.VMEM((block, cols), BF16)] if last else [])
            + [pltpu.SemaphoreType.DMA((len(blocks) + 1,))],
            limit=40,
            flops=2 * len(group) * long * head_width * cols,
        )
    keep, send, keep_all, send_all = given
    for b in range(bits):
        received = swap(send, 1 << b)
        if b < bits - 1:
            part = keep.shape[0] // 2
            send = (keep[part:] + received[part:].astype(F32)).astype(BF16)
            keep = keep[:part] + received[:part].astype(F32)
    (rows_out,) = call(
        rows_kernel,
        place,
        [keep, received, moe_gain_2, router_t, sign],
        [sds((slots, cols + 128), BF16)],
    )
    send_all = behind([send_all], [rows_out])[0]
    for b in range(bits):
        received_all = swap(send_all, 1 << b)
        if b < bits - 1:
            n = keep_all.shape[0] // 2
            both = keep_all.astype(F32) + received_all.astype(F32)
            send_all, keep_all = both[n:].astype(BF16), both[:n].astype(BF16)
    rows = share // ny
    last_rows = behind([last_rows], [rows_out])[0]
    final_rows = jnp.zeros((head_count, rows, hd), F32)
    for d in range(ny):
        sent = lax.dynamic_slice_in_dim(last_rows, (y + d) % ny * rows, rows, 1)
        got = sent if d == 0 else y_turn(sent, d)
        final_rows = lax.dynamic_update_slice_in_dim(
            final_rows, got, (y - d) % ny * heads, 0
        )

    in_vmem = pl.BlockSpec(memory_space=pltpu.VMEM)

    def up(n, group, arrived, state):
        first, last = n == 0, n == len(groups) - 1
        ahead = []
        outs = [sds((slots, units), F32)] * 2 + [sds((slots, 128), F32)]
        outs += [sds((len(ahead), units, cols), BF16)] * (2 if ahead else 0)
        weights = [anywhere(w_gate), anywhere(w_up)]
        if last:
            outs = [sds((slots, units), BF16), sds((slots, 128), F32)]
        state = call(
            functools.partial(up_kernel, nz, ny, group, ahead, first, last, features),
            place,
            [arrived[p] for p in group] + list(state) + weights,
            outs,
            [pltpu.VMEM((len(group), units, cols), BF16)] * 2
            + [pltpu.SemaphoreType.DMA((2 * (len(group) + len(ahead)),))],
            limit=40,
            flops=4 * len(group) * slots * units * cols,
            held=2 if ahead else 0,
        )
        if ahead:
            fetched["up"] = state[3:]
        return state[:3]

    def down(n, group, arrived, state):
        first, last = n == 0, n == len(groups) - 1
        ahead = groups[-1] if first else []
        outs = [sds((slots, cols), F32)]
        outs += [sds((len(ahead), units, cols), BF16)] if ahead else []
        weights = [anywhere(w_down)]
        if last:
            outs = [sds((ret_rows, cols), BF16)] * nz
            weights = [(fetched["down"], in_vmem), weight, padded[:, None], own_base.T]
        state = call(
            functools.partial(down_kernel, nz, ny, cap, group, ahead, first, last),
            place,
            [arrived[p] for p in group] + list(state) + weights,
            outs,
            []
            if last
            else [
                pltpu.VMEM((len(group), units, cols), BF16),
                pltpu.SemaphoreType.DMA((len(group) + len(ahead),)),
            ],
            limit=40,
            flops=2 * len(group) * slots * units * cols,
            held=1 if ahead else 0,
        )
        if ahead:
            fetched["down"] = state[1]
        return state if last else state[:1]

    fetched = {}
    if cols % 128:
        arrived = gather_z(rows_out)
        gather_y(arrived, [])
        order = jnp.stack([(z - dz) % nz * ny + (y - dy) % ny for dz, dy in places])
        at = jnp.argsort(order)
        rows_all = jnp.take(jnp.stack([arrived[p] for p in places]), at, axis=0)
        stats = jnp.sum(rows_all[:, :, cols:].astype(F32), axis=0)
        rows_all = jnp.swapaxes(rows_all[:, :, :cols], 0, 1).reshape(slots, features)
        inverse = lax.rsqrt(jnp.sum(stats[:, :3], axis=1) / features + EPS)[:, None]
        gate = mm(rows_all, w_gate[0], NT) * inverse
        hidden = (gate * sigmoid(gate) * (mm(rows_all, w_up[0], NT) * inverse)).astype(BF16)
        weight = sigmoid(jnp.sum(stats[:, 3:6], axis=1)[:, None] * inverse)
        weight = jnp.broadcast_to(weight, (slots, 128))
    else:
        hidden, weight = stages(up, rows_out)
    state = stages(down, hidden)
    returned = [state[0]] + [swap(state[r], r) for r in range(1, nz)]
    (layer_out,) = call(
        functools.partial(combine_kernel, nz, cap),
        place,
        returned + [keep_all[0], received_all[0], hbm(residual), codes, ret_r, ret_base],
        [sds((block, cols), BF16)],
        [
            pltpu.VMEM((nz * ret_rows, cols), BF16),
            pltpu.VMEM((block, cols), BF16),
            pltpu.SemaphoreType.DMA((1,)),
        ],
    )
    return layer_out, final_rows


def solution(mesh):
    in_specs = (
        P("exp", "seq"),
        P("seq", "exp"),
        P("seq", "exp"),
        P("seq", "exp"),
        P("seq", "exp"),
        P("seq", "exp"),
        P("exp", None, None),
        P("exp"),
        P("exp", "seq"),
        P("seq"),
        P("seq", None),
        P("exp", "seq", None),
        P("exp", "seq", None),
        P("exp", None, "seq"),
        P("exp", None),
        P(),
    )
    out_specs = (P("exp", "seq"), P("exp", "seq", None))
    return jax.shard_map(local, mesh=mesh, in_specs=in_specs, out_specs=out_specs, check_vma=False)
```

```python
import functools
import jax
import jax.numpy as jnp
import numpy as np
from jax import lax
from jax.experimental import pallas as pl
from jax.experimental.pallas import tpu as pltpu
from jax.sharding import PartitionSpec as P

EPS = 1e-05
F32 = jnp.float32
BF16 = jnp.bfloat16
I32 = jnp.int32
HIGHEST = lax.Precision.HIGHEST
NT = (((1,), (1,)), ((), ()))
TN = (((0,), (0,)), ((), ()))
NN = (((1,), (0,)), ((), ()))


def mm(a, b, dims=NN, precision=None):
    return lax.dot_general(a, b, dims, precision=precision, preferred_element_type=F32)


def sigmoid(v):
    return 1.0 / (1.0 + jnp.exp(-v))


def bit_reversed(p, bits):
    r = 0
    for b in range(bits):
        r = r * 2 + ((p >> b) & 1)
    return r


def whole(shape):
    return pl.BlockSpec(tuple(shape), lambda i, s: (0,) * len(shape))


def call(kernel, place, operands, outs, scratch=(), flops=0, limit=40, held=0):
    arrays, specs, moved = [], [], 0
    for item in operands:
        array, spec = item if isinstance(item, tuple) else (item, whole(item.shape))
        arrays.append(array)
        specs.append(spec)
        moved += array.size * array.dtype.itemsize
    moved += sum(o.size * o.dtype.itemsize for o in outs)
    return pl.pallas_call(
        kernel,
        out_shape=list(outs),
        grid_spec=pltpu.PrefetchScalarGridSpec(
            num_scalar_prefetch=1,
            grid=(1,),
            in_specs=specs,
            out_specs=[
                pl.BlockSpec(memory_space=pltpu.VMEM) if n >= len(outs) - held else whole(o.shape)
                for n, o in enumerate(outs)
            ],
            scratch_shapes=list(scratch),
        ),
        compiler_params=pltpu.CompilerParams(vmem_limit_bytes=limit * 1024 * 1024),
        cost_estimate=pl.CostEstimate(flops=flops, bytes_accessed=moved, transcendentals=0),
    )(place, *arrays)


def hbm(array):
    return (array, pl.BlockSpec(memory_space=pltpu.HBM))


def anywhere(array):
    return (array, pl.BlockSpec(memory_space=pl.ANY))


def run_copies(pairs, sem):
    copies = [pltpu.make_async_copy(a, b, sem.at[n]) for n, (a, b) in enumerate(pairs)]
    for c in copies:
        c.start()
    return copies


def one_hot(mask):
    return mask.astype(F32).astype(BF16)


def turned_back(z, back, nz):
    return jnp.where(z < back, z - back + nz, z - back)


def sds(shape, dtype):
    return jax.ShapeDtypeStruct(tuple(shape), dtype)


def pieces(x):
    hi = x.astype(BF16)
    rest = x - hi.astype(F32)
    mid = rest.astype(BF16)
    return hi, mid, (rest - mid.astype(F32)).astype(BF16)


def routing_kernel(nz, cap, own_rows, s, *refs):
    keep = refs[0]
    given = refs[1 : nz + 1]
    base, state, codes, sign, start, ids, sem = refs[nz + 1 :]
    j = s[2]
    heads, share, _ = start.shape
    rows = pl.ds(pl.multiple_of(s[0] * share, share), share)
    fetch = pltpu.make_async_copy(state.at[pl.ds(s[1] * heads, heads), rows, :], start, sem)
    fetch.start()
    block = given[0].shape[1]
    for r in range(nz):
        ids[lax.bitwise_xor(j, r)] = given[r][...]
    rows = lax.broadcasted_iota(I32, (block, block), 0)
    cols = lax.broadcasted_iota(I32, (block, block), 1)
    strict = one_hot(rows < cols)
    own = base[...] + j * (nz * cap)
    earlier = [jnp.zeros((1, 1), I32) for _ in range(nz)]
    other = jnp.zeros((own_rows, 1), I32)
    place = lax.broadcasted_iota(I32, (16, block), 0)
    for b in range(nz):
        first, second = ids[b, 0:1, :], ids[b, 1:2, :]
        named = ((place == first) | (place == second)) & (place < nz)
        ranks = mm(one_hot(named), strict).astype(I32)
        slots = []
        for e in range(nz):
            hit = (first == e) | (second == e)
            rank = ranks[e : e + 1, :]
            kept = hit & (rank + earlier[e] < keep[e])
            slots.append(jnp.where(kept, (e * nz + b) * cap + rank, -1))
            earlier[e] = earlier[e] + jnp.sum(hit.astype(I32), axis=1, keepdims=True)
        top = functools.reduce(jnp.maximum, slots)
        rest = functools.reduce(jnp.maximum, [jnp.where(c == top, -1, c) for c in slots])
        codes[b, 0:1, :] = top
        codes[b, 1:2, :] = rest
        holds = (own == top) | (own == rest)
        other = other + jnp.sum(jnp.where(holds, first + second, 0), axis=1, keepdims=True)
    every = lax.broadcasted_iota(I32, sign.shape, 1)
    sign[...] = (every == j).astype(F32) - (every == other - j).astype(F32)
    fetch.wait()


def pack_kernel(away, ny, a, b, out, sem):
    width = out.shape[2]
    share = lax.rem(lax.rem(lax.axis_index("seq"), ny) + away, ny)
    at = pl.ds(pl.multiple_of(share * width, 128), width)
    for c in run_copies([(a.at[:, at], out.at[0]), (b.at[:, at], out.at[1])], sem):
        c.wait()


def update_kernel(nz, ny, heads, hd, s, *refs):
    z, y = s[0], s[1]
    n = ny - 1
    k_arg, v_arg = refs[0], refs[1]
    kv = refs[2 : 2 + n]
    logs = refs[2 + n : 2 + n + ny]
    outs = refs[2 + n + ny : 2 + n + ny + nz]
    c_row, c_col, log_all, state, tail, own, sem = refs[2 + n + ny + nz :]
    tok = k_arg.shape[0]
    total_tok = tok * ny
    share = hd // nz
    mine = pl.ds(pl.multiple_of(y * heads * hd, 128), heads * hd)
    copies = run_copies([(x.at[:, mine], own.at[m]) for m, x in enumerate((k_arg, v_arg))], sem)
    for d in range(ny):
        at = pl.multiple_of(lax.rem(y + ny - d, ny) * tok, tok)
        log_all[:, pl.ds(at, tok)] = logs[d][pl.ds(y * heads, heads), :]
    rows = lax.broadcasted_iota(I32, (total_tok, total_tok), 0)
    cols = lax.broadcasted_iota(I32, (total_tok, total_tok), 1)
    c_row[...] = mm(log_all[...], (rows <= cols).astype(F32), precision=HIGHEST)
    c_col[...] = mm((rows >= cols).astype(F32), log_all[...], NT, precision=HIGHEST)
    total = c_row[:, total_tok - 1 : total_tok]
    for c in copies:
        c.wait()
    for h in range(heads):
        add = None
        for d in range(ny):
            at = pl.multiple_of(lax.rem(y + ny - d, ny) * tok, tok)
            lanes = slice(h * hd, (h + 1) * hd)
            pair = own if d == 0 else kv[d - 1]
            key = pair[0, :, lanes].astype(F32)
            decay = jnp.exp(total[h : h + 1, :] - c_col[pl.ds(at, tok), h : h + 1])
            weighted = (key * sigmoid(key) * decay).astype(BF16)
            part = mm(weighted, pair[1, :, lanes], TN)
            add = part if add is None else add + part
        state[h] = add.astype(BF16)
    tail[...] = jnp.zeros_like(tail)
    hi, mid, lo = pieces(total)
    lane = lax.broadcasted_iota(I32, (heads, hd), 1)
    tail[0:heads, :] = jnp.where(
        lane == 0,
        hi.astype(F32),
        jnp.where(lane == 1, mid.astype(F32), jnp.where(lane == 2, lo.astype(F32), 0.0)),
    )
    for d in range(nz):
        at = pl.multiple_of(lax.rem(z + d, nz) * share, share)
        for h in range(heads):
            outs[d][h * share : (h + 1) * share, :] = state[h, pl.ds(at, share), :]
        outs[d][heads * share :, :] = tail[...].astype(BF16)


def prefix_kernel(nz, heads, hd, s, *refs):
    z = s[0]
    parts = refs[:nz]
    start = refs[nz]
    outs = refs[nz + 1 : 2 * nz + 1]
    final, held, entering, run = refs[2 * nz + 1 :]
    share = hd // nz
    run[...] = start[...]
    for d in range(nz):
        held[lax.rem(z + nz - d, nz)] = parts[d][...]
    for p in range(nz):
        logs = jnp.sum(held[p, heads * share :, :].astype(F32), axis=1, keepdims=True)
        keep = jnp.exp(logs)
        for h in range(heads):
            rows = slice(h * share, (h + 1) * share)
            now = run[h]
            entering[p, rows, :] = now.astype(BF16)
            run[h] = keep[h : h + 1, :] * now + held[p, rows, :].astype(F32)
    final[...] = run[...]
    for d in range(nz):
        outs[d][...] = entering[lax.rem(z + d, nz)]


def attention_kernel(nz, ny, heads, hd, s, *refs):
    z, y = s[0], s[1]
    n = ny - 1
    args = refs[:4]
    kv = refs[4 : 4 + n]
    qg = refs[4 + n : 4 + 2 * n]
    states = refs[4 + 2 * n : 4 + 2 * n + nz]
    c_row, c_col, gain, out, ks, vs, qs, gs, state, sem = refs[4 + 2 * n + nz :]
    tok = args[0].shape[0]
    total_tok = tok * ny
    share = hd // nz
    mine = pl.ds(pl.multiple_of(y * heads * hd, 128), heads * hd)
    moves = []
    for d in range(ny):
        at = pl.ds(pl.multiple_of(lax.rem(y + ny - d, ny) * tok, tok), tok)
        for m, to in enumerate((ks, vs, qs, gs)):
            if d == 0:
                source = args[m].at[:, mine]
            else:
                source = (kv if m < 2 else qg)[d - 1].at[m % 2]
            moves.append((source, to.at[at, :]))
    copies = run_copies(moves, sem)
    for d in range(nz):
        at = pl.ds(pl.multiple_of(lax.rem(z + nz - d, nz) * share, share), share)
        for h in range(heads):
            state[h, at, :] = states[d][h * share : (h + 1) * share, :]
    rows = lax.broadcasted_iota(I32, (total_tok, total_tok), 0)
    cols = lax.broadcasted_iota(I32, (total_tok, total_tok), 1)
    causal = rows >= cols
    for c in copies:
        c.wait()
    for h in range(heads):
        lanes = slice(h * hd, (h + 1) * hd)
        query = qs[:, lanes].astype(F32)
        query = query * sigmoid(query)
        key = ks[:, lanes].astype(F32)
        key = (key * sigmoid(key)).astype(BF16)
        col = c_col[:, h : h + 1]
        gap = jnp.where(causal, col - c_row[h : h + 1, :], 0.0)
        decay = jnp.where(causal, jnp.exp(gap), 0.0)
        scores = mm(query.astype(BF16), key, NT) * decay
        att = mm(scores.astype(BF16), vs[:, lanes])
        att = att + mm((query * jnp.exp(col)).astype(BF16), state[h])
        square = jnp.mean(att * att, axis=1, keepdims=True)
        gate = sigmoid(gs[:, lanes].astype(F32))
        out[:, lanes] = (att * lax.rsqrt(square + EPS) * gain[:, lanes] * gate).astype(BF16)


def project_kernel(nz, ny, cap, dzs, last, s, *refs):
    z, j = s[0], s[2]
    bits = nz.bit_length() - 1
    parts = [len(p) for p in dzs.values()]
    count = sum(parts) * ny
    blocks = refs[:count]
    weights = refs[count : count + ny]
    r_ids, b_ids, codes = refs[count + ny : count + ny + 3]
    refs = refs[count + ny + 3 :]
    if last:
        done, sums, residual = refs[:3]
        keep, send, keep_all, send_all, stacked, own, sem = refs[3:]
    else:
        done, sums, stacked, sem = refs
    rows = stacked.shape[2]
    moves = []
    at = 0
    for dy in range(ny):
        for n, (dz, pieces_of) in enumerate(dzs.items()):
            first = 0
            for _ in pieces_of:
                size = blocks[at].shape[0]
                moves.append((blocks[at], stacked.at[dy, n, pl.ds(first, size)]))
                first += size
                at += 1
    if last:
        moves.append((residual, own))
    copies = run_copies(moves, sem)
    ids = lax.bitwise_xor(r_ids[...], j) * (nz * cap) + b_ids[...]
    pick = lambda b: one_hot((ids == codes[b, 0:1, :]) | (ids == codes[b, 1:2, :]))
    total_rows = sums[...] if last else None
    for c in copies:
        c.wait()
    projected = {}
    for n, dz in enumerate(dzs):
        total = None
        for dy in range(ny):
            part = mm(stacked[dy, n], weights[dy][...])
            total = part if total is None else total + part
        projected[dz] = total.astype(BF16)
        part = mm(pick(lax.rem(z + nz - dz, nz)), projected[dz])
        total_rows = part if total_rows is None else total_rows + part
    if not last:
        for n, dz in enumerate(dzs):
            done[n] = projected[dz]
        sums[...] = total_rows
        return
    total_rows = total_rows + mm(pick(j), own[...])
    half = keep.shape[0]
    keep[...] = total_rows[:half, :]
    send[...] = total_rows[half:, :].astype(BF16)
    before = [dz for dz in range(nz) if dz not in dzs]
    for p in range(nz):
        block = lax.bitwise_xor(jnp.int32(bit_reversed(p, bits)), j)
        away = lax.rem(z + nz - block, nz)
        to = keep_all.at[p] if p < nz // 2 else send_all.at[p - nz // 2]
        for dz in range(nz):

            @pl.when(away == dz)
            def _(dz=dz):
                to[...] = projected[dz] if dz in dzs else done[before.index(dz)]


def rows_kernel(s, keep, received, gain, router_t, sign, out):
    width = gain.shape[1]
    rows = keep[...] + received[...].astype(F32)
    square = jnp.sum(rows * rows, axis=1, keepdims=True)
    scaled = rows * gain[...]
    logits = mm(scaled, router_t[...], NT, precision=HIGHEST)
    gap = jnp.sum(logits * sign[...], axis=1, keepdims=True)
    out[:, :width] = scaled.astype(BF16)
    lane = lax.broadcasted_iota(I32, (rows.shape[0], 128), 1)
    stats = jnp.zeros((rows.shape[0], 128), F32)
    for at, value in ((0, square), (3, gap)):
        for k, piece in enumerate(pieces(value)):
            stats = jnp.where(lane == at + k, piece.astype(F32), stats)
    out[:, width:] = stats.astype(BF16)


def source_of(s, nz, ny, place):
    z = lax.rem(s[0] + nz - place[0], nz)
    return z * ny + lax.rem(s[1] + ny - place[1], ny)


def throttled(copies, n, depth):
    if n < 0:
        for c in copies[:depth]:
            c.start()
        return
    copies[n].wait()
    if n + depth < len(copies):
        copies[n + depth].start()


def up_kernel(nz, ny, places, ahead, first, last, features, s, *refs):
    count = len(places)
    blocks = refs[:count]
    refs = refs[count:]
    before = () if first else refs[:3]
    refs = refs[0 if first else 3 :]
    weights = refs[:2]
    refs = refs[2:]
    if last:
        outs, buffers, sem = refs[:2], refs[2:4], refs[4]
    elif ahead:
        outs, kept, buffers, sem = refs[:3], refs[3:5], refs[5:7], refs[7]
    else:
        outs, buffers, sem = refs[:3], refs[3:5], refs[5]
    width = blocks[0].shape[1] - 128

    copies = []
    if True:
        jobs = [(p, buffers, n) for n, p in enumerate(places)]
        jobs += [(p, kept, n) for n, p in enumerate(ahead)]
        for p, to, n in jobs:
            lanes = pl.ds(pl.multiple_of(source_of(s, nz, ny, p) * width, 128), width)
            for m in range(2):
                source = weights[m].at[0, :, lanes]
                copies.append(pltpu.make_async_copy(source, to[m].at[n], sem.at[len(copies)]))
        throttled(copies, -1, 4)
    gate, up, stats = (None, None, None) if first else (b[...] for b in before)
    for n in range(count):
        rows = blocks[n][:, :width]
        part = blocks[n][:, width:].astype(F32)
        stats = part if stats is None else stats + part
        if True:
            throttled(copies, 2 * n, 4)
        part = mm(rows, buffers[0][n], NT)
        gate = part if gate is None else gate + part
        if True:
            throttled(copies, 2 * n + 1, 4)
        part = mm(rows, buffers[1][n], NT)
        up = part if up is None else up + part
    if not last:
        outs[0][...] = gate
        outs[1][...] = up
        outs[2][...] = stats
        for n in range(2 * count, len(copies)):
            throttled(copies, n, 4)
        return
    square = stats[:, 0:1] + stats[:, 1:2] + stats[:, 2:3]
    gap = stats[:, 3:4] + stats[:, 4:5] + stats[:, 5:6]
    inverse = lax.rsqrt(square / features + EPS)
    gate = gate * inverse
    outs[0][...] = (gate * sigmoid(gate) * (up * inverse)).astype(BF16)
    outs[1][...] = jnp.broadcast_to(sigmoid(gap * inverse), outs[1].shape)


def down_kernel(nz, ny, cap, places, ahead, first, last, s, *refs):
    j = s[2]
    count = len(places)
    blocks = refs[:count]
    refs = refs[count:]
    before = None if first else refs[0]
    refs = refs[0 if first else 1 :]
    w_down = refs[0]
    refs = refs[1:]
    depth = blocks[0].shape[1]
    copies = []
    if last:
        weight, out_base, row_base = refs[:3]
        outs, buf = refs[3:], w_down
    else:
        outs = refs[:1]
        kept = refs[1] if ahead else None
        buf, sem = refs[-2:]
        jobs = [(p, buf, n) for n, p in enumerate(places)]
        jobs += [(p, kept, n) for n, p in enumerate(ahead)]
        for p, to, n in jobs:
            at = pl.ds(pl.multiple_of(source_of(s, nz, ny, p) * depth, depth), depth)
            source = w_down.at[0, at, :]
            copies.append(pltpu.make_async_copy(source, to.at[n], sem.at[len(copies)]))
        throttled(copies, -1, 3)
    total = None if first else before[...]
    for n in range(count):
        if not last:
            throttled(copies, n, 3)
        part = mm(blocks[n][...], buf[n])
        total = part if total is None else total + part
    if not last:
        outs[0][...] = total
        for n in range(count, len(copies)):
            throttled(copies, n, 3)
        return
    result = (total * weight[:, 0:1]).astype(BF16)
    for r, out in enumerate(outs):
        wanted = out_base[...] + lax.bitwise_xor(j, r) * cap
        out[...] = mm(one_hot(wanted == row_base[...]), result).astype(BF16)


def combine_kernel(nz, cap, s, *refs):
    j = s[2]
    returned = refs[:nz]
    keep, received, residual, codes, ret_r, ret_base, out, stacked, own, sem = refs[nz:]
    copies = run_copies([(residual, own)], sem)
    rows = returned[0].shape[0]
    for n in range(nz):
        stacked[n * rows : (n + 1) * rows, :] = returned[n][...]
    ids = lax.bitwise_xor(ret_r[...], j) * (nz * cap) + ret_base[...] + j * cap
    pick = (ids == codes[j, 0:1, :]) | (ids == codes[j, 1:2, :])
    added = mm(one_hot(pick), stacked[...], TN)
    copies[0].wait()
    total = own[...].astype(F32) + (keep[...].astype(F32) + received[...].astype(F32))
    out[...] = (total + added).astype(BF16)


def local(
    residual,
    query,
    key_in,
    value_in,
    gate_in,
    log_decay,
    state_in,
    attn_gain,
    w_out,
    moe_gain,
    router,
    w_gate,
    w_up,
    w_down,
    expert_ids,
    keep_counts,
):
    nz = lax.axis_size("exp")
    ny = lax.axis_size("seq") // nz
    bits = nz.bit_length() - 1
    i = lax.axis_index("seq").astype(I32)
    j = lax.axis_index("exp").astype(I32)
    z, y = i // ny, i % ny
    place = jnp.stack([z, y, j])

    tok, head_width = query.shape
    head_count, hd = state_in.shape[0], state_in.shape[2]
    heads = head_count // ny
    width = heads * hd
    block, cols = residual.shape
    features = w_gate.shape[2]
    units = w_gate.shape[1]
    experts = router.shape[1]
    cap = 5 * block * nz // (2 * nz * experts)
    slots = nz * cap

    def z_turn(a, d):
        pairs = [(p * ny + q, (p + d) % nz * ny + q) for p in range(nz) for q in range(ny)]
        return lax.ppermute(a, "seq", pairs)

    def y_turn(a, d):
        pairs = [(p * ny + q, p * ny + (q + d) % ny) for p in range(nz) for q in range(ny)]
        return lax.ppermute(a, "seq", pairs)

    def swap(a, r):
        return lax.ppermute(a, "exp", [(p, p ^ r) for p in range(nz)])

    z_order = sorted(range(1, nz), key=lambda d: (min(d, nz - d), d))
    near = [d for d in z_order if min(d, nz - d) == 1]
    distant = [d for d in z_order if d not in near]
    places = [(dz, dy) for dy in range(ny) for dz in range(nz)]

    def behind(values, events):
        return list(lax.optimization_barrier((tuple(values), tuple(events)))[0])

    def gather_z(a):
        held = {(0, 0): a}
        for d in range(1, ny):
            held[0, d] = y_turn(a, d)
        for d in z_order:
            held[d, 0] = z_turn(a, d)
        return held

    def gather_y(held, events):
        for d in z_order:
            x = held[d, 0]
            if d == z_order[-1]:
                x = held[d, 0] = behind([x], events)[0]
            for e in range(1, ny):
                held[d, e] = y_turn(x, e)

    def stages(run, a):
        arrived = gather_z(a)
        state = run(0, groups[0], arrived, [])
        gather_y(arrived, state)
        for n in (1, 2):
            state = run(n, groups[n], arrived, state)
        return state

    groups = [[(0, 0)], [(0, d) for d in range(1, ny)] + [(d, 0) for d in z_order]]
    groups.append([(d, e) for d in z_order for e in range(1, ny)])

    slot = np.arange(cap)
    row_r = np.repeat([bit_reversed(p, bits) for p in range(nz)], slots).astype(np.int32)[:, None]
    row_base = np.tile((np.arange(nz)[:, None] * cap + slot).reshape(slots), nz)
    row_base = row_base.astype(np.int32)[:, None]
    own_base = row_base[:slots]
    ret_rows = cap + -cap % 16
    padded = np.where(np.arange(ret_rows) < cap, np.arange(ret_rows), -(10**8)).astype(np.int32)
    ret_r = np.repeat(np.arange(nz), ret_rows).astype(np.int32)[:, None]
    ret_base = np.tile(padded, nz)[:, None]

    logs_t = jnp.transpose(log_decay)
    logs, kvs, qgs = [logs_t], [], []
    for d in range(1, ny):
        pack = pl.pallas_call(
            functools.partial(pack_kernel, d, ny),
            out_shape=sds((2, tok, width), BF16),
            in_specs=[pl.BlockSpec(memory_space=pltpu.HBM)] * 2,
            out_specs=pl.BlockSpec(memory_space=pltpu.VMEM),
            scratch_shapes=[pltpu.SemaphoreType.DMA((2,))],
            compiler_params=pltpu.CompilerParams(vmem_limit_bytes=60 * 1024 * 1024),
        )
        kvs.append(y_turn(pack(key_in, value_in), d))
        logs.append(y_turn(logs_t, d))
        qgs.append(pack(query, gate_in))
    ids = jnp.transpose(expert_ids)
    share = hd // nz
    codes, sign, start = call(
        functools.partial(routing_kernel, nz, cap, slots),
        place,
        [(keep_counts, pl.BlockSpec(memory_space=pltpu.SMEM))]
        + [ids]
        + [swap(ids, r) for r in range(1, nz)]
        + [own_base, hbm(state_in)],
        [sds((nz, 2, block), I32), sds((slots, experts), F32), sds((heads, share, hd), F32)],
        [pltpu.VMEM((nz, 2, block), I32), pltpu.SemaphoreType.DMA],
    )
    attn_gain_2, moe_gain_2, router_t = attn_gain[None], moe_gain[None], jnp.transpose(router)
    prepared = [codes, sign, start, attn_gain_2, moe_gain_2]
    qgs = [y_turn(qg, d + 1) for d, qg in enumerate(behind(qgs, kvs + logs + prepared))]
    share = hd // nz
    long = tok * ny
    *parts, c_row, c_col = call(
        functools.partial(update_kernel, nz, ny, heads, hd),
        place,
        [hbm(key_in), hbm(value_in), *kvs, *logs],
        [sds((heads * share + 16, hd), BF16)] * nz
        + [sds((heads, long), F32), sds((long, heads), F32)],
        [
            pltpu.VMEM((heads, long), F32),
            pltpu.VMEM((heads, hd, hd), BF16),
            pltpu.VMEM((16, hd), F32),
            pltpu.VMEM((2, tok, width), BF16),
            pltpu.SemaphoreType.DMA((2,)),
        ],
        limit=40,
            flops=2 * long * hd * hd * heads,
    )
    parts = [parts[0]] + [z_turn(parts[d], d) for d in range(1, nz)]
    *entering, last_rows = call(
        functools.partial(prefix_kernel, nz, heads, hd),
        place,
        [*parts, start],
        [sds((heads * share, hd), BF16)] * nz + [sds((heads, share, hd), F32)],
        [
            pltpu.VMEM((nz, heads * share + 16, hd), BF16),
            pltpu.VMEM((nz, heads * share, hd), BF16),
            pltpu.VMEM((heads, share, hd), F32),
        ],
    )
    entering = [entering[0]] + [z_turn(entering[d], d) for d in range(1, nz)]
    (mixed,) = call(
        functools.partial(attention_kernel, nz, ny, heads, hd),
        place,
        [
            hbm(key_in),
            hbm(value_in),
            hbm(query),
            hbm(gate_in),
            *[anywhere(x) for x in kvs],
            *[anywhere(x) for x in qgs],
            *entering,
            c_row,
            c_col,
            (attn_gain_2, pl.BlockSpec((1, width), lambda n, s: (0, s[1]))),
        ],
        [sds((long, width), BF16)],
        [pltpu.VMEM((long, width), BF16)] * 4
        + [pltpu.VMEM((heads, hd, hd), BF16), pltpu.SemaphoreType.DMA((4 * ny,))],
        limit=40,
            flops=4 * long * long * width,
    )

    def across(blocks):
        return [[y_turn(x, e) for x in blocks] for e in range(1, ny)]

    held = {0: [[mixed]] + across([mixed])}
    for d in near:
        held[d] = [[z_turn(mixed, d)]]
    free = behind([mixed], [held[near[0]][0][0]])[0]
    for d in near:
        held[d] += across(held[d][0])
    halves = [free[: long // 2], free[long // 2 :]]
    for d in distant:
        held[d] = [[z_turn(x, d) for x in halves]]
    for d in distant:
        held[d] += across(held[d][0])
    w_parts = [
        (w_out, pl.BlockSpec((width, cols), lambda n, s, d=d: (lax.rem(s[1] + ny - d, ny), 0)))
        for d in range(ny)
    ]
    given = []
    for group in ([0] + near, distant):
        last = group is distant
        dzs = {d: held[d][0] for d in group}
        blocks = [x for dy in range(ny) for d in group for x in held[d][dy]]
        half = nz * slots // 2
        outs = [sds((len(group), block, cols), BF16), sds((nz * slots, cols), F32)]
        if last:
            outs = [sds((half, cols), F32), sds((half, cols), BF16)]
            outs += [sds((nz // 2, block, cols), BF16)] * 2
        given = call(
            functools.partial(project_kernel, nz, ny, cap, dzs, last),
            place,
            [anywhere(x) for x in blocks]
            + w_parts
            + [row_r, row_base, codes]
            + list(given)
            + ([hbm(residual)] if last else []),
            outs,
            [pltpu.VMEM((ny, len(group), long, width), BF16)]
            + ([pltpu.VMEM((block, cols), BF16)] if last else [])
            + [pltpu.SemaphoreType.DMA((len(blocks) + 1,))],
            limit=40,
            flops=2 * len(group) * long * head_width * cols,
        )
    keep, send, keep_all, send_all = given
    for b in range(bits):
        received = swap(send, 1 << b)
        if b < bits - 1:
            part = keep.shape[0] // 2
            send = (keep[part:] + received[part:].astype(F32)).astype(BF16)
            keep = keep[:part] + received[:part].astype(F32)
    (rows_out,) = call(
        rows_kernel,
        place,
        [keep, received, moe_gain_2, router_t, sign],
        [sds((slots, cols + 128), BF16)],
    )
    send_all = behind([send_all], [rows_out])[0]
    for b in range(bits):
        received_all = swap(send_all, 1 << b)
        if b < bits - 1:
            n = keep_all.shape[0] // 2
            both = keep_all.astype(F32) + received_all.astype(F32)
            send_all, keep_all = both[n:].astype(BF16), both[:n].astype(BF16)
    rows = share // ny
    last_rows = behind([last_rows], [rows_out])[0]
    final_rows = jnp.zeros((head_count, rows, hd), F32)
    for d in range(ny):
        sent = lax.dynamic_slice_in_dim(last_rows, (y + d) % ny * rows, rows, 1)
        got = sent if d == 0 else y_turn(sent, d)
        final_rows = lax.dynamic_update_slice_in_dim(
            final_rows, got, (y - d) % ny * heads, 0
        )

    in_vmem = pl.BlockSpec(memory_space=pltpu.VMEM)

    def up(n, group, arrived, state):
        first, last = n == 0, n == len(groups) - 1
        ahead = []
        outs = [sds((slots, units), F32)] * 2 + [sds((slots, 128), F32)]
        outs += [sds((len(ahead), units, cols), BF16)] * (2 if ahead else 0)
        weights = [anywhere(w_gate), anywhere(w_up)]
        if last:
            outs = [sds((slots, units), BF16), sds((slots, 128), F32)]
        state = call(
            functools.partial(up_kernel, nz, ny, group, ahead, first, last, features),
            place,
            [arrived[p] for p in group] + list(state) + weights,
            outs,
            [pltpu.VMEM((len(group), units, cols), BF16)] * 2
            + [pltpu.SemaphoreType.DMA((2 * (len(group) + len(ahead)),))],
            limit=40,
            flops=4 * len(group) * slots * units * cols,
            held=2 if ahead else 0,
        )
        if ahead:
            fetched["up"] = state[3:]
        return state[:3]

    def down(n, group, arrived, state):
        first, last = n == 0, n == len(groups) - 1
        ahead = groups[-1] if first else []
        outs = [sds((slots, cols), F32)]
        outs += [sds((len(ahead), units, cols), BF16)] if ahead else []
        weights = [anywhere(w_down)]
        if last:
            outs = [sds((ret_rows, cols), BF16)] * nz
            weights = [(fetched["down"], in_vmem), weight, padded[:, None], own_base.T]
        state = call(
            functools.partial(down_kernel, nz, ny, cap, group, ahead, first, last),
            place,
            [arrived[p] for p in group] + list(state) + weights,
            outs,
            []
            if last
            else [
                pltpu.VMEM((len(group), units, cols), BF16),
                pltpu.SemaphoreType.DMA((len(group) + len(ahead),)),
            ],
            limit=40,
            flops=2 * len(group) * slots * units * cols,
            held=1 if ahead else 0,
        )
        if ahead:
            fetched["down"] = state[1]
        return state if last else state[:1]

    fetched = {}
    if cols % 128:
        arrived = gather_z(rows_out)
        gather_y(arrived, [])
        order = jnp.stack([(z - dz) % nz * ny + (y - dy) % ny for dz, dy in places])
        at = jnp.argsort(order)
        rows_all = jnp.take(jnp.stack([arrived[p] for p in places]), at, axis=0)
        stats = jnp.sum(rows_all[:, :, cols:].astype(F32), axis=0)
        rows_all = jnp.swapaxes(rows_all[:, :, :cols], 0, 1).reshape(slots, features)
        inverse = lax.rsqrt(jnp.sum(stats[:, :3], axis=1) / features + EPS)[:, None]
        gate = mm(rows_all, w_gate[0], NT) * inverse
        hidden = (gate * sigmoid(gate) * (mm(rows_all, w_up[0], NT) * inverse)).astype(BF16)
        weight = sigmoid(jnp.sum(stats[:, 3:6], axis=1)[:, None] * inverse)
        weight = jnp.broadcast_to(weight, (slots, 128))
    else:
        hidden, weight = stages(up, rows_out)
    state = stages(down, hidden)
    returned = [state[0]] + [swap(state[r], r) for r in range(1, nz)]
    (layer_out,) = call(
        functools.partial(combine_kernel, nz, cap),
        place,
        returned + [keep_all[0], received_all[0], hbm(residual), codes, ret_r, ret_base],
        [sds((block, cols), BF16)],
        [
            pltpu.VMEM((nz * ret_rows, cols), BF16),
            pltpu.VMEM((block, cols), BF16),
            pltpu.SemaphoreType.DMA((1,)),
        ],
    )
    return layer_out, final_rows


def solution(mesh):
    in_specs = (
        P("exp", "seq"),
        P("seq", "exp"),
        P("seq", "exp"),
        P("seq", "exp"),
        P("seq", "exp"),
        P("seq", "exp"),
        P("exp", None, None),
        P("exp"),
        P("exp", "seq"),
        P("seq"),
        P("seq", None),
        P("exp", "seq", None),
        P("exp", "seq", None),
        P("exp", None, "seq"),
        P("exp", None),
        P(),
    )
    out_specs = (P("exp", "seq"), P("exp", "seq", None))
    return jax.shard_map(local, mesh=mesh, in_specs=in_specs, out_specs=out_specs, check_vma=False)
```

```python
import functools
import jax
import jax.numpy as jnp
import numpy as np
from jax import lax
from jax.experimental import pallas as pl
from jax.experimental.pallas import tpu as pltpu
from jax.sharding import PartitionSpec as P

EPS = 1e-05
F32 = jnp.float32
BF16 = jnp.bfloat16
I32 = jnp.int32
HIGHEST = lax.Precision.HIGHEST
NT = (((1,), (1,)), ((), ()))
TN = (((0,), (0,)), ((), ()))
NN = (((1,), (0,)), ((), ()))


def mm(a, b, dims=NN, precision=None):
    return lax.dot_general(a, b, dims, precision=precision, preferred_element_type=F32)


def sigmoid(v):
    return 1.0 / (1.0 + jnp.exp(-v))


def bit_reversed(p, bits):
    r = 0
    for b in range(bits):
        r = r * 2 + ((p >> b) & 1)
    return r


def whole(shape):
    return pl.BlockSpec(tuple(shape), lambda i, s: (0,) * len(shape))


def call(kernel, place, operands, outs, scratch=(), flops=0, limit=40, held=0):
    arrays, specs, moved = [], [], 0
    for item in operands:
        array, spec = item if isinstance(item, tuple) else (item, whole(item.shape))
        arrays.append(array)
        specs.append(spec)
        moved += array.size * array.dtype.itemsize
    moved += sum(o.size * o.dtype.itemsize for o in outs)
    return pl.pallas_call(
        kernel,
        out_shape=list(outs),
        grid_spec=pltpu.PrefetchScalarGridSpec(
            num_scalar_prefetch=1,
            grid=(1,),
            in_specs=specs,
            out_specs=[
                pl.BlockSpec(memory_space=pltpu.VMEM) if n >= len(outs) - held else whole(o.shape)
                for n, o in enumerate(outs)
            ],
            scratch_shapes=list(scratch),
        ),
        compiler_params=pltpu.CompilerParams(vmem_limit_bytes=limit * 1024 * 1024),
        cost_estimate=pl.CostEstimate(flops=flops, bytes_accessed=moved, transcendentals=0),
    )(place, *arrays)


def hbm(array):
    return (array, pl.BlockSpec(memory_space=pltpu.HBM))


def anywhere(array):
    return (array, pl.BlockSpec(memory_space=pl.ANY))


def run_copies(pairs, sem):
    copies = [pltpu.make_async_copy(a, b, sem.at[n]) for n, (a, b) in enumerate(pairs)]
    for c in copies:
        c.start()
    return copies


def one_hot(mask):
    return mask.astype(F32).astype(BF16)


def turned_back(z, back, nz):
    return jnp.where(z < back, z - back + nz, z - back)


def sds(shape, dtype):
    return jax.ShapeDtypeStruct(tuple(shape), dtype)


def pieces(x):
    hi = x.astype(BF16)
    rest = x - hi.astype(F32)
    mid = rest.astype(BF16)
    return hi, mid, (rest - mid.astype(F32)).astype(BF16)


def routing_kernel(nz, cap, own_rows, s, *refs):
    keep = refs[0]
    given = refs[1 : nz + 1]
    base, state, codes, sign, spare, start, ids, sem = refs[nz + 1 :]
    j = s[2]
    heads, share, _ = start.shape
    rows = pl.ds(pl.multiple_of(s[0] * share, share), share)
    fetch = pltpu.make_async_copy(state.at[pl.ds(s[1] * heads, heads), rows, :], start, sem)
    fetch.start()
    block = given[0].shape[1]
    for r in range(nz):
        ids[lax.bitwise_xor(j, r)] = given[r][...]
    rows = lax.broadcasted_iota(I32, (block, block), 0)
    cols = lax.broadcasted_iota(I32, (block, block), 1)
    strict = one_hot(rows < cols)
    own = base[...] + j * (nz * cap)
    earlier = [jnp.zeros((1, 1), I32) for _ in range(nz)]
    other = jnp.zeros((own_rows, 1), I32)
    taken = jnp.zeros((own_rows, 1), I32)
    place = lax.broadcasted_iota(I32, (16, block), 0)
    for b in range(nz):
        first, second = ids[b, 0:1, :], ids[b, 1:2, :]
        named = ((place == first) | (place == second)) & (place < nz)
        ranks = mm(one_hot(named), strict).astype(I32)
        slots = []
        for e in range(nz):
            hit = (first == e) | (second == e)
            rank = ranks[e : e + 1, :]
            kept = hit & (rank + earlier[e] < keep[e])
            slots.append(jnp.where(kept, (e * nz + b) * cap + rank, -1))
            earlier[e] = earlier[e] + jnp.sum(hit.astype(I32), axis=1, keepdims=True)
        top = functools.reduce(jnp.maximum, slots)
        rest = functools.reduce(jnp.maximum, [jnp.where(c == top, -1, c) for c in slots])
        codes[b, 0:1, :] = top
        codes[b, 1:2, :] = rest
        holds = (own == top) | (own == rest)
        taken = taken + jnp.sum(holds.astype(I32), axis=1, keepdims=True)
        other = other + jnp.sum(jnp.where(holds, first + second, 0), axis=1, keepdims=True)
    every = lax.broadcasted_iota(I32, sign.shape, 1)
    sign[...] = (every == j).astype(F32) - (every == other - j).astype(F32)
    index = lax.broadcasted_iota(I32, (own_rows, 1), 0)
    unused = jnp.min(jnp.where(taken == 0, index, own_rows), axis=0, keepdims=True)
    spare[...] = jnp.broadcast_to((index == unused).astype(F32), spare.shape)
    fetch.wait()


def pack_kernel(away, ny, a, b, out, sem):
    width = out.shape[2]
    share = lax.rem(lax.rem(lax.axis_index("seq"), ny) + away, ny)
    at = pl.ds(pl.multiple_of(share * width, 128), width)
    for c in run_copies([(a.at[:, at], out.at[0]), (b.at[:, at], out.at[1])], sem):
        c.wait()


def update_kernel(nz, ny, heads, hd, s, *refs):
    z, y = s[0], s[1]
    n = ny - 1
    k_arg, v_arg = refs[0], refs[1]
    kv = refs[2 : 2 + n]
    logs = refs[2 + n : 2 + n + ny]
    outs = refs[2 + n + ny : 2 + n + ny + nz]
    c_row, c_col, log_all, state, tail, own, sem = refs[2 + n + ny + nz :]
    tok = k_arg.shape[0]
    total_tok = tok * ny
    share = hd // nz
    mine = pl.ds(pl.multiple_of(y * heads * hd, 128), heads * hd)
    copies = run_copies([(x.at[:, mine], own.at[m]) for m, x in enumerate((k_arg, v_arg))], sem)
    for d in range(ny):
        at = pl.multiple_of(lax.rem(y + ny - d, ny) * tok, tok)
        log_all[:, pl.ds(at, tok)] = logs[d][pl.ds(y * heads, heads), :]
    rows = lax.broadcasted_iota(I32, (total_tok, total_tok), 0)
    cols = lax.broadcasted_iota(I32, (total_tok, total_tok), 1)
    c_row[...] = mm(log_all[...], (rows <= cols).astype(F32), precision=HIGHEST)
    c_col[...] = mm((rows >= cols).astype(F32), log_all[...], NT, precision=HIGHEST)
    total = c_row[:, total_tok - 1 : total_tok]
    for c in copies:
        c.wait()
    for h in range(heads):
        add = None
        for d in range(ny):
            at = pl.multiple_of(lax.rem(y + ny - d, ny) * tok, tok)
            lanes = slice(h * hd, (h + 1) * hd)
            pair = own if d == 0 else kv[d - 1]
            key = pair[0, :, lanes].astype(F32)
            decay = jnp.exp(total[h : h + 1, :] - c_col[pl.ds(at, tok), h : h + 1])
            weighted = (key * sigmoid(key) * decay).astype(BF16)
            part = mm(weighted, pair[1, :, lanes], TN)
            add = part if add is None else add + part
        state[h] = add.astype(BF16)
    tail[...] = jnp.zeros_like(tail)
    hi, mid, lo = pieces(total)
    lane = lax.broadcasted_iota(I32, (heads, hd), 1)
    tail[0:heads, :] = jnp.where(
        lane == 0,
        hi.astype(F32),
        jnp.where(lane == 1, mid.astype(F32), jnp.where(lane == 2, lo.astype(F32), 0.0)),
    )
    for d in range(nz):
        at = pl.multiple_of(lax.rem(z + d, nz) * share, share)
        for h in range(heads):
            outs[d][h * share : (h + 1) * share, :] = state[h, pl.ds(at, share), :]
        outs[d][heads * share :, :] = tail[...].astype(BF16)


def prefix_kernel(nz, heads, hd, s, *refs):
    z = s[0]
    parts = refs[:nz]
    start = refs[nz]
    outs = refs[nz + 1 : 2 * nz + 1]
    final, held, entering, run = refs[2 * nz + 1 :]
    share = hd // nz
    run[...] = start[...]
    for d in range(nz):
        held[lax.rem(z + nz - d, nz)] = parts[d][...]
    for p in range(nz):
        logs = jnp.sum(held[p, heads * share :, :].astype(F32), axis=1, keepdims=True)
        keep = jnp.exp(logs)
        for h in range(heads):
            rows = slice(h * share, (h + 1) * share)
            now = run[h]
            entering[p, rows, :] = now.astype(BF16)
            run[h] = keep[h : h + 1, :] * now + held[p, rows, :].astype(F32)
    final[...] = run[...]
    for d in range(nz):
        outs[d][...] = entering[lax.rem(z + d, nz)]


def attention_kernel(nz, ny, heads, hd, s, *refs):
    z, y = s[0], s[1]
    n = ny - 1
    args = refs[:4]
    kv = refs[4 : 4 + n]
    qg = refs[4 + n : 4 + 2 * n]
    states = refs[4 + 2 * n : 4 + 2 * n + nz]
    c_row, c_col, gain, out, ks, vs, qs, gs, state, sem = refs[4 + 2 * n + nz :]
    tok = args[0].shape[0]
    total_tok = tok * ny
    share = hd // nz
    mine = pl.ds(pl.multiple_of(y * heads * hd, 128), heads * hd)
    moves = []
    for d in range(ny):
        at = pl.ds(pl.multiple_of(lax.rem(y + ny - d, ny) * tok, tok), tok)
        for m, to in enumerate((ks, vs, qs, gs)):
            if d == 0:
                source = args[m].at[:, mine]
            else:
                source = (kv if m < 2 else qg)[d - 1].at[m % 2]
            moves.append((source, to.at[at, :]))
    copies = run_copies(moves, sem)
    for d in range(nz):
        at = pl.ds(pl.multiple_of(lax.rem(z + nz - d, nz) * share, share), share)
        for h in range(heads):
            state[h, at, :] = states[d][h * share : (h + 1) * share, :]
    rows = lax.broadcasted_iota(I32, (total_tok, total_tok), 0)
    cols = lax.broadcasted_iota(I32, (total_tok, total_tok), 1)
    causal = rows >= cols
    for c in copies:
        c.wait()
    for h in range(heads):
        lanes = slice(h * hd, (h + 1) * hd)
        query = qs[:, lanes].astype(F32)
        query = query * sigmoid(query)
        key = ks[:, lanes].astype(F32)
        key = (key * sigmoid(key)).astype(BF16)
        col = c_col[:, h : h + 1]
        gap = jnp.where(causal, col - c_row[h : h + 1, :], 0.0)
        decay = jnp.where(causal, jnp.exp(gap), 0.0)
        scores = mm(query.astype(BF16), key, NT) * decay
        att = mm(scores.astype(BF16), vs[:, lanes])
        att = att + mm((query * jnp.exp(col)).astype(BF16), state[h])
        square = jnp.mean(att * att, axis=1, keepdims=True)
        gate = sigmoid(gs[:, lanes].astype(F32))
        out[:, lanes] = (att * lax.rsqrt(square + EPS) * gain[:, lanes] * gate).astype(BF16)


def project_kernel(nz, ny, cap, dzs, last, s, *refs):
    z, j = s[0], s[2]
    bits = nz.bit_length() - 1
    parts = [len(p) for p in dzs.values()]
    count = sum(parts) * ny
    blocks = refs[:count]
    weights = refs[count : count + ny]
    r_ids, b_ids, codes = refs[count + ny : count + ny + 3]
    refs = refs[count + ny + 3 :]
    if last:
        done, sums, residual = refs[:3]
        keep, send, keep_all, send_all, stacked, own, sem = refs[3:]
    else:
        done, sums, stacked, sem = refs
    rows = stacked.shape[2]
    moves = []
    at = 0
    for dy in range(ny):
        for n, (dz, pieces_of) in enumerate(dzs.items()):
            first = 0
            for _ in pieces_of:
                size = blocks[at].shape[0]
                moves.append((blocks[at], stacked.at[dy, n, pl.ds(first, size)]))
                first += size
                at += 1
    if last:
        moves.append((residual, own))
    copies = run_copies(moves, sem)
    ids = lax.bitwise_xor(r_ids[...], j) * (nz * cap) + b_ids[...]
    pick = lambda b: one_hot((ids == codes[b, 0:1, :]) | (ids == codes[b, 1:2, :]))
    total_rows = sums[...] if last else None
    for c in copies:
        c.wait()
    projected = {}
    for n, dz in enumerate(dzs):
        total = None
        for dy in range(ny):
            part = mm(stacked[dy, n], weights[dy][...])
            total = part if total is None else total + part
        projected[dz] = total.astype(BF16)
        part = mm(pick(lax.rem(z + nz - dz, nz)), projected[dz])
        total_rows = part if total_rows is None else total_rows + part
    if not last:
        for n, dz in enumerate(dzs):
            done[n] = projected[dz]
        sums[...] = total_rows
        return
    total_rows = total_rows + mm(pick(j), own[...])
    half = keep.shape[0]
    keep[...] = total_rows[:half, :]
    send[...] = total_rows[half:, :].astype(BF16)
    before = [dz for dz in range(nz) if dz not in dzs]
    for p in range(nz):
        block = lax.bitwise_xor(jnp.int32(bit_reversed(p, bits)), j)
        away = lax.rem(z + nz - block, nz)
        to = keep_all.at[p] if p < nz // 2 else send_all.at[p - nz // 2]
        for dz in range(nz):

            @pl.when(away == dz)
            def _(dz=dz):
                to[...] = projected[dz] if dz in dzs else done[before.index(dz)]


def diagonal(rows):
    shape = (rows, 128)
    return lax.broadcasted_iota(I32, shape, 0) == lax.broadcasted_iota(I32, shape, 1)


def rows_kernel(s, keep, received, gain, router_t, sign, spare, out):
    width = gain.shape[1]
    rows = keep[...] + received[...].astype(F32)
    square = jnp.sum(rows * rows, axis=1, keepdims=True)
    scaled = rows * gain[...]
    logits = mm(scaled, router_t[...], NT, precision=HIGHEST)
    gap = jnp.sum(logits * sign[...], axis=1, keepdims=True)
    if out.shape[1] == width:
        lines = []
        for value in (square, gap):
            for piece in pieces(value)[:2]:
                spread = jnp.where(diagonal(rows.shape[0]), piece.astype(F32), 0.0)
                lines.append(jnp.sum(spread, axis=0, keepdims=True))
        lines.append(jnp.zeros((1, width - 128 * len(lines)), F32))
        line = jnp.concatenate(lines, axis=1)
        out[...] = jnp.where(spare[:, 0:1] > 0.0, line, scaled).astype(BF16)
        return
    out[:, :width] = scaled.astype(BF16)
    lane = lax.broadcasted_iota(I32, (rows.shape[0], 128), 1)
    stats = jnp.zeros((rows.shape[0], 128), F32)
    for at, value in ((0, square), (3, gap)):
        for k, piece in enumerate(pieces(value)):
            stats = jnp.where(lane == at + k, piece.astype(F32), stats)
    out[:, width:] = stats.astype(BF16)


def source_of(s, nz, ny, place):
    z = lax.rem(s[0] + nz - place[0], nz)
    return z * ny + lax.rem(s[1] + ny - place[1], ny)


def throttled(copies, n, depth):
    if n < 0:
        for c in copies[:depth]:
            c.start()
        return
    copies[n].wait()
    if n + depth < len(copies):
        copies[n + depth].start()


def up_kernel(nz, ny, places, first, last, features, s, *refs):
    count = len(places)
    blocks = refs[:count]
    refs = refs[count:]
    before = () if first else refs[:3]
    refs = refs[0 if first else 3 :]
    weights, spare = refs[:2], refs[2]
    outs, buffers, sem = refs[3:-3], refs[-3:-1], refs[-1]
    slots, width = blocks[0].shape
    is_spare = spare[:, 0:1] > 0.0
    copies = []
    for n, p in enumerate(places):
        lanes = pl.ds(pl.multiple_of(source_of(s, nz, ny, p) * width, 128), width)
        for m in range(2):
            source = weights[m].at[0, :, lanes]
            copies.append(pltpu.make_async_copy(source, buffers[m].at[n], sem.at[len(copies)]))
    throttled(copies, -1, 4)
    gate, up, stats = (None, None, None) if first else (b[...] for b in before)
    for n in range(count):
        rows = blocks[n][...].astype(F32)
        part = jnp.sum(jnp.where(is_spare, rows, 0.0), axis=0, keepdims=True)
        stats = part if stats is None else stats + part
        rows = jnp.where(is_spare, 0.0, rows).astype(BF16)
        throttled(copies, 2 * n, 4)
        part = mm(rows, buffers[0][n], NT)
        gate = part if gate is None else gate + part
        throttled(copies, 2 * n + 1, 4)
        part = mm(rows, buffers[1][n], NT)
        up = part if up is None else up + part
    if not last:
        outs[0][...] = gate
        outs[1][...] = up
        outs[2][...] = stats
        return
    sums = [stats[:, at : at + 128] + stats[:, at + 128 : at + 256] for at in (0, 256)]
    sums = [jnp.where(diagonal(slots), line, 0.0) for line in sums]
    square, gap = [jnp.sum(line, axis=1, keepdims=True) for line in sums]
    inverse = lax.rsqrt(square / features + EPS)
    gate = gate * inverse
    outs[0][...] = (gate * sigmoid(gate) * (up * inverse)).astype(BF16)
    outs[1][...] = jnp.broadcast_to(sigmoid(gap * inverse), outs[1].shape)


def down_kernel(nz, ny, cap, places, ahead, first, last, s, *refs):
    j = s[2]
    count = len(places)
    blocks = refs[:count]
    refs = refs[count:]
    before = None if first else refs[0]
    refs = refs[0 if first else 1 :]
    w_down = refs[0]
    refs = refs[1:]
    depth = blocks[0].shape[1]
    copies = []
    if last:
        weight, out_base, row_base = refs[:3]
        outs, buf = refs[3:], w_down
    else:
        outs = refs[:1]
        kept = refs[1] if ahead else None
        buf, sem = refs[-2:]
        jobs = [(p, buf, n) for n, p in enumerate(places)]
        jobs += [(p, kept, n) for n, p in enumerate(ahead)]
        for p, to, n in jobs:
            at = pl.ds(pl.multiple_of(source_of(s, nz, ny, p) * depth, depth), depth)
            source = w_down.at[0, at, :]
            copies.append(pltpu.make_async_copy(source, to.at[n], sem.at[len(copies)]))
        throttled(copies, -1, 3)
    total = None if first else before[...]
    for n in range(count):
        if not last:
            throttled(copies, n, 3)
        part = mm(blocks[n][...], buf[n])
        total = part if total is None else total + part
    if not last:
        outs[0][...] = total
        for n in range(count, len(copies)):
            throttled(copies, n, 3)
        return
    result = (total * weight[:, 0:1]).astype(BF16)
    for r, out in enumerate(outs):
        wanted = out_base[...] + lax.bitwise_xor(j, r) * cap
        out[...] = mm(one_hot(wanted == row_base[...]), result).astype(BF16)


def combine_kernel(nz, cap, s, *refs):
    j = s[2]
    returned = refs[:nz]
    keep, received, residual, codes, ret_r, ret_base, out, stacked, own, sem = refs[nz:]
    copies = run_copies([(residual, own)], sem)
    rows = returned[0].shape[0]
    for n in range(nz):
        stacked[n * rows : (n + 1) * rows, :] = returned[n][...]
    ids = lax.bitwise_xor(ret_r[...], j) * (nz * cap) + ret_base[...] + j * cap
    pick = (ids == codes[j, 0:1, :]) | (ids == codes[j, 1:2, :])
    added = mm(one_hot(pick), stacked[...], TN)
    copies[0].wait()
    total = own[...].astype(F32) + (keep[...].astype(F32) + received[...].astype(F32))
    out[...] = (total + added).astype(BF16)


def local(
    residual,
    query,
    key_in,
    value_in,
    gate_in,
    log_decay,
    state_in,
    attn_gain,
    w_out,
    moe_gain,
    router,
    w_gate,
    w_up,
    w_down,
    expert_ids,
    keep_counts,
):
    nz = lax.axis_size("exp")
    ny = lax.axis_size("seq") // nz
    bits = nz.bit_length() - 1
    i = lax.axis_index("seq").astype(I32)
    j = lax.axis_index("exp").astype(I32)
    z, y = i // ny, i % ny
    place = jnp.stack([z, y, j])

    tok, head_width = query.shape
    head_count, hd = state_in.shape[0], state_in.shape[2]
    heads = head_count // ny
    width = heads * hd
    block, cols = residual.shape
    features = w_gate.shape[2]
    units = w_gate.shape[1]
    experts = router.shape[1]
    cap = 5 * block * nz // (2 * nz * experts)
    slots = nz * cap

    def z_turn(a, d):
        pairs = [(p * ny + q, (p + d) % nz * ny + q) for p in range(nz) for q in range(ny)]
        return lax.ppermute(a, "seq", pairs)

    def y_turn(a, d):
        pairs = [(p * ny + q, p * ny + (q + d) % ny) for p in range(nz) for q in range(ny)]
        return lax.ppermute(a, "seq", pairs)

    def swap(a, r):
        return lax.ppermute(a, "exp", [(p, p ^ r) for p in range(nz)])

    z_order = sorted(range(1, nz), key=lambda d: (min(d, nz - d), d))
    near = [d for d in z_order if min(d, nz - d) == 1]
    distant = [d for d in z_order if d not in near]
    places = [(dz, dy) for dy in range(ny) for dz in range(nz)]

    def behind(values, events):
        return list(lax.optimization_barrier((tuple(values), tuple(events)))[0])

    def gather_z(a):
        held = {(0, 0): a}
        for d in range(1, ny):
            held[0, d] = y_turn(a, d)
        for d in z_order:
            held[d, 0] = z_turn(a, d)
        return held

    def gather_y(held, events):
        for d in z_order:
            x = held[d, 0]
            if d == z_order[-1]:
                x = held[d, 0] = behind([x], events)[0]
            for e in range(1, ny):
                held[d, e] = y_turn(x, e)

    def stages(run, a):
        arrived = gather_z(a)
        state = []
        for n, group in enumerate(groups):
            state = run(n, group, [arrived[p] for p in group], state)
            if n == 0:
                gather_y(arrived, state)
        return state

    groups = [[(0, 0)], [(0, d) for d in range(1, ny)] + [(d, 0) for d in z_order]]
    groups.append([(d, e) for d in z_order for e in range(1, ny)])

    slot = np.arange(cap)
    row_r = np.repeat([bit_reversed(p, bits) for p in range(nz)], slots).astype(np.int32)[:, None]
    row_base = np.tile((np.arange(nz)[:, None] * cap + slot).reshape(slots), nz)
    row_base = row_base.astype(np.int32)[:, None]
    own_base = row_base[:slots]
    ret_rows = cap + -cap % 16
    padded = np.where(np.arange(ret_rows) < cap, np.arange(ret_rows), -(10**8)).astype(np.int32)
    ret_r = np.repeat(np.arange(nz), ret_rows).astype(np.int32)[:, None]
    ret_base = np.tile(padded, nz)[:, None]

    logs_t = jnp.transpose(log_decay)
    logs, kvs, qgs = [logs_t], [], []
    for d in range(1, ny):
        pack = pl.pallas_call(
            functools.partial(pack_kernel, d, ny),
            out_shape=sds((2, tok, width), BF16),
            in_specs=[pl.BlockSpec(memory_space=pltpu.HBM)] * 2,
            out_specs=pl.BlockSpec(memory_space=pltpu.VMEM),
            scratch_shapes=[pltpu.SemaphoreType.DMA((2,))],
            compiler_params=pltpu.CompilerParams(vmem_limit_bytes=60 * 1024 * 1024),
        )
        kvs.append(y_turn(pack(key_in, value_in), d))
        logs.append(y_turn(logs_t, d))
        qgs.append(pack(query, gate_in))
    ids = jnp.transpose(expert_ids)
    share = hd // nz
    codes, sign, spare, start = call(
        functools.partial(routing_kernel, nz, cap, slots),
        place,
        [(keep_counts, pl.BlockSpec(memory_space=pltpu.SMEM))]
        + [ids]
        + [swap(ids, r) for r in range(1, nz)]
        + [own_base, hbm(state_in)],
        [
            sds((nz, 2, block), I32),
            sds((slots, experts), F32),
            sds((slots, 128), F32),
            sds((heads, share, hd), F32),
        ],
        [pltpu.VMEM((nz, 2, block), I32), pltpu.SemaphoreType.DMA],
    )
    attn_gain_2, moe_gain_2, router_t = attn_gain[None], moe_gain[None], jnp.transpose(router)
    prepared = [codes, sign, spare, start, attn_gain_2, moe_gain_2]
    qgs = [y_turn(qg, d + 1) for d, qg in enumerate(behind(qgs, kvs + logs + prepared))]
    share = hd // nz
    long = tok * ny
    *parts, c_row, c_col = call(
        functools.partial(update_kernel, nz, ny, heads, hd),
        place,
        [hbm(key_in), hbm(value_in), *kvs, *logs],
        [sds((heads * share + 16, hd), BF16)] * nz
        + [sds((heads, long), F32), sds((long, heads), F32)],
        [
            pltpu.VMEM((heads, long), F32),
            pltpu.VMEM((heads, hd, hd), BF16),
            pltpu.VMEM((16, hd), F32),
            pltpu.VMEM((2, tok, width), BF16),
            pltpu.SemaphoreType.DMA((2,)),
        ],
        limit=40,
            flops=2 * long * hd * hd * heads,
    )
    parts = [parts[0]] + [z_turn(parts[d], d) for d in range(1, nz)]
    *entering, last_rows = call(
        functools.partial(prefix_kernel, nz, heads, hd),
        place,
        [*parts, start],
        [sds((heads * share, hd), BF16)] * nz + [sds((heads, share, hd), F32)],
        [
            pltpu.VMEM((nz, heads * share + 16, hd), BF16),
            pltpu.VMEM((nz, heads * share, hd), BF16),
            pltpu.VMEM((heads, share, hd), F32),
        ],
    )
    entering = [entering[0]] + [z_turn(entering[d], d) for d in range(1, nz)]
    (mixed,) = call(
        functools.partial(attention_kernel, nz, ny, heads, hd),
        place,
        [
            hbm(key_in),
            hbm(value_in),
            hbm(query),
            hbm(gate_in),
            *[anywhere(x) for x in kvs],
            *[anywhere(x) for x in qgs],
            *entering,
            c_row,
            c_col,
            (attn_gain_2, pl.BlockSpec((1, width), lambda n, s: (0, s[1]))),
        ],
        [sds((long, width), BF16)],
        [pltpu.VMEM((long, width), BF16)] * 4
        + [pltpu.VMEM((heads, hd, hd), BF16), pltpu.SemaphoreType.DMA((4 * ny,))],
        limit=40,
            flops=4 * long * long * width,
    )

    def across(blocks):
        return [[y_turn(x, e) for x in blocks] for e in range(1, ny)]

    held = {0: [[mixed]] + across([mixed])}
    for d in near:
        held[d] = [[z_turn(mixed, d)]]
    free = behind([mixed], [held[near[0]][0][0]])[0]
    for d in near:
        held[d] += across(held[d][0])
    halves = [free[: long // 2], free[long // 2 :]]
    for d in distant:
        held[d] = [[z_turn(x, d) for x in halves]]
    for d in distant:
        held[d] += across(held[d][0])
    w_parts = [
        (w_out, pl.BlockSpec((width, cols), lambda n, s, d=d: (lax.rem(s[1] + ny - d, ny), 0)))
        for d in range(ny)
    ]
    given = []
    for group in ([0] + near, distant):
        last = group is distant
        dzs = {d: held[d][0] for d in group}
        blocks = [x for dy in range(ny) for d in group for x in held[d][dy]]
        half = nz * slots // 2
        outs = [sds((len(group), block, cols), BF16), sds((nz * slots, cols), F32)]
        if last:
            outs = [sds((half, cols), F32), sds((half, cols), BF16)]
            outs += [sds((nz // 2, block, cols), BF16)] * 2
        given = call(
            functools.partial(project_kernel, nz, ny, cap, dzs, last),
            place,
            [anywhere(x) for x in blocks]
            + w_parts
            + [row_r, row_base, codes]
            + list(given)
            + ([hbm(residual)] if last else []),
            outs,
            [pltpu.VMEM((ny, len(group), long, width), BF16)]
            + ([pltpu.VMEM((block, cols), BF16)] if last else [])
            + [pltpu.SemaphoreType.DMA((len(blocks) + 1,))],
            limit=40,
            flops=2 * len(group) * long * head_width * cols,
        )
    keep, send, keep_all, send_all = given
    for b in range(bits):
        received = swap(send, 1 << b)
        if b < bits - 1:
            part = keep.shape[0] // 2
            send = (keep[part:] + received[part:].astype(F32)).astype(BF16)
            keep = keep[:part] + received[:part].astype(F32)
    fits = cols % 128 == 0 and cols >= 512 and slots <= 128
    (rows_out,) = call(
        rows_kernel,
        place,
        [keep, received, moe_gain_2, router_t, sign, spare],
        [sds((slots, cols if fits else cols + 128), BF16)],
    )
    send_all = behind([send_all], [rows_out])[0]
    for b in range(bits):
        received_all = swap(send_all, 1 << b)
        if b < bits - 1:
            n = keep_all.shape[0] // 2
            both = keep_all.astype(F32) + received_all.astype(F32)
            send_all, keep_all = both[n:].astype(BF16), both[:n].astype(BF16)
    rows = share // ny
    last_rows = behind([last_rows], [rows_out])[0]
    final_rows = jnp.zeros((head_count, rows, hd), F32)
    for d in range(ny):
        sent = lax.dynamic_slice_in_dim(last_rows, (y + d) % ny * rows, rows, 1)
        got = sent if d == 0 else y_turn(sent, d)
        final_rows = lax.dynamic_update_slice_in_dim(
            final_rows, got, (y - d) % ny * heads, 0
        )

    in_vmem = pl.BlockSpec(memory_space=pltpu.VMEM)

    def up(n, group, blocks, state):
        first, last = n == 0, n == len(groups) - 1
        outs = [sds((slots, units), F32)] * 2 + [sds((1, cols), F32)]
        if last:
            outs = [sds((slots, units), BF16), sds((slots, 128), F32)]
        return call(
            functools.partial(up_kernel, nz, ny, group, first, last, features),
            place,
            blocks + list(state) + [anywhere(w_gate), anywhere(w_up), spare],
            outs,
            [pltpu.VMEM((len(group), units, cols), BF16)] * 2
            + [pltpu.SemaphoreType.DMA((2 * len(group),))],
            limit=40,
            flops=4 * len(group) * slots * units * cols,
        )

    def down(n, group, blocks, state):
        first, last = n == 0, n == len(groups) - 1
        ahead = groups[-1] if first else []
        outs = [sds((slots, cols), F32)]
        outs += [sds((len(ahead), units, cols), BF16)] if ahead else []
        weights = [anywhere(w_down)]
        if last:
            outs = [sds((ret_rows, cols), BF16)] * nz
            weights = [(fetched["down"], in_vmem), weight, padded[:, None], own_base.T]
        state = call(
            functools.partial(down_kernel, nz, ny, cap, group, ahead, first, last),
            place,
            blocks + list(state) + weights,
            outs,
            []
            if last
            else [
                pltpu.VMEM((len(group), units, cols), BF16),
                pltpu.SemaphoreType.DMA((len(group) + len(ahead),)),
            ],
            limit=40,
            flops=2 * len(group) * slots * units * cols,
            held=1 if ahead else 0,
        )
        if ahead:
            fetched["down"] = state[1]
        return state if last else state[:1]

    fetched = {}
    if not fits:
        arrived = gather_z(rows_out)
        gather_y(arrived, [])
        order = jnp.stack([(z - dz) % nz * ny + (y - dy) % ny for dz, dy in places])
        at = jnp.argsort(order)
        rows_all = jnp.take(jnp.stack([arrived[p] for p in places]), at, axis=0)
        stats = jnp.sum(rows_all[:, :, cols:].astype(F32), axis=0)
        rows_all = jnp.swapaxes(rows_all[:, :, :cols], 0, 1).reshape(slots, features)
        inverse = lax.rsqrt(jnp.sum(stats[:, :3], axis=1) / features + EPS)[:, None]
        gate = mm(rows_all, w_gate[0], NT) * inverse
        hidden = (gate * sigmoid(gate) * (mm(rows_all, w_up[0], NT) * inverse)).astype(BF16)
        weight = sigmoid(jnp.sum(stats[:, 3:6], axis=1)[:, None] * inverse)
        weight = jnp.broadcast_to(weight, (slots, 128))
    else:
        hidden, weight = stages(up, rows_out)
    state = stages(down, hidden)
    returned = [state[0]] + [swap(state[r], r) for r in range(1, nz)]
    (layer_out,) = call(
        functools.partial(combine_kernel, nz, cap),
        place,
        returned + [keep_all[0], received_all[0], hbm(residual), codes, ret_r, ret_base],
        [sds((block, cols), BF16)],
        [
            pltpu.VMEM((nz * ret_rows, cols), BF16),
            pltpu.VMEM((block, cols), BF16),
            pltpu.SemaphoreType.DMA((1,)),
        ],
    )
    return layer_out, final_rows


def solution(mesh):
    in_specs = (
        P("exp", "seq"),
        P("seq", "exp"),
        P("seq", "exp"),
        P("seq", "exp"),
        P("seq", "exp"),
        P("seq", "exp"),
        P("exp", None, None),
        P("exp"),
        P("exp", "seq"),
        P("seq"),
        P("seq", None),
        P("exp", "seq", None),
        P("exp", "seq", None),
        P("exp", None, "seq"),
        P("exp", None),
        P(),
    )
    out_specs = (P("exp", "seq"), P("exp", "seq", None))
    return jax.shard_map(local, mesh=mesh, in_specs=in_specs, out_specs=out_specs, check_vma=False)
```

```python
import functools
import jax
import jax.numpy as jnp
import numpy as np
from jax import lax
from jax.experimental import pallas as pl
from jax.experimental.pallas import tpu as pltpu
from jax.sharding import PartitionSpec as P

EPS = 1e-05
F32 = jnp.float32
BF16 = jnp.bfloat16
I32 = jnp.int32
HIGHEST = lax.Precision.HIGHEST
NT = (((1,), (1,)), ((), ()))
TN = (((0,), (0,)), ((), ()))
NN = (((1,), (0,)), ((), ()))


def mm(a, b, dims=NN, precision=None):
    return lax.dot_general(a, b, dims, precision=precision, preferred_element_type=F32)


def sigmoid(v):
    return 1.0 / (1.0 + jnp.exp(-v))


def bit_reversed(p, bits):
    r = 0
    for b in range(bits):
        r = r * 2 + ((p >> b) & 1)
    return r


def whole(shape):
    return pl.BlockSpec(tuple(shape), lambda i, s: (0,) * len(shape))


def call(kernel, place, operands, outs, scratch=(), flops=0, limit=40, held=0):
    arrays, specs, moved = [], [], 0
    for item in operands:
        array, spec = item if isinstance(item, tuple) else (item, whole(item.shape))
        arrays.append(array)
        specs.append(spec)
        moved += array.size * array.dtype.itemsize
    moved += sum(o.size * o.dtype.itemsize for o in outs)
    return pl.pallas_call(
        kernel,
        out_shape=list(outs),
        grid_spec=pltpu.PrefetchScalarGridSpec(
            num_scalar_prefetch=1,
            grid=(1,),
            in_specs=specs,
            out_specs=[
                pl.BlockSpec(memory_space=pltpu.VMEM) if n >= len(outs) - held else whole(o.shape)
                for n, o in enumerate(outs)
            ],
            scratch_shapes=list(scratch),
        ),
        compiler_params=pltpu.CompilerParams(vmem_limit_bytes=limit * 1024 * 1024),
        cost_estimate=pl.CostEstimate(flops=flops, bytes_accessed=moved, transcendentals=0),
    )(place, *arrays)


def hbm(array):
    return (array, pl.BlockSpec(memory_space=pltpu.HBM))


def anywhere(array):
    return (array, pl.BlockSpec(memory_space=pl.ANY))


def run_copies(pairs, sem):
    copies = [pltpu.make_async_copy(a, b, sem.at[n]) for n, (a, b) in enumerate(pairs)]
    for c in copies:
        c.start()
    return copies


def one_hot(mask):
    return mask.astype(F32).astype(BF16)


def turned_back(z, back, nz):
    return jnp.where(z < back, z - back + nz, z - back)


def sds(shape, dtype):
    return jax.ShapeDtypeStruct(tuple(shape), dtype)


def pieces(x):
    hi = x.astype(BF16)
    rest = x - hi.astype(F32)
    mid = rest.astype(BF16)
    return hi, mid, (rest - mid.astype(F32)).astype(BF16)


def routing_kernel(nz, cap, own_rows, s, *refs):
    keep = refs[0]
    given = refs[1 : nz + 1]
    base, state, codes, sign, spare, start, ids, sem = refs[nz + 1 :]
    j = s[2]
    heads, share, _ = start.shape
    rows = pl.ds(pl.multiple_of(s[0] * share, share), share)
    fetch = pltpu.make_async_copy(state.at[pl.ds(s[1] * heads, heads), rows, :], start, sem)
    fetch.start()
    block = given[0].shape[1]
    for r in range(nz):
        ids[lax.bitwise_xor(j, r)] = given[r][...]
    rows = lax.broadcasted_iota(I32, (block, block), 0)
    cols = lax.broadcasted_iota(I32, (block, block), 1)
    strict = one_hot(rows < cols)
    own = base[...] + j * (nz * cap)
    earlier = [jnp.zeros((1, 1), I32) for _ in range(nz)]
    other = jnp.zeros((own_rows, 1), I32)
    taken = jnp.zeros((own_rows, 1), I32)
    place = lax.broadcasted_iota(I32, (16, block), 0)
    for b in range(nz):
        first, second = ids[b, 0:1, :], ids[b, 1:2, :]
        named = ((place == first) | (place == second)) & (place < nz)
        ranks = mm(one_hot(named), strict).astype(I32)
        slots = []
        for e in range(nz):
            hit = (first == e) | (second == e)
            rank = ranks[e : e + 1, :]
            kept = hit & (rank + earlier[e] < keep[e])
            slots.append(jnp.where(kept, (e * nz + b) * cap + rank, -1))
            earlier[e] = earlier[e] + jnp.sum(hit.astype(I32), axis=1, keepdims=True)
        top = functools.reduce(jnp.maximum, slots)
        rest = functools.reduce(jnp.maximum, [jnp.where(c == top, -1, c) for c in slots])
        codes[b, 0:1, :] = top
        codes[b, 1:2, :] = rest
        holds = (own == top) | (own == rest)
        taken = taken + jnp.sum(holds.astype(I32), axis=1, keepdims=True)
        other = other + jnp.sum(jnp.where(holds, first + second, 0), axis=1, keepdims=True)
    every = lax.broadcasted_iota(I32, sign.shape, 1)
    sign[...] = (every == j).astype(F32) - (every == other - j).astype(F32)
    index = lax.broadcasted_iota(I32, (own_rows, 1), 0)
    unused = jnp.min(jnp.where(taken == 0, index, own_rows), axis=0, keepdims=True)
    spare[...] = jnp.broadcast_to((index == unused).astype(F32), spare.shape)
    fetch.wait()


def pack_kernel(away, ny, a, b, out, sem):
    width = out.shape[2]
    share = lax.rem(lax.rem(lax.axis_index("seq"), ny) + away, ny)
    at = pl.ds(pl.multiple_of(share * width, 128), width)
    for c in run_copies([(a.at[:, at], out.at[0]), (b.at[:, at], out.at[1])], sem):
        c.wait()


def update_kernel(nz, ny, heads, hd, s, *refs):
    z, y = s[0], s[1]
    n = ny - 1
    k_arg, v_arg = refs[0], refs[1]
    kv = refs[2 : 2 + n]
    logs = refs[2 + n : 2 + n + ny]
    outs = refs[2 + n + ny : 2 + n + ny + nz]
    c_row, c_col, log_all, state, tail, own, sem = refs[2 + n + ny + nz :]
    tok = k_arg.shape[0]
    total_tok = tok * ny
    share = hd // nz
    mine = pl.ds(pl.multiple_of(y * heads * hd, 128), heads * hd)
    copies = run_copies([(x.at[:, mine], own.at[m]) for m, x in enumerate((k_arg, v_arg))], sem)
    for d in range(ny):
        at = pl.multiple_of(lax.rem(y + ny - d, ny) * tok, tok)
        log_all[:, pl.ds(at, tok)] = logs[d][pl.ds(y * heads, heads), :]
    rows = lax.broadcasted_iota(I32, (total_tok, total_tok), 0)
    cols = lax.broadcasted_iota(I32, (total_tok, total_tok), 1)
    c_row[...] = mm(log_all[...], (rows <= cols).astype(F32), precision=HIGHEST)
    c_col[...] = mm((rows >= cols).astype(F32), log_all[...], NT, precision=HIGHEST)
    total = c_row[:, total_tok - 1 : total_tok]
    for c in copies:
        c.wait()
    for h in range(heads):
        add = None
        for d in range(ny):
            at = pl.multiple_of(lax.rem(y + ny - d, ny) * tok, tok)
            lanes = slice(h * hd, (h + 1) * hd)
            pair = own if d == 0 else kv[d - 1]
            key = pair[0, :, lanes].astype(F32)
            decay = jnp.exp(total[h : h + 1, :] - c_col[pl.ds(at, tok), h : h + 1])
            weighted = (key * sigmoid(key) * decay).astype(BF16)
            part = mm(weighted, pair[1, :, lanes], TN)
            add = part if add is None else add + part
        state[h] = add.astype(BF16)
    tail[...] = jnp.zeros_like(tail)
    hi, mid, lo = pieces(total)
    lane = lax.broadcasted_iota(I32, (heads, hd), 1)
    tail[0:heads, :] = jnp.where(
        lane == 0,
        hi.astype(F32),
        jnp.where(lane == 1, mid.astype(F32), jnp.where(lane == 2, lo.astype(F32), 0.0)),
    )
    for d in range(nz):
        at = pl.multiple_of(lax.rem(z + d, nz) * share, share)
        for h in range(heads):
            outs[d][h * share : (h + 1) * share, :] = state[h, pl.ds(at, share), :]
        outs[d][heads * share :, :] = tail[...].astype(BF16)


def prefix_kernel(nz, heads, hd, s, *refs):
    z = s[0]
    parts = refs[:nz]
    start = refs[nz]
    outs = refs[nz + 1 : 2 * nz + 1]
    final, held, entering, run = refs[2 * nz + 1 :]
    share = hd // nz
    run[...] = start[...]
    for d in range(nz):
        held[lax.rem(z + nz - d, nz)] = parts[d][...]
    for p in range(nz):
        logs = jnp.sum(held[p, heads * share :, :].astype(F32), axis=1, keepdims=True)
        keep = jnp.exp(logs)
        for h in range(heads):
            rows = slice(h * share, (h + 1) * share)
            now = run[h]
            entering[p, rows, :] = now.astype(BF16)
            run[h] = keep[h : h + 1, :] * now + held[p, rows, :].astype(F32)
    final[...] = run[...]
    for d in range(nz):
        outs[d][...] = entering[lax.rem(z + d, nz)]


def attention_kernel(nz, ny, heads, hd, s, *refs):
    z, y = s[0], s[1]
    n = ny - 1
    args = refs[:4]
    kv = refs[4 : 4 + n]
    qg = refs[4 + n : 4 + 2 * n]
    states = refs[4 + 2 * n : 4 + 2 * n + nz]
    c_row, c_col, gain, out, ks, vs, qs, gs, state, sem = refs[4 + 2 * n + nz :]
    tok = args[0].shape[0]
    total_tok = tok * ny
    share = hd // nz
    mine = pl.ds(pl.multiple_of(y * heads * hd, 128), heads * hd)
    moves = []
    for d in range(ny):
        at = pl.ds(pl.multiple_of(lax.rem(y + ny - d, ny) * tok, tok), tok)
        for m, to in enumerate((ks, vs, qs, gs)):
            if d == 0:
                source = args[m].at[:, mine]
            else:
                source = (kv if m < 2 else qg)[d - 1].at[m % 2]
            moves.append((source, to.at[at, :]))
    copies = run_copies(moves, sem)
    for d in range(nz):
        at = pl.ds(pl.multiple_of(lax.rem(z + nz - d, nz) * share, share), share)
        for h in range(heads):
            state[h, at, :] = states[d][h * share : (h + 1) * share, :]
    rows = lax.broadcasted_iota(I32, (total_tok, total_tok), 0)
    cols = lax.broadcasted_iota(I32, (total_tok, total_tok), 1)
    causal = rows >= cols
    for c in copies:
        c.wait()
    for h in range(heads):
        lanes = slice(h * hd, (h + 1) * hd)
        query = qs[:, lanes].astype(F32)
        query = query * sigmoid(query)
        key = ks[:, lanes].astype(F32)
        key = (key * sigmoid(key)).astype(BF16)
        col = c_col[:, h : h + 1]
        gap = jnp.where(causal, col - c_row[h : h + 1, :], 0.0)
        decay = jnp.where(causal, jnp.exp(gap), 0.0)
        scores = mm(query.astype(BF16), key, NT) * decay
        att = mm(scores.astype(BF16), vs[:, lanes])
        att = att + mm((query * jnp.exp(col)).astype(BF16), state[h])
        square = jnp.mean(att * att, axis=1, keepdims=True)
        gate = sigmoid(gs[:, lanes].astype(F32))
        out[:, lanes] = (att * lax.rsqrt(square + EPS) * gain[:, lanes] * gate).astype(BF16)


def project_kernel(nz, ny, cap, dzs, last, s, *refs):
    z, j = s[0], s[2]
    bits = nz.bit_length() - 1
    parts = [len(p) for p in dzs.values()]
    count = sum(parts) * ny
    blocks = refs[:count]
    weights = refs[count : count + ny]
    r_ids, b_ids, codes = refs[count + ny : count + ny + 3]
    refs = refs[count + ny + 3 :]
    if last:
        done, sums, residual = refs[:3]
        keep, send, keep_all, send_all, stacked, own, sem = refs[3:]
    else:
        done, sums, stacked, sem = refs
    rows = stacked.shape[2]
    moves = []
    at = 0
    for dy in range(ny):
        for n, (dz, pieces_of) in enumerate(dzs.items()):
            first = 0
            for _ in pieces_of:
                size = blocks[at].shape[0]
                moves.append((blocks[at], stacked.at[dy, n, pl.ds(first, size)]))
                first += size
                at += 1
    if last:
        moves.append((residual, own))
    copies = run_copies(moves, sem)
    ids = lax.bitwise_xor(r_ids[...], j) * (nz * cap) + b_ids[...]
    pick = lambda b: one_hot((ids == codes[b, 0:1, :]) | (ids == codes[b, 1:2, :]))
    total_rows = sums[...] if last else None
    for c in copies:
        c.wait()
    projected = {}
    for n, dz in enumerate(dzs):
        total = None
        for dy in range(ny):
            part = mm(stacked[dy, n], weights[dy][...])
            total = part if total is None else total + part
        projected[dz] = total.astype(BF16)
        part = mm(pick(lax.rem(z + nz - dz, nz)), projected[dz])
        total_rows = part if total_rows is None else total_rows + part
    if not last:
        for n, dz in enumerate(dzs):
            done[n] = projected[dz]
        sums[...] = total_rows
        return
    total_rows = total_rows + mm(pick(j), own[...])
    half = keep.shape[0]
    keep[...] = total_rows[:half, :]
    send[...] = total_rows[half:, :].astype(BF16)
    before = [dz for dz in range(nz) if dz not in dzs]
    for p in range(nz):
        block = lax.bitwise_xor(jnp.int32(bit_reversed(p, bits)), j)
        away = lax.rem(z + nz - block, nz)
        to = keep_all.at[p] if p < nz // 2 else send_all.at[p - nz // 2]
        for dz in range(nz):

            @pl.when(away == dz)
            def _(dz=dz):
                to[...] = projected[dz] if dz in dzs else done[before.index(dz)]


def diagonal(rows):
    shape = (rows, 128)
    return lax.broadcasted_iota(I32, shape, 0) == lax.broadcasted_iota(I32, shape, 1)


def rows_kernel(s, keep, received, gain, router_t, sign, spare, out):
    width = gain.shape[1]
    rows = keep[...] + received[...].astype(F32)
    square = jnp.sum(rows * rows, axis=1, keepdims=True)
    scaled = rows * gain[...]
    logits = mm(scaled, router_t[...], NT, precision=HIGHEST)
    gap = jnp.sum(logits * sign[...], axis=1, keepdims=True)
    if out.shape[1] == width:
        lines = []
        for value in (square, gap):
            for piece in pieces(value)[:2]:
                spread = jnp.where(diagonal(rows.shape[0]), piece.astype(F32), 0.0)
                lines.append(jnp.sum(spread, axis=0, keepdims=True))
        lines.append(jnp.zeros((1, width - 128 * len(lines)), F32))
        line = jnp.concatenate(lines, axis=1)
        out[...] = jnp.where(spare[:, 0:1] > 0.0, line, scaled).astype(BF16)
        return
    out[:, :width] = scaled.astype(BF16)
    lane = lax.broadcasted_iota(I32, (rows.shape[0], 128), 1)
    stats = jnp.zeros((rows.shape[0], 128), F32)
    for at, value in ((0, square), (3, gap)):
        for k, piece in enumerate(pieces(value)):
            stats = jnp.where(lane == at + k, piece.astype(F32), stats)
    out[:, width:] = stats.astype(BF16)


def source_of(s, nz, ny, place):
    z = lax.rem(s[0] + nz - place[0], nz)
    return z * ny + lax.rem(s[1] + ny - place[1], ny)


def throttled(copies, n, depth):
    if n < 0:
        for c in copies[:depth]:
            c.start()
        return
    copies[n].wait()
    if n + depth < len(copies):
        copies[n + depth].start()


def up_kernel(nz, ny, places, first, last, features, s, *refs):
    count = len(places)
    blocks = refs[:count]
    refs = refs[count:]
    before = () if first else refs[:3]
    refs = refs[0 if first else 3 :]
    weights, spare = refs[:2], refs[2]
    outs, buffers, sem = refs[3:-3], refs[-3:-1], refs[-1]
    slots, width = blocks[0].shape
    is_spare = spare[:, 0:1] > 0.0
    copies = []
    for n, p in enumerate(places):
        lanes = pl.ds(pl.multiple_of(source_of(s, nz, ny, p) * width, 128), width)
        for m in range(2):
            source = weights[m].at[0, :, lanes]
            copies.append(pltpu.make_async_copy(source, buffers[m].at[n], sem.at[len(copies)]))
    throttled(copies, -1, 6)
    gate, up, stats = (None, None, None) if first else (b[...] for b in before)
    for n in range(count):
        rows = blocks[n][...].astype(F32)
        part = jnp.sum(jnp.where(is_spare, rows, 0.0), axis=0, keepdims=True)
        stats = part if stats is None else stats + part
        rows = jnp.where(is_spare, 0.0, rows).astype(BF16)
        throttled(copies, 2 * n, 6)
        part = mm(rows, buffers[0][n], NT)
        gate = part if gate is None else gate + part
        throttled(copies, 2 * n + 1, 6)
        part = mm(rows, buffers[1][n], NT)
        up = part if up is None else up + part
    if not last:
        outs[0][...] = gate
        outs[1][...] = up
        outs[2][...] = stats
        return
    sums = [stats[:, at : at + 128] + stats[:, at + 128 : at + 256] for at in (0, 256)]
    sums = [jnp.where(diagonal(slots), line, 0.0) for line in sums]
    square, gap = [jnp.sum(line, axis=1, keepdims=True) for line in sums]
    inverse = lax.rsqrt(square / features + EPS)
    gate = gate * inverse
    outs[0][...] = (gate * sigmoid(gate) * (up * inverse)).astype(BF16)
    outs[1][...] = jnp.broadcast_to(sigmoid(gap * inverse), outs[1].shape)


def down_kernel(nz, ny, cap, places, ahead, first, last, s, *refs):
    j = s[2]
    count = len(places)
    blocks = refs[:count]
    refs = refs[count:]
    before = None if first else refs[0]
    refs = refs[0 if first else 1 :]
    w_down = refs[0]
    refs = refs[1:]
    depth = blocks[0].shape[1]
    copies = []
    if last:
        weight, out_base, row_base = refs[:3]
        outs, buf = refs[3:], w_down
    else:
        outs = refs[:1]
        kept = refs[1] if ahead else None
        buf, sem = refs[-2:]
        jobs = [(p, buf, n) for n, p in enumerate(places)]
        jobs += [(p, kept, n) for n, p in enumerate(ahead)]
        for p, to, n in jobs:
            at = pl.ds(pl.multiple_of(source_of(s, nz, ny, p) * depth, depth), depth)
            source = w_down.at[0, at, :]
            copies.append(pltpu.make_async_copy(source, to.at[n], sem.at[len(copies)]))
        throttled(copies, -1, 5)
    total = None if first else before[...]
    for n in range(count):
        if not last:
            throttled(copies, n, 5)
        part = mm(blocks[n][...], buf[n])
        total = part if total is None else total + part
    if not last:
        outs[0][...] = total
        for n in range(count, len(copies)):
            throttled(copies, n, 5)
        return
    result = (total * weight[:, 0:1]).astype(BF16)
    for r, out in enumerate(outs):
        wanted = out_base[...] + lax.bitwise_xor(j, r) * cap
        out[...] = mm(one_hot(wanted == row_base[...]), result).astype(BF16)


def combine_kernel(nz, cap, s, *refs):
    j = s[2]
    returned = refs[:nz]
    keep, received, residual, codes, ret_r, ret_base, out, stacked, own, sem = refs[nz:]
    copies = run_copies([(residual, own)], sem)
    rows = returned[0].shape[0]
    for n in range(nz):
        stacked[n * rows : (n + 1) * rows, :] = returned[n][...]
    ids = lax.bitwise_xor(ret_r[...], j) * (nz * cap) + ret_base[...] + j * cap
    pick = (ids == codes[j, 0:1, :]) | (ids == codes[j, 1:2, :])
    added = mm(one_hot(pick), stacked[...], TN)
    copies[0].wait()
    total = own[...].astype(F32) + (keep[...].astype(F32) + received[...].astype(F32))
    out[...] = (total + added).astype(BF16)


def local(
    residual,
    query,
    key_in,
    value_in,
    gate_in,
    log_decay,
    state_in,
    attn_gain,
    w_out,
    moe_gain,
    router,
    w_gate,
    w_up,
    w_down,
    expert_ids,
    keep_counts,
):
    nz = lax.axis_size("exp")
    ny = lax.axis_size("seq") // nz
    bits = nz.bit_length() - 1
    i = lax.axis_index("seq").astype(I32)
    j = lax.axis_index("exp").astype(I32)
    z, y = i // ny, i % ny
    place = jnp.stack([z, y, j])

    tok, head_width = query.shape
    head_count, hd = state_in.shape[0], state_in.shape[2]
    heads = head_count // ny
    width = heads * hd
    block, cols = residual.shape
    features = w_gate.shape[2]
    units = w_gate.shape[1]
    experts = router.shape[1]
    cap = 5 * block * nz // (2 * nz * experts)
    slots = nz * cap

    def z_turn(a, d):
        pairs = [(p * ny + q, (p + d) % nz * ny + q) for p in range(nz) for q in range(ny)]
        return lax.ppermute(a, "seq", pairs)

    def y_turn(a, d):
        pairs = [(p * ny + q, p * ny + (q + d) % ny) for p in range(nz) for q in range(ny)]
        return lax.ppermute(a, "seq", pairs)

    def swap(a, r):
        return lax.ppermute(a, "exp", [(p, p ^ r) for p in range(nz)])

    z_order = sorted(range(1, nz), key=lambda d: (min(d, nz - d), d))
    near = [d for d in z_order if min(d, nz - d) == 1]
    distant = [d for d in z_order if d not in near]
    places = [(dz, dy) for dy in range(ny) for dz in range(nz)]

    def behind(values, events):
        return list(lax.optimization_barrier((tuple(values), tuple(events)))[0])

    def gather_z(a):
        held = {(0, 0): a}
        for d in range(1, ny):
            held[0, d] = y_turn(a, d)
        for d in z_order:
            held[d, 0] = z_turn(a, d)
        return held

    def gather_y(held, events):
        for d in z_order:
            x = held[d, 0]
            if d == z_order[-1] and events:
                x = held[d, 0] = behind([x], events)[0]
            for e in range(1, ny):
                held[d, e] = y_turn(x, e)

    def stages(run, a, groups):
        arrived = gather_z(a)
        state = []
        if len(groups) == 2:
            gather_y(arrived, [])
        for n, group in enumerate(groups):
            blocks = [arrived[p] for p in group]
            state = run(group, blocks, state, n == 0, n == len(groups) - 1)
            if n == 0 and len(groups) == 3:
                gather_y(arrived, state)
        return state

    groups = [[(0, 0)], [(0, d) for d in range(1, ny)] + [(d, 0) for d in z_order]]
    groups.append([(d, e) for d in z_order for e in range(1, ny)])

    slot = np.arange(cap)
    row_r = np.repeat([bit_reversed(p, bits) for p in range(nz)], slots).astype(np.int32)[:, None]
    row_base = np.tile((np.arange(nz)[:, None] * cap + slot).reshape(slots), nz)
    row_base = row_base.astype(np.int32)[:, None]
    own_base = row_base[:slots]
    ret_rows = cap + -cap % 16
    padded = np.where(np.arange(ret_rows) < cap, np.arange(ret_rows), -(10**8)).astype(np.int32)
    ret_r = np.repeat(np.arange(nz), ret_rows).astype(np.int32)[:, None]
    ret_base = np.tile(padded, nz)[:, None]

    logs_t = jnp.transpose(log_decay)
    logs, kvs, qgs = [logs_t], [], []
    for d in range(1, ny):
        pack = pl.pallas_call(
            functools.partial(pack_kernel, d, ny),
            out_shape=sds((2, tok, width), BF16),
            in_specs=[pl.BlockSpec(memory_space=pltpu.HBM)] * 2,
            out_specs=pl.BlockSpec(memory_space=pltpu.VMEM),
            scratch_shapes=[pltpu.SemaphoreType.DMA((2,))],
            compiler_params=pltpu.CompilerParams(vmem_limit_bytes=60 * 1024 * 1024),
        )
        kvs.append(y_turn(pack(key_in, value_in), d))
        logs.append(y_turn(logs_t, d))
        qgs.append(pack(query, gate_in))
    ids = jnp.transpose(expert_ids)
    share = hd // nz
    codes, sign, spare, start = call(
        functools.partial(routing_kernel, nz, cap, slots),
        place,
        [(keep_counts, pl.BlockSpec(memory_space=pltpu.SMEM))]
        + [ids]
        + [swap(ids, r) for r in range(1, nz)]
        + [own_base, hbm(state_in)],
        [
            sds((nz, 2, block), I32),
            sds((slots, experts), F32),
            sds((slots, 128), F32),
            sds((heads, share, hd), F32),
        ],
        [pltpu.VMEM((nz, 2, block), I32), pltpu.SemaphoreType.DMA],
    )
    attn_gain_2, moe_gain_2, router_t = attn_gain[None], moe_gain[None], jnp.transpose(router)
    prepared = [codes, sign, spare, start, attn_gain_2, moe_gain_2]
    qgs = [y_turn(qg, d + 1) for d, qg in enumerate(behind(qgs, kvs + logs + prepared))]
    share = hd // nz
    long = tok * ny
    *parts, c_row, c_col = call(
        functools.partial(update_kernel, nz, ny, heads, hd),
        place,
        [hbm(key_in), hbm(value_in), *kvs, *logs],
        [sds((heads * share + 16, hd), BF16)] * nz
        + [sds((heads, long), F32), sds((long, heads), F32)],
        [
            pltpu.VMEM((heads, long), F32),
            pltpu.VMEM((heads, hd, hd), BF16),
            pltpu.VMEM((16, hd), F32),
            pltpu.VMEM((2, tok, width), BF16),
            pltpu.SemaphoreType.DMA((2,)),
        ],
        limit=40,
            flops=2 * long * hd * hd * heads,
    )
    parts = [parts[0]] + [z_turn(parts[d], d) for d in range(1, nz)]
    *entering, last_rows = call(
        functools.partial(prefix_kernel, nz, heads, hd),
        place,
        [*parts, start],
        [sds((heads * share, hd), BF16)] * nz + [sds((heads, share, hd), F32)],
        [
            pltpu.VMEM((nz, heads * share + 16, hd), BF16),
            pltpu.VMEM((nz, heads * share, hd), BF16),
            pltpu.VMEM((heads, share, hd), F32),
        ],
    )
    entering = [entering[0]] + [z_turn(entering[d], d) for d in range(1, nz)]
    (mixed,) = call(
        functools.partial(attention_kernel, nz, ny, heads, hd),
        place,
        [
            hbm(key_in),
            hbm(value_in),
            hbm(query),
            hbm(gate_in),
            *[anywhere(x) for x in kvs],
            *[anywhere(x) for x in qgs],
            *entering,
            c_row,
            c_col,
            (attn_gain_2, pl.BlockSpec((1, width), lambda n, s: (0, s[1]))),
        ],
        [sds((long, width), BF16)],
        [pltpu.VMEM((long, width), BF16)] * 4
        + [pltpu.VMEM((heads, hd, hd), BF16), pltpu.SemaphoreType.DMA((4 * ny,))],
        limit=40,
            flops=4 * long * long * width,
    )

    def across(blocks):
        return [[y_turn(x, e) for x in blocks] for e in range(1, ny)]

    held = {0: [[mixed]] + across([mixed])}
    for d in near:
        held[d] = [[z_turn(mixed, d)]]
    free = behind([mixed], [held[near[0]][0][0]])[0]
    for d in near:
        held[d] += across(held[d][0])
    halves = [free[: long // 2], free[long // 2 :]]
    for d in distant:
        held[d] = [[z_turn(x, d) for x in halves]]
    for d in distant:
        held[d] += across(held[d][0])
    w_parts = [
        (w_out, pl.BlockSpec((width, cols), lambda n, s, d=d: (lax.rem(s[1] + ny - d, ny), 0)))
        for d in range(ny)
    ]
    given = []
    for group in ([0] + near, distant):
        last = group is distant
        dzs = {d: held[d][0] for d in group}
        blocks = [x for dy in range(ny) for d in group for x in held[d][dy]]
        half = nz * slots // 2
        outs = [sds((len(group), block, cols), BF16), sds((nz * slots, cols), F32)]
        if last:
            outs = [sds((half, cols), F32), sds((half, cols), BF16)]
            outs += [sds((nz // 2, block, cols), BF16)] * 2
        given = call(
            functools.partial(project_kernel, nz, ny, cap, dzs, last),
            place,
            [anywhere(x) for x in blocks]
            + w_parts
            + [row_r, row_base, codes]
            + list(given)
            + ([hbm(residual)] if last else []),
            outs,
            [pltpu.VMEM((ny, len(group), long, width), BF16)]
            + ([pltpu.VMEM((block, cols), BF16)] if last else [])
            + [pltpu.SemaphoreType.DMA((len(blocks) + 1,))],
            limit=40,
            flops=2 * len(group) * long * head_width * cols,
        )
    keep, send, keep_all, send_all = given
    for b in range(bits):
        received = swap(send, 1 << b)
        if b < bits - 1:
            part = keep.shape[0] // 2
            send = (keep[part:] + received[part:].astype(F32)).astype(BF16)
            keep = keep[:part] + received[:part].astype(F32)
    fits = cols % 128 == 0 and cols >= 512 and slots <= 128
    (rows_out,) = call(
        rows_kernel,
        place,
        [keep, received, moe_gain_2, router_t, sign, spare],
        [sds((slots, cols if fits else cols + 128), BF16)],
    )
    send_all = behind([send_all], [rows_out])[0]
    for b in range(bits):
        received_all = swap(send_all, 1 << b)
        if b < bits - 1:
            n = keep_all.shape[0] // 2
            both = keep_all.astype(F32) + received_all.astype(F32)
            send_all, keep_all = both[n:].astype(BF16), both[:n].astype(BF16)
    rows = share // ny
    last_rows = behind([last_rows], [rows_out])[0]
    final_rows = jnp.zeros((head_count, rows, hd), F32)
    for d in range(ny):
        sent = lax.dynamic_slice_in_dim(last_rows, (y + d) % ny * rows, rows, 1)
        got = sent if d == 0 else y_turn(sent, d)
        final_rows = lax.dynamic_update_slice_in_dim(
            final_rows, got, (y - d) % ny * heads, 0
        )

    in_vmem = pl.BlockSpec(memory_space=pltpu.VMEM)

    def up(group, blocks, state, first, last):
        outs = [sds((slots, units), F32)] * 2 + [sds((1, cols), F32)]
        if last:
            outs = [sds((slots, units), BF16), sds((slots, 128), F32)]
        return call(
            functools.partial(up_kernel, nz, ny, group, first, last, features),
            place,
            blocks + list(state) + [anywhere(w_gate), anywhere(w_up), spare],
            outs,
            [pltpu.VMEM((len(group), units, cols), BF16)] * 2
            + [pltpu.SemaphoreType.DMA((2 * len(group),))],
            limit=40,
            flops=4 * len(group) * slots * units * cols,
        )

    def down(group, blocks, state, first, last):
        ahead = groups[-1] if first else []
        outs = [sds((slots, cols), F32)]
        outs += [sds((len(ahead), units, cols), BF16)] if ahead else []
        weights = [anywhere(w_down)]
        if last:
            outs = [sds((ret_rows, cols), BF16)] * nz
            weights = [(fetched["down"], in_vmem), weight, padded[:, None], own_base.T]
        state = call(
            functools.partial(down_kernel, nz, ny, cap, group, ahead, first, last),
            place,
            blocks + list(state) + weights,
            outs,
            []
            if last
            else [
                pltpu.VMEM((len(group), units, cols), BF16),
                pltpu.SemaphoreType.DMA((len(group) + len(ahead),)),
            ],
            limit=40,
            flops=2 * len(group) * slots * units * cols,
            held=1 if ahead else 0,
        )
        if ahead:
            fetched["down"] = state[1]
        return state if last else state[:1]

    fetched = {}
    if not fits:
        arrived = gather_z(rows_out)
        gather_y(arrived, [])
        order = jnp.stack([(z - dz) % nz * ny + (y - dy) % ny for dz, dy in places])
        at = jnp.argsort(order)
        rows_all = jnp.take(jnp.stack([arrived[p] for p in places]), at, axis=0)
        stats = jnp.sum(rows_all[:, :, cols:].astype(F32), axis=0)
        rows_all = jnp.swapaxes(rows_all[:, :, :cols], 0, 1).reshape(slots, features)
        inverse = lax.rsqrt(jnp.sum(stats[:, :3], axis=1) / features + EPS)[:, None]
        gate = mm(rows_all, w_gate[0], NT) * inverse
        hidden = (gate * sigmoid(gate) * (mm(rows_all, w_up[0], NT) * inverse)).astype(BF16)
        weight = sigmoid(jnp.sum(stats[:, 3:6], axis=1)[:, None] * inverse)
        weight = jnp.broadcast_to(weight, (slots, 128))
    else:
        hidden, weight = stages(up, rows_out, groups)
    state = stages(down, hidden, [groups[0] + groups[1], groups[2]])
    returned = [state[0]] + [swap(state[r], r) for r in range(1, nz)]
    (layer_out,) = call(
        functools.partial(combine_kernel, nz, cap),
        place,
        returned + [keep_all[0], received_all[0], hbm(residual), codes, ret_r, ret_base],
        [sds((block, cols), BF16)],
        [
            pltpu.VMEM((nz * ret_rows, cols), BF16),
            pltpu.VMEM((block, cols), BF16),
            pltpu.SemaphoreType.DMA((1,)),
        ],
    )
    return layer_out, final_rows


def solution(mesh):
    in_specs = (
        P("exp", "seq"),
        P("seq", "exp"),
        P("seq", "exp"),
        P("seq", "exp"),
        P("seq", "exp"),
        P("seq", "exp"),
        P("exp", None, None),
        P("exp"),
        P("exp", "seq"),
        P("seq"),
        P("seq", None),
        P("exp", "seq", None),
        P("exp", "seq", None),
        P("exp", None, "seq"),
        P("exp", None),
        P(),
    )
    out_specs = (P("exp", "seq"), P("exp", "seq", None))
    return jax.shard_map(local, mesh=mesh, in_specs=in_specs, out_specs=out_specs, check_vma=False)
```

```python
import functools
import jax
import jax.numpy as jnp
import numpy as np
from jax import lax
from jax.experimental import pallas as pl
from jax.experimental.pallas import tpu as pltpu
from jax.sharding import PartitionSpec as P

EPS = 1e-05
F32 = jnp.float32
BF16 = jnp.bfloat16
I32 = jnp.int32
HIGHEST = lax.Precision.HIGHEST
NT = (((1,), (1,)), ((), ()))
TN = (((0,), (0,)), ((), ()))
NN = (((1,), (0,)), ((), ()))


def mm(a, b, dims=NN, precision=None):
    return lax.dot_general(a, b, dims, precision=precision, preferred_element_type=F32)


def sigmoid(v):
    return 1.0 / (1.0 + jnp.exp(-v))


def bit_reversed(p, bits):
    r = 0
    for b in range(bits):
        r = r * 2 + ((p >> b) & 1)
    return r


def whole(shape):
    return pl.BlockSpec(tuple(shape), lambda i, s: (0,) * len(shape))


def call(kernel, place, operands, outs, scratch=(), flops=0, limit=40, held=0):
    arrays, specs, moved = [], [], 0
    for item in operands:
        array, spec = item if isinstance(item, tuple) else (item, whole(item.shape))
        arrays.append(array)
        specs.append(spec)
        moved += array.size * array.dtype.itemsize
    moved += sum(o.size * o.dtype.itemsize for o in outs)
    return pl.pallas_call(
        kernel,
        out_shape=list(outs),
        grid_spec=pltpu.PrefetchScalarGridSpec(
            num_scalar_prefetch=1,
            grid=(1,),
            in_specs=specs,
            out_specs=[
                pl.BlockSpec(memory_space=pltpu.VMEM) if n >= len(outs) - held else whole(o.shape)
                for n, o in enumerate(outs)
            ],
            scratch_shapes=list(scratch),
        ),
        compiler_params=pltpu.CompilerParams(vmem_limit_bytes=limit * 1024 * 1024),
        cost_estimate=pl.CostEstimate(flops=flops, bytes_accessed=moved, transcendentals=0),
    )(place, *arrays)


def hbm(array):
    return (array, pl.BlockSpec(memory_space=pltpu.HBM))


def anywhere(array):
    return (array, pl.BlockSpec(memory_space=pl.ANY))


def run_copies(pairs, sem):
    copies = [pltpu.make_async_copy(a, b, sem.at[n]) for n, (a, b) in enumerate(pairs)]
    for c in copies:
        c.start()
    return copies


def one_hot(mask):
    return mask.astype(F32).astype(BF16)


def turned_back(z, back, nz):
    return jnp.where(z < back, z - back + nz, z - back)


def sds(shape, dtype):
    return jax.ShapeDtypeStruct(tuple(shape), dtype)


def pieces(x):
    hi = x.astype(BF16)
    rest = x - hi.astype(F32)
    mid = rest.astype(BF16)
    return hi, mid, (rest - mid.astype(F32)).astype(BF16)


def routing_kernel(nz, cap, own_rows, s, *refs):
    keep = refs[0]
    given = refs[1 : nz + 1]
    base, state, codes, sign, spare, start, ids, sem = refs[nz + 1 :]
    j = s[2]
    heads, share, _ = start.shape
    rows = pl.ds(pl.multiple_of(s[0] * share, share), share)
    fetch = pltpu.make_async_copy(state.at[pl.ds(s[1] * heads, heads), rows, :], start, sem)
    fetch.start()
    block = given[0].shape[1]
    for r in range(nz):
        ids[lax.bitwise_xor(j, r)] = given[r][...]
    rows = lax.broadcasted_iota(I32, (block, block), 0)
    cols = lax.broadcasted_iota(I32, (block, block), 1)
    strict = one_hot(rows < cols)
    own = base[...] + j * (nz * cap)
    earlier = [jnp.zeros((1, 1), I32) for _ in range(nz)]
    other = jnp.zeros((own_rows, 1), I32)
    taken = jnp.zeros((own_rows, 1), I32)
    place = lax.broadcasted_iota(I32, (16, block), 0)
    for b in range(nz):
        first, second = ids[b, 0:1, :], ids[b, 1:2, :]
        named = ((place == first) | (place == second)) & (place < nz)
        ranks = mm(one_hot(named), strict).astype(I32)
        slots = []
        for e in range(nz):
            hit = (first == e) | (second == e)
            rank = ranks[e : e + 1, :]
            kept = hit & (rank + earlier[e] < keep[e])
            slots.append(jnp.where(kept, (e * nz + b) * cap + rank, -1))
            earlier[e] = earlier[e] + jnp.sum(hit.astype(I32), axis=1, keepdims=True)
        top = functools.reduce(jnp.maximum, slots)
        rest = functools.reduce(jnp.maximum, [jnp.where(c == top, -1, c) for c in slots])
        codes[b, 0:1, :] = top
        codes[b, 1:2, :] = rest
        holds = (own == top) | (own == rest)
        taken = taken + jnp.sum(holds.astype(I32), axis=1, keepdims=True)
        other = other + jnp.sum(jnp.where(holds, first + second, 0), axis=1, keepdims=True)
    every = lax.broadcasted_iota(I32, sign.shape, 1)
    sign[...] = (every == j).astype(F32) - (every == other - j).astype(F32)
    index = lax.broadcasted_iota(I32, (own_rows, 1), 0)
    unused = jnp.min(jnp.where(taken == 0, index, own_rows), axis=0, keepdims=True)
    spare[...] = jnp.broadcast_to((index == unused).astype(F32), spare.shape)
    fetch.wait()


def pack_kernel(away, ny, a, b, out, sem):
    width = out.shape[2]
    share = lax.rem(lax.rem(lax.axis_index("seq"), ny) + away, ny)
    at = pl.ds(pl.multiple_of(share * width, 128), width)
    for c in run_copies([(a.at[:, at], out.at[0]), (b.at[:, at], out.at[1])], sem):
        c.wait()


def update_kernel(nz, ny, heads, hd, s, *refs):
    z, y = s[0], s[1]
    n = ny - 1
    k_arg, v_arg = refs[0], refs[1]
    kv = refs[2 : 2 + n]
    logs = refs[2 + n : 2 + n + ny]
    outs = refs[2 + n + ny : 2 + n + ny + nz]
    c_row, c_col, log_all, state, tail, own, sem = refs[2 + n + ny + nz :]
    tok = k_arg.shape[0]
    total_tok = tok * ny
    share = hd // nz
    mine = pl.ds(pl.multiple_of(y * heads * hd, 128), heads * hd)
    copies = run_copies([(x.at[:, mine], own.at[m]) for m, x in enumerate((k_arg, v_arg))], sem)
    for d in range(ny):
        at = pl.multiple_of(lax.rem(y + ny - d, ny) * tok, tok)
        log_all[:, pl.ds(at, tok)] = logs[d][pl.ds(y * heads, heads), :]
    rows = lax.broadcasted_iota(I32, (total_tok, total_tok), 0)
    cols = lax.broadcasted_iota(I32, (total_tok, total_tok), 1)
    c_row[...] = mm(log_all[...], (rows <= cols).astype(F32), precision=HIGHEST)
    c_col[...] = mm((rows >= cols).astype(F32), log_all[...], NT, precision=HIGHEST)
    total = c_row[:, total_tok - 1 : total_tok]
    for c in copies:
        c.wait()
    for h in range(heads):
        add = None
        for d in range(ny):
            at = pl.multiple_of(lax.rem(y + ny - d, ny) * tok, tok)
            lanes = slice(h * hd, (h + 1) * hd)
            pair = own if d == 0 else kv[d - 1]
            key = pair[0, :, lanes].astype(F32)
            decay = jnp.exp(total[h : h + 1, :] - c_col[pl.ds(at, tok), h : h + 1])
            weighted = (key * sigmoid(key) * decay).astype(BF16)
            part = mm(weighted, pair[1, :, lanes], TN)
            add = part if add is None else add + part
        state[h] = add.astype(BF16)
    tail[...] = jnp.zeros_like(tail)
    hi, mid, lo = pieces(total)
    lane = lax.broadcasted_iota(I32, (heads, hd), 1)
    tail[0:heads, :] = jnp.where(
        lane == 0,
        hi.astype(F32),
        jnp.where(lane == 1, mid.astype(F32), jnp.where(lane == 2, lo.astype(F32), 0.0)),
    )
    for d in range(nz):
        at = pl.multiple_of(lax.rem(z + d, nz) * share, share)
        for h in range(heads):
            outs[d][h * share : (h + 1) * share, :] = state[h, pl.ds(at, share), :]
        outs[d][heads * share :, :] = tail[...].astype(BF16)


def prefix_kernel(nz, heads, hd, s, *refs):
    z = s[0]
    parts = refs[:nz]
    start = refs[nz]
    outs = refs[nz + 1 : 2 * nz + 1]
    final, held, entering, run = refs[2 * nz + 1 :]
    share = hd // nz
    run[...] = start[...]
    for d in range(nz):
        held[lax.rem(z + nz - d, nz)] = parts[d][...]
    for p in range(nz):
        logs = jnp.sum(held[p, heads * share :, :].astype(F32), axis=1, keepdims=True)
        keep = jnp.exp(logs)
        for h in range(heads):
            rows = slice(h * share, (h + 1) * share)
            now = run[h]
            entering[p, rows, :] = now.astype(BF16)
            run[h] = keep[h : h + 1, :] * now + held[p, rows, :].astype(F32)
    final[...] = run[...]
    for d in range(nz):
        outs[d][...] = entering[lax.rem(z + d, nz)]


def attention_kernel(nz, ny, heads, hd, s, *refs):
    z, y = s[0], s[1]
    n = ny - 1
    args = refs[:4]
    kv = refs[4 : 4 + n]
    qg = refs[4 + n : 4 + 2 * n]
    states = refs[4 + 2 * n : 4 + 2 * n + nz]
    c_row, c_col, gain, out, ks, vs, qs, gs, state, sem = refs[4 + 2 * n + nz :]
    tok = args[0].shape[0]
    total_tok = tok * ny
    share = hd // nz
    mine = pl.ds(pl.multiple_of(y * heads * hd, 128), heads * hd)
    moves = []
    for d in range(ny):
        at = pl.ds(pl.multiple_of(lax.rem(y + ny - d, ny) * tok, tok), tok)
        for m, to in enumerate((ks, vs, qs, gs)):
            if d == 0:
                source = args[m].at[:, mine]
            else:
                source = (kv if m < 2 else qg)[d - 1].at[m % 2]
            moves.append((source, to.at[at, :]))
    copies = run_copies(moves, sem)
    for d in range(nz):
        at = pl.ds(pl.multiple_of(lax.rem(z + nz - d, nz) * share, share), share)
        for h in range(heads):
            state[h, at, :] = states[d][h * share : (h + 1) * share, :]
    rows = lax.broadcasted_iota(I32, (total_tok, total_tok), 0)
    cols = lax.broadcasted_iota(I32, (total_tok, total_tok), 1)
    causal = rows >= cols
    for c in copies:
        c.wait()
    for h in range(heads):
        lanes = slice(h * hd, (h + 1) * hd)
        query = qs[:, lanes].astype(F32)
        query = query * sigmoid(query)
        key = ks[:, lanes].astype(F32)
        key = (key * sigmoid(key)).astype(BF16)
        col = c_col[:, h : h + 1]
        gap = jnp.where(causal, col - c_row[h : h + 1, :], 0.0)
        decay = jnp.where(causal, jnp.exp(gap), 0.0)
        scores = mm(query.astype(BF16), key, NT) * decay
        att = mm(scores.astype(BF16), vs[:, lanes])
        att = att + mm((query * jnp.exp(col)).astype(BF16), state[h])
        square = jnp.mean(att * att, axis=1, keepdims=True)
        gate = sigmoid(gs[:, lanes].astype(F32))
        out[:, lanes] = (att * lax.rsqrt(square + EPS) * gain[:, lanes] * gate).astype(BF16)


def project_kernel(nz, ny, cap, dzs, last, s, *refs):
    z, j = s[0], s[2]
    bits = nz.bit_length() - 1
    parts = [len(p) for p in dzs.values()]
    count = sum(parts) * ny
    blocks = refs[:count]
    weights = refs[count : count + ny]
    r_ids, b_ids, codes = refs[count + ny : count + ny + 3]
    refs = refs[count + ny + 3 :]
    if last:
        done, sums, residual = refs[:3]
        keep, send, keep_all, send_all, stacked, own, sem = refs[3:]
    else:
        done, sums, stacked, sem = refs
    rows = stacked.shape[2]
    moves = []
    at = 0
    for dy in range(ny):
        for n, (dz, pieces_of) in enumerate(dzs.items()):
            first = 0
            for _ in pieces_of:
                size = blocks[at].shape[0]
                moves.append((blocks[at], stacked.at[dy, n, pl.ds(first, size)]))
                first += size
                at += 1
    if last:
        moves.append((residual, own))
    copies = run_copies(moves, sem)
    ids = lax.bitwise_xor(r_ids[...], j) * (nz * cap) + b_ids[...]
    pick = lambda b: one_hot((ids == codes[b, 0:1, :]) | (ids == codes[b, 1:2, :]))
    total_rows = sums[...] if last else None
    for c in copies:
        c.wait()
    projected = {}
    for n, dz in enumerate(dzs):
        total = None
        for dy in range(ny):
            part = mm(stacked[dy, n], weights[dy][...])
            total = part if total is None else total + part
        projected[dz] = total.astype(BF16)
        part = mm(pick(lax.rem(z + nz - dz, nz)), projected[dz])
        total_rows = part if total_rows is None else total_rows + part
    if not last:
        for n, dz in enumerate(dzs):
            done[n] = projected[dz]
        sums[...] = total_rows
        return
    total_rows = total_rows + mm(pick(j), own[...])
    half = keep.shape[0]
    keep[...] = total_rows[:half, :]
    send[...] = total_rows[half:, :].astype(BF16)
    before = [dz for dz in range(nz) if dz not in dzs]
    for p in range(nz):
        block = lax.bitwise_xor(jnp.int32(bit_reversed(p, bits)), j)
        away = lax.rem(z + nz - block, nz)
        to = keep_all.at[p] if p < nz // 2 else send_all.at[p - nz // 2]
        for dz in range(nz):

            @pl.when(away == dz)
            def _(dz=dz):
                to[...] = projected[dz] if dz in dzs else done[before.index(dz)]


def diagonal(rows):
    shape = (rows, 128)
    return lax.broadcasted_iota(I32, shape, 0) == lax.broadcasted_iota(I32, shape, 1)


def rows_kernel(s, keep, received, gain, router_t, sign, spare, out):
    width = gain.shape[1]
    rows = keep[...] + received[...].astype(F32)
    square = jnp.sum(rows * rows, axis=1, keepdims=True)
    scaled = rows * gain[...]
    logits = mm(scaled, router_t[...], NT, precision=HIGHEST)
    gap = jnp.sum(logits * sign[...], axis=1, keepdims=True)
    if out.shape[1] == width:
        lines = []
        for value in (square, gap):
            for piece in pieces(value)[:2]:
                spread = jnp.where(diagonal(rows.shape[0]), piece.astype(F32), 0.0)
                lines.append(jnp.sum(spread, axis=0, keepdims=True))
        lines.append(jnp.zeros((1, width - 128 * len(lines)), F32))
        line = jnp.concatenate(lines, axis=1)
        out[...] = jnp.where(spare[:, 0:1] > 0.0, line, scaled).astype(BF16)
        return
    out[:, :width] = scaled.astype(BF16)
    lane = lax.broadcasted_iota(I32, (rows.shape[0], 128), 1)
    stats = jnp.zeros((rows.shape[0], 128), F32)
    for at, value in ((0, square), (3, gap)):
        for k, piece in enumerate(pieces(value)):
            stats = jnp.where(lane == at + k, piece.astype(F32), stats)
    out[:, width:] = stats.astype(BF16)


def source_of(s, nz, ny, place):
    z = lax.rem(s[0] + nz - place[0], nz)
    return z * ny + lax.rem(s[1] + ny - place[1], ny)


def throttled(copies, n, depth):
    if n < 0:
        for c in copies[:depth]:
            c.start()
        return
    copies[n].wait()
    if n + depth < len(copies):
        copies[n + depth].start()


def up_kernel(nz, ny, places, first, last, features, s, *refs):
    count = len(places)
    blocks = refs[:count]
    refs = refs[count:]
    before = () if first else refs[:3]
    refs = refs[0 if first else 3 :]
    weights, spare = refs[:2], refs[2]
    outs, buffers, sem = refs[3:-3], refs[-3:-1], refs[-1]
    slots, width = blocks[0].shape
    is_spare = spare[:, 0:1] > 0.0
    copies = []
    for n, p in enumerate(places):
        lanes = pl.ds(pl.multiple_of(source_of(s, nz, ny, p) * width, 128), width)
        for m in range(2):
            source = weights[m].at[0, :, lanes]
            copies.append(pltpu.make_async_copy(source, buffers[m].at[n], sem.at[len(copies)]))
    throttled(copies, -1, 6)
    gate, up, stats = (None, None, None) if first else (b[...] for b in before)
    for n in range(count):
        rows = blocks[n][...].astype(F32)
        part = jnp.sum(jnp.where(is_spare, rows, 0.0), axis=0, keepdims=True)
        stats = part if stats is None else stats + part
        rows = jnp.where(is_spare, 0.0, rows).astype(BF16)
        throttled(copies, 2 * n, 6)
        part = mm(rows, buffers[0][n], NT)
        gate = part if gate is None else gate + part
        throttled(copies, 2 * n + 1, 6)
        part = mm(rows, buffers[1][n], NT)
        up = part if up is None else up + part
    if not last:
        outs[0][...] = gate
        outs[1][...] = up
        outs[2][...] = stats
        return
    sums = [stats[:, at : at + 128] + stats[:, at + 128 : at + 256] for at in (0, 256)]
    sums = [jnp.where(diagonal(slots), line, 0.0) for line in sums]
    square, gap = [jnp.sum(line, axis=1, keepdims=True) for line in sums]
    inverse = lax.rsqrt(square / features + EPS)
    gate = gate * inverse
    outs[0][...] = (gate * sigmoid(gate) * (up * inverse)).astype(BF16)
    outs[1][...] = jnp.broadcast_to(sigmoid(gap * inverse), outs[1].shape)


def down_kernel(nz, ny, cap, places, ahead, first, last, s, *refs):
    j = s[2]
    count = len(places)
    blocks = refs[:count]
    refs = refs[count:]
    before = None if first else refs[0]
    refs = refs[0 if first else 1 :]
    w_down = refs[0]
    refs = refs[1:]
    depth = blocks[0].shape[1]
    copies = []
    if last:
        weight, out_base, row_base = refs[:3]
        outs, buf = refs[3:], w_down
    else:
        outs = refs[:1]
        kept = refs[1] if ahead else None
        buf, sem = refs[-2:]
        jobs = [(p, buf, n) for n, p in enumerate(places)]
        jobs += [(p, kept, n) for n, p in enumerate(ahead)]
        for p, to, n in jobs:
            at = pl.ds(pl.multiple_of(source_of(s, nz, ny, p) * depth, depth), depth)
            source = w_down.at[0, at, :]
            copies.append(pltpu.make_async_copy(source, to.at[n], sem.at[len(copies)]))
        throttled(copies, -1, 5)
    total = None if first else before[...]
    for n in range(count):
        if not last:
            throttled(copies, n, 5)
        part = mm(blocks[n][...], buf[n])
        total = part if total is None else total + part
    if not last:
        outs[0][...] = total
        for n in range(count, len(copies)):
            throttled(copies, n, 5)
        return
    result = (total * weight[:, 0:1]).astype(BF16)
    for r, out in enumerate(outs):
        wanted = out_base[...] + lax.bitwise_xor(j, r) * cap
        out[...] = mm(one_hot(wanted == row_base[...]), result).astype(BF16)


def stream_kernel(cap, s, keep, received, residual, codes, ret_r, ret_base, out, pick):
    nz = codes.shape[0]
    j = s[2]
    out[...] = residual[...].astype(F32) + (keep[...].astype(F32) + received[...].astype(F32))
    ids = (lax.bitwise_xor(ret_r[...], j) * nz + j) * cap + ret_base[...]
    pick[...] = one_hot((ids == codes[j, 0:1, :]) | (ids == codes[j, 1:2, :]))


def combine_kernel(nz, s, *refs):
    returned = refs[:nz]
    before, pick, out, stacked = refs[nz:]
    rows = returned[0].shape[0]
    for n in range(nz):
        stacked[n * rows : (n + 1) * rows, :] = returned[n][...]
    out[...] = (before[...] + mm(pick[...], stacked[...], TN)).astype(BF16)


def local(
    residual,
    query,
    key_in,
    value_in,
    gate_in,
    log_decay,
    state_in,
    attn_gain,
    w_out,
    moe_gain,
    router,
    w_gate,
    w_up,
    w_down,
    expert_ids,
    keep_counts,
):
    nz = lax.axis_size("exp")
    ny = lax.axis_size("seq") // nz
    bits = nz.bit_length() - 1
    i = lax.axis_index("seq").astype(I32)
    j = lax.axis_index("exp").astype(I32)
    z, y = i // ny, i % ny
    place = jnp.stack([z, y, j])

    tok, head_width = query.shape
    head_count, hd = state_in.shape[0], state_in.shape[2]
    heads = head_count // ny
    width = heads * hd
    block, cols = residual.shape
    features = w_gate.shape[2]
    units = w_gate.shape[1]
    experts = router.shape[1]
    cap = 5 * block * nz // (2 * nz * experts)
    slots = nz * cap

    def z_turn(a, d):
        pairs = [(p * ny + q, (p + d) % nz * ny + q) for p in range(nz) for q in range(ny)]
        return lax.ppermute(a, "seq", pairs)

    def y_turn(a, d):
        pairs = [(p * ny + q, p * ny + (q + d) % ny) for p in range(nz) for q in range(ny)]
        return lax.ppermute(a, "seq", pairs)

    def swap(a, r):
        return lax.ppermute(a, "exp", [(p, p ^ r) for p in range(nz)])

    z_order = sorted(range(1, nz), key=lambda d: (min(d, nz - d), d))
    near = [d for d in z_order if min(d, nz - d) == 1]
    distant = [d for d in z_order if d not in near]
    places = [(dz, dy) for dy in range(ny) for dz in range(nz)]

    def behind(values, events):
        return list(lax.optimization_barrier((tuple(values), tuple(events)))[0])

    def gather_z(a):
        held = {(0, 0): a}
        for d in range(1, ny):
            held[0, d] = y_turn(a, d)
        for d in z_order:
            held[d, 0] = z_turn(a, d)
        return held

    def gather_y(held, events):
        for d in z_order:
            x = held[d, 0]
            if d == z_order[-1] and events:
                x = held[d, 0] = behind([x], events)[0]
            for e in range(1, ny):
                held[d, e] = y_turn(x, e)

    def stages(run, a, groups):
        arrived = gather_z(a)
        state = []
        if len(groups) == 2:
            gather_y(arrived, [])
        for n, group in enumerate(groups):
            blocks = [arrived[p] for p in group]
            state = run(group, blocks, state, n == 0, n == len(groups) - 1)
            if n == 0 and len(groups) == 3:
                gather_y(arrived, state)
        return state

    groups = [[(0, 0)], [(0, d) for d in range(1, ny)] + [(d, 0) for d in z_order]]
    groups.append([(d, e) for d in z_order for e in range(1, ny)])

    slot = np.arange(cap)
    row_r = np.repeat([bit_reversed(p, bits) for p in range(nz)], slots).astype(np.int32)[:, None]
    row_base = np.tile((np.arange(nz)[:, None] * cap + slot).reshape(slots), nz)
    row_base = row_base.astype(np.int32)[:, None]
    own_base = row_base[:slots]
    ret_rows = cap + -cap % 16
    padded = np.where(np.arange(ret_rows) < cap, np.arange(ret_rows), -(10**8)).astype(np.int32)
    ret_r = np.repeat(np.arange(nz), ret_rows).astype(np.int32)[:, None]
    ret_base = np.tile(padded, nz)[:, None]

    logs_t = jnp.transpose(log_decay)
    logs, kvs, qgs = [logs_t], [], []
    for d in range(1, ny):
        pack = pl.pallas_call(
            functools.partial(pack_kernel, d, ny),
            out_shape=sds((2, tok, width), BF16),
            in_specs=[pl.BlockSpec(memory_space=pltpu.HBM)] * 2,
            out_specs=pl.BlockSpec(memory_space=pltpu.VMEM),
            scratch_shapes=[pltpu.SemaphoreType.DMA((2,))],
            compiler_params=pltpu.CompilerParams(vmem_limit_bytes=60 * 1024 * 1024),
        )
        kvs.append(y_turn(pack(key_in, value_in), d))
        logs.append(y_turn(logs_t, d))
        qgs.append(pack(query, gate_in))
    ids = jnp.transpose(expert_ids)
    share = hd // nz
    codes, sign, spare, start = call(
        functools.partial(routing_kernel, nz, cap, slots),
        place,
        [(keep_counts, pl.BlockSpec(memory_space=pltpu.SMEM))]
        + [ids]
        + [swap(ids, r) for r in range(1, nz)]
        + [own_base, hbm(state_in)],
        [
            sds((nz, 2, block), I32),
            sds((slots, experts), F32),
            sds((slots, 128), F32),
            sds((heads, share, hd), F32),
        ],
        [pltpu.VMEM((nz, 2, block), I32), pltpu.SemaphoreType.DMA],
    )
    attn_gain_2, moe_gain_2, router_t = attn_gain[None], moe_gain[None], jnp.transpose(router)
    prepared = [codes, sign, spare, start, attn_gain_2, moe_gain_2]
    qgs = [y_turn(qg, d + 1) for d, qg in enumerate(behind(qgs, kvs + logs + prepared))]
    share = hd // nz
    long = tok * ny
    *parts, c_row, c_col = call(
        functools.partial(update_kernel, nz, ny, heads, hd),
        place,
        [hbm(key_in), hbm(value_in), *kvs, *logs],
        [sds((heads * share + 16, hd), BF16)] * nz
        + [sds((heads, long), F32), sds((long, heads), F32)],
        [
            pltpu.VMEM((heads, long), F32),
            pltpu.VMEM((heads, hd, hd), BF16),
            pltpu.VMEM((16, hd), F32),
            pltpu.VMEM((2, tok, width), BF16),
            pltpu.SemaphoreType.DMA((2,)),
        ],
        limit=40,
            flops=2 * long * hd * hd * heads,
    )
    parts = [parts[0]] + [z_turn(parts[d], d) for d in range(1, nz)]
    *entering, last_rows = call(
        functools.partial(prefix_kernel, nz, heads, hd),
        place,
        [*parts, start],
        [sds((heads * share, hd), BF16)] * nz + [sds((heads, share, hd), F32)],
        [
            pltpu.VMEM((nz, heads * share + 16, hd), BF16),
            pltpu.VMEM((nz, heads * share, hd), BF16),
            pltpu.VMEM((heads, share, hd), F32),
        ],
    )
    entering = [entering[0]] + [z_turn(entering[d], d) for d in range(1, nz)]
    (mixed,) = call(
        functools.partial(attention_kernel, nz, ny, heads, hd),
        place,
        [
            hbm(key_in),
            hbm(value_in),
            hbm(query),
            hbm(gate_in),
            *[anywhere(x) for x in kvs],
            *[anywhere(x) for x in qgs],
            *entering,
            c_row,
            c_col,
            (attn_gain_2, pl.BlockSpec((1, width), lambda n, s: (0, s[1]))),
        ],
        [sds((long, width), BF16)],
        [pltpu.VMEM((long, width), BF16)] * 4
        + [pltpu.VMEM((heads, hd, hd), BF16), pltpu.SemaphoreType.DMA((4 * ny,))],
        limit=40,
            flops=4 * long * long * width,
    )

    def across(blocks):
        return [[y_turn(x, e) for x in blocks] for e in range(1, ny)]

    held = {0: [[mixed]] + across([mixed])}
    for d in near:
        held[d] = [[z_turn(mixed, d)]]
    free = behind([mixed], [held[near[0]][0][0]])[0]
    for d in near:
        held[d] += across(held[d][0])
    halves = [free[: long // 2], free[long // 2 :]]
    for d in distant:
        held[d] = [[z_turn(x, d) for x in halves]]
    for d in distant:
        held[d] += across(held[d][0])
    w_parts = [
        (w_out, pl.BlockSpec((width, cols), lambda n, s, d=d: (lax.rem(s[1] + ny - d, ny), 0)))
        for d in range(ny)
    ]
    given = []
    for group in ([0] + near, distant):
        last = group is distant
        dzs = {d: held[d][0] for d in group}
        blocks = [x for dy in range(ny) for d in group for x in held[d][dy]]
        half = nz * slots // 2
        outs = [sds((len(group), block, cols), BF16), sds((nz * slots, cols), F32)]
        if last:
            outs = [sds((half, cols), F32), sds((half, cols), BF16)]
            outs += [sds((nz // 2, block, cols), BF16)] * 2
        given = call(
            functools.partial(project_kernel, nz, ny, cap, dzs, last),
            place,
            [anywhere(x) for x in blocks]
            + w_parts
            + [row_r, row_base, codes]
            + list(given)
            + ([hbm(residual)] if last else []),
            outs,
            [pltpu.VMEM((ny, len(group), long, width), BF16)]
            + ([pltpu.VMEM((block, cols), BF16)] if last else [])
            + [pltpu.SemaphoreType.DMA((len(blocks) + 1,))],
            limit=40,
            flops=2 * len(group) * long * head_width * cols,
        )
    keep, send, keep_all, send_all = given
    for b in range(bits):
        received = swap(send, 1 << b)
        if b < bits - 1:
            part = keep.shape[0] // 2
            send = (keep[part:] + received[part:].astype(F32)).astype(BF16)
            keep = keep[:part] + received[:part].astype(F32)
    fits = cols % 128 == 0 and cols >= 512 and slots <= 128
    (rows_out,) = call(
        rows_kernel,
        place,
        [keep, received, moe_gain_2, router_t, sign, spare],
        [sds((slots, cols if fits else cols + 128), BF16)],
    )
    send_all = behind([send_all], [rows_out])[0]
    for b in range(bits):
        received_all = swap(send_all, 1 << b)
        if b < bits - 1:
            n = keep_all.shape[0] // 2
            both = keep_all.astype(F32) + received_all.astype(F32)
            send_all, keep_all = both[n:].astype(BF16), both[:n].astype(BF16)
    rows = share // ny
    last_rows = behind([last_rows], [rows_out])[0]
    final_rows = jnp.zeros((head_count, rows, hd), F32)
    for d in range(ny):
        sent = lax.dynamic_slice_in_dim(last_rows, (y + d) % ny * rows, rows, 1)
        got = sent if d == 0 else y_turn(sent, d)
        final_rows = lax.dynamic_update_slice_in_dim(
            final_rows, got, (y - d) % ny * heads, 0
        )

    in_vmem = pl.BlockSpec(memory_space=pltpu.VMEM)

    def up(group, blocks, state, first, last):
        outs = [sds((slots, units), F32)] * 2 + [sds((1, cols), F32)]
        if last:
            outs = [sds((slots, units), BF16), sds((slots, 128), F32)]
        return call(
            functools.partial(up_kernel, nz, ny, group, first, last, features),
            place,
            blocks + list(state) + [anywhere(w_gate), anywhere(w_up), spare],
            outs,
            [pltpu.VMEM((len(group), units, cols), BF16)] * 2
            + [pltpu.SemaphoreType.DMA((2 * len(group),))],
            limit=40,
            flops=4 * len(group) * slots * units * cols,
        )

    def down(group, blocks, state, first, last):
        ahead = groups[-1] if first else []
        outs = [sds((slots, cols), F32)]
        outs += [sds((len(ahead), units, cols), BF16)] if ahead else []
        weights = [anywhere(w_down)]
        if last:
            outs = [sds((ret_rows, cols), BF16)] * nz
            weights = [(fetched["down"], in_vmem), weight, padded[:, None], own_base.T]
        state = call(
            functools.partial(down_kernel, nz, ny, cap, group, ahead, first, last),
            place,
            blocks + list(state) + weights,
            outs,
            []
            if last
            else [
                pltpu.VMEM((len(group), units, cols), BF16),
                pltpu.SemaphoreType.DMA((len(group) + len(ahead),)),
            ],
            limit=40,
            flops=2 * len(group) * slots * units * cols,
            held=1 if ahead else 0,
        )
        if ahead:
            fetched["down"] = state[1]
        return state if last else state[:1]

    fetched = {}
    if not fits:
        arrived = gather_z(rows_out)
        gather_y(arrived, [])
        order = jnp.stack([(z - dz) % nz * ny + (y - dy) % ny for dz, dy in places])
        at = jnp.argsort(order)
        rows_all = jnp.take(jnp.stack([arrived[p] for p in places]), at, axis=0)
        stats = jnp.sum(rows_all[:, :, cols:].astype(F32), axis=0)
        rows_all = jnp.swapaxes(rows_all[:, :, :cols], 0, 1).reshape(slots, features)
        inverse = lax.rsqrt(jnp.sum(stats[:, :3], axis=1) / features + EPS)[:, None]
        gate = mm(rows_all, w_gate[0], NT) * inverse
        hidden = (gate * sigmoid(gate) * (mm(rows_all, w_up[0], NT) * inverse)).astype(BF16)
        weight = sigmoid(jnp.sum(stats[:, 3:6], axis=1)[:, None] * inverse)
        weight = jnp.broadcast_to(weight, (slots, 128))
    else:
        hidden, weight = stages(up, rows_out, groups)
    state = stages(down, hidden, [groups[0] + groups[1], groups[2]])
    stream, picks = call(
        functools.partial(stream_kernel, cap),
        place,
        [keep_all[0], received_all[0], residual, codes, ret_r, ret_base],
        [sds((block, cols), F32), sds((nz * ret_rows, block), BF16)],
    )
    returned = [state[0]] + [swap(state[r], r) for r in range(1, nz)]
    (layer_out,) = call(
        functools.partial(combine_kernel, nz),
        place,
        returned + [stream, picks],
        [sds((block, cols), BF16)],
        [pltpu.VMEM((nz * ret_rows, cols), BF16)],
    )
    return layer_out, final_rows


def solution(mesh):
    in_specs = (
        P("exp", "seq"),
        P("seq", "exp"),
        P("seq", "exp"),
        P("seq", "exp"),
        P("seq", "exp"),
        P("seq", "exp"),
        P("exp", None, None),
        P("exp"),
        P("exp", "seq"),
        P("seq"),
        P("seq", None),
        P("exp", "seq", None),
        P("exp", "seq", None),
        P("exp", None, "seq"),
        P("exp", None),
        P(),
    )
    out_specs = (P("exp", "seq"), P("exp", "seq", None))
    return jax.shard_map(local, mesh=mesh, in_specs=in_specs, out_specs=out_specs, check_vma=False)
```

```python
import functools
import jax
import jax.numpy as jnp
import numpy as np
from jax import lax
from jax.experimental import pallas as pl
from jax.experimental.pallas import tpu as pltpu
from jax.sharding import PartitionSpec as P

EPS = 1e-05
F32 = jnp.float32
BF16 = jnp.bfloat16
I32 = jnp.int32
HIGHEST = lax.Precision.HIGHEST
NT = (((1,), (1,)), ((), ()))
TN = (((0,), (0,)), ((), ()))
NN = (((1,), (0,)), ((), ()))


def mm(a, b, dims=NN, precision=None):
    return lax.dot_general(a, b, dims, precision=precision, preferred_element_type=F32)


def sigmoid(v):
    return 1.0 / (1.0 + jnp.exp(-v))


def bit_reversed(p, bits):
    r = 0
    for b in range(bits):
        r = r * 2 + ((p >> b) & 1)
    return r


def whole(shape):
    return pl.BlockSpec(tuple(shape), lambda i, s: (0,) * len(shape))


def call(kernel, place, operands, outs, scratch=(), flops=0, limit=40, held=0):
    arrays, specs, moved = [], [], 0
    for item in operands:
        array, spec = item if isinstance(item, tuple) else (item, whole(item.shape))
        arrays.append(array)
        specs.append(spec)
        moved += array.size * array.dtype.itemsize
    moved += sum(o.size * o.dtype.itemsize for o in outs)
    return pl.pallas_call(
        kernel,
        out_shape=list(outs),
        grid_spec=pltpu.PrefetchScalarGridSpec(
            num_scalar_prefetch=1,
            grid=(1,),
            in_specs=specs,
            out_specs=[
                pl.BlockSpec(memory_space=pltpu.VMEM) if n >= len(outs) - held else whole(o.shape)
                for n, o in enumerate(outs)
            ],
            scratch_shapes=list(scratch),
        ),
        compiler_params=pltpu.CompilerParams(vmem_limit_bytes=limit * 1024 * 1024),
        cost_estimate=pl.CostEstimate(flops=flops, bytes_accessed=moved, transcendentals=0),
    )(place, *arrays)


def hbm(array):
    return (array, pl.BlockSpec(memory_space=pltpu.HBM))


def anywhere(array):
    return (array, pl.BlockSpec(memory_space=pl.ANY))


def run_copies(pairs, sem):
    copies = [pltpu.make_async_copy(a, b, sem.at[n]) for n, (a, b) in enumerate(pairs)]
    for c in copies:
        c.start()
    return copies


CUTS = 4


def cut_rows(pairs):
    cut = []
    for a, b in pairs:
        rows = a.shape[0] // CUTS
        cut += [(a.at[pl.ds(n * rows, rows)], b.at[pl.ds(n * rows, rows)]) for n in range(CUTS)]
    return cut


def one_hot(mask):
    return mask.astype(F32).astype(BF16)


def turned_back(z, back, nz):
    return jnp.where(z < back, z - back + nz, z - back)


def sds(shape, dtype):
    return jax.ShapeDtypeStruct(tuple(shape), dtype)


def pieces(x):
    hi = x.astype(BF16)
    rest = x - hi.astype(F32)
    mid = rest.astype(BF16)
    return hi, mid, (rest - mid.astype(F32)).astype(BF16)


def routing_kernel(nz, cap, own_rows, s, *refs):
    keep = refs[0]
    given = refs[1 : nz + 1]
    base, state, codes, sign, spare, start, ids, sem = refs[nz + 1 :]
    j = s[2]
    heads, share, _ = start.shape
    rows = pl.ds(pl.multiple_of(s[0] * share, share), share)
    fetch = pltpu.make_async_copy(state.at[pl.ds(s[1] * heads, heads), rows, :], start, sem)
    fetch.start()
    block = given[0].shape[1]
    for r in range(nz):
        ids[lax.bitwise_xor(j, r)] = given[r][...]
    rows = lax.broadcasted_iota(I32, (block, block), 0)
    cols = lax.broadcasted_iota(I32, (block, block), 1)
    strict = one_hot(rows < cols)
    own = base[...] + j * (nz * cap)
    earlier = [jnp.zeros((1, 1), I32) for _ in range(nz)]
    other = jnp.zeros((own_rows, 1), I32)
    taken = jnp.zeros((own_rows, 1), I32)
    place = lax.broadcasted_iota(I32, (16, block), 0)
    for b in range(nz):
        first, second = ids[b, 0:1, :], ids[b, 1:2, :]
        named = ((place == first) | (place == second)) & (place < nz)
        ranks = mm(one_hot(named), strict).astype(I32)
        slots = []
        for e in range(nz):
            hit = (first == e) | (second == e)
            rank = ranks[e : e + 1, :]
            kept = hit & (rank + earlier[e] < keep[e])
            slots.append(jnp.where(kept, (e * nz + b) * cap + rank, -1))
            earlier[e] = earlier[e] + jnp.sum(hit.astype(I32), axis=1, keepdims=True)
        top = functools.reduce(jnp.maximum, slots)
        rest = functools.reduce(jnp.maximum, [jnp.where(c == top, -1, c) for c in slots])
        codes[b, 0:1, :] = top
        codes[b, 1:2, :] = rest
        holds = (own == top) | (own == rest)
        taken = taken + jnp.sum(holds.astype(I32), axis=1, keepdims=True)
        other = other + jnp.sum(jnp.where(holds, first + second, 0), axis=1, keepdims=True)
    every = lax.broadcasted_iota(I32, sign.shape, 1)
    sign[...] = (every == j).astype(F32) - (every == other - j).astype(F32)
    index = lax.broadcasted_iota(I32, (own_rows, 1), 0)
    unused = jnp.min(jnp.where(taken == 0, index, own_rows), axis=0, keepdims=True)
    spare[...] = jnp.broadcast_to((index == unused).astype(F32), spare.shape)
    fetch.wait()


def pack_kernel(away, ny, a, b, out, sem):
    width = out.shape[2]
    share = lax.rem(lax.rem(lax.axis_index("seq"), ny) + away, ny)
    at = pl.ds(pl.multiple_of(share * width, 128), width)
    for c in run_copies(cut_rows([(a.at[:, at], out.at[0]), (b.at[:, at], out.at[1])]), sem):
        c.wait()


def update_kernel(nz, ny, heads, hd, s, *refs):
    z, y = s[0], s[1]
    n = ny - 1
    k_arg, v_arg = refs[0], refs[1]
    kv = refs[2 : 2 + n]
    logs = refs[2 + n : 2 + n + ny]
    outs = refs[2 + n + ny : 2 + n + ny + nz]
    c_row, c_col, log_all, state, tail, own, sem = refs[2 + n + ny + nz :]
    tok = k_arg.shape[0]
    total_tok = tok * ny
    share = hd // nz
    mine = pl.ds(pl.multiple_of(y * heads * hd, 128), heads * hd)
    pairs = [(x.at[:, mine], own.at[m]) for m, x in enumerate((k_arg, v_arg))]
    copies = run_copies(cut_rows(pairs), sem)
    for d in range(ny):
        at = pl.multiple_of(lax.rem(y + ny - d, ny) * tok, tok)
        log_all[:, pl.ds(at, tok)] = logs[d][pl.ds(y * heads, heads), :]
    rows = lax.broadcasted_iota(I32, (total_tok, total_tok), 0)
    cols = lax.broadcasted_iota(I32, (total_tok, total_tok), 1)
    c_row[...] = mm(log_all[...], (rows <= cols).astype(F32), precision=HIGHEST)
    c_col[...] = mm((rows >= cols).astype(F32), log_all[...], NT, precision=HIGHEST)
    total = c_row[:, total_tok - 1 : total_tok]
    for c in copies:
        c.wait()
    for h in range(heads):
        add = None
        for d in range(ny):
            at = pl.multiple_of(lax.rem(y + ny - d, ny) * tok, tok)
            lanes = slice(h * hd, (h + 1) * hd)
            pair = own if d == 0 else kv[d - 1]
            key = pair[0, :, lanes].astype(F32)
            decay = jnp.exp(total[h : h + 1, :] - c_col[pl.ds(at, tok), h : h + 1])
            weighted = (key * sigmoid(key) * decay).astype(BF16)
            part = mm(weighted, pair[1, :, lanes], TN)
            add = part if add is None else add + part
        state[h] = add.astype(BF16)
    tail[...] = jnp.zeros_like(tail)
    hi, mid, lo = pieces(total)
    lane = lax.broadcasted_iota(I32, (heads, hd), 1)
    tail[0:heads, :] = jnp.where(
        lane == 0,
        hi.astype(F32),
        jnp.where(lane == 1, mid.astype(F32), jnp.where(lane == 2, lo.astype(F32), 0.0)),
    )
    for d in range(nz):
        at = pl.multiple_of(lax.rem(z + d, nz) * share, share)
        for h in range(heads):
            outs[d][h * share : (h + 1) * share, :] = state[h, pl.ds(at, share), :]
        outs[d][heads * share :, :] = tail[...].astype(BF16)


def prefix_kernel(nz, heads, hd, s, *refs):
    z = s[0]
    parts = refs[:nz]
    start = refs[nz]
    outs = refs[nz + 1 : 2 * nz + 1]
    final, held, entering, run = refs[2 * nz + 1 :]
    share = hd // nz
    run[...] = start[...]
    for d in range(nz):
        held[lax.rem(z + nz - d, nz)] = parts[d][...]
    for p in range(nz):
        logs = jnp.sum(held[p, heads * share :, :].astype(F32), axis=1, keepdims=True)
        keep = jnp.exp(logs)
        for h in range(heads):
            rows = slice(h * share, (h + 1) * share)
            now = run[h]
            entering[p, rows, :] = now.astype(BF16)
            run[h] = keep[h : h + 1, :] * now + held[p, rows, :].astype(F32)
    final[...] = run[...]
    for d in range(nz):
        outs[d][...] = entering[lax.rem(z + d, nz)]


def attention_kernel(nz, ny, heads, hd, s, *refs):
    z, y = s[0], s[1]
    n = ny - 1
    args = refs[:4]
    kv = refs[4 : 4 + n]
    qg = refs[4 + n : 4 + 2 * n]
    states = refs[4 + 2 * n : 4 + 2 * n + nz]
    c_row, c_col, gain, out, ks, vs, qs, gs, state, sem = refs[4 + 2 * n + nz :]
    tok = args[0].shape[0]
    total_tok = tok * ny
    share = hd // nz
    mine = pl.ds(pl.multiple_of(y * heads * hd, 128), heads * hd)
    moves = []
    for d in range(ny):
        at = pl.ds(pl.multiple_of(lax.rem(y + ny - d, ny) * tok, tok), tok)
        for m, to in enumerate((ks, vs, qs, gs)):
            if d == 0:
                source = args[m].at[:, mine]
            else:
                source = (kv if m < 2 else qg)[d - 1].at[m % 2]
            moves.append((source, to.at[at, :]))
    copies = run_copies(moves, sem)
    for d in range(nz):
        at = pl.ds(pl.multiple_of(lax.rem(z + nz - d, nz) * share, share), share)
        for h in range(heads):
            state[h, at, :] = states[d][h * share : (h + 1) * share, :]
    rows = lax.broadcasted_iota(I32, (total_tok, total_tok), 0)
    cols = lax.broadcasted_iota(I32, (total_tok, total_tok), 1)
    causal = rows >= cols
    for c in copies:
        c.wait()
    for h in range(heads):
        lanes = slice(h * hd, (h + 1) * hd)
        query = qs[:, lanes].astype(F32)
        query = query * sigmoid(query)
        key = ks[:, lanes].astype(F32)
        key = (key * sigmoid(key)).astype(BF16)
        col = c_col[:, h : h + 1]
        gap = jnp.where(causal, col - c_row[h : h + 1, :], 0.0)
        decay = jnp.where(causal, jnp.exp(gap), 0.0)
        scores = mm(query.astype(BF16), key, NT) * decay
        att = mm(scores.astype(BF16), vs[:, lanes])
        att = att + mm((query * jnp.exp(col)).astype(BF16), state[h])
        square = jnp.mean(att * att, axis=1, keepdims=True)
        gate = sigmoid(gs[:, lanes].astype(F32))
        out[:, lanes] = (att * lax.rsqrt(square + EPS) * gain[:, lanes] * gate).astype(BF16)


def project_kernel(nz, ny, cap, dzs, last, s, *refs):
    z, j = s[0], s[2]
    bits = nz.bit_length() - 1
    parts = [len(p) for p in dzs.values()]
    count = sum(parts) * ny
    blocks = refs[:count]
    weights = refs[count : count + ny]
    r_ids, b_ids, codes = refs[count + ny : count + ny + 3]
    refs = refs[count + ny + 3 :]
    if last:
        done, sums, residual = refs[:3]
        keep, send, keep_all, send_all, stacked, own, sem = refs[3:]
    else:
        done, sums, stacked, sem = refs
    rows = stacked.shape[2]
    moves = []
    at = 0
    for dy in range(ny):
        for n, (dz, pieces_of) in enumerate(dzs.items()):
            first = 0
            for _ in pieces_of:
                size = blocks[at].shape[0]
                moves.append((blocks[at], stacked.at[dy, n, pl.ds(first, size)]))
                first += size
                at += 1
    if last:
        moves.append((residual, own))
    copies = run_copies(moves, sem)
    ids = lax.bitwise_xor(r_ids[...], j) * (nz * cap) + b_ids[...]
    pick = lambda b: one_hot((ids == codes[b, 0:1, :]) | (ids == codes[b, 1:2, :]))
    total_rows = sums[...] if last else None
    for c in copies:
        c.wait()
    projected = {}
    for n, dz in enumerate(dzs):
        total = None
        for dy in range(ny):
            part = mm(stacked[dy, n], weights[dy][...])
            total = part if total is None else total + part
        projected[dz] = total.astype(BF16)
        part = mm(pick(lax.rem(z + nz - dz, nz)), projected[dz])
        total_rows = part if total_rows is None else total_rows + part
    if not last:
        for n, dz in enumerate(dzs):
            done[n] = projected[dz]
        sums[...] = total_rows
        return
    total_rows = total_rows + mm(pick(j), own[...])
    half = keep.shape[0]
    keep[...] = total_rows[:half, :]
    send[...] = total_rows[half:, :].astype(BF16)
    before = [dz for dz in range(nz) if dz not in dzs]
    for p in range(nz):
        block = lax.bitwise_xor(jnp.int32(bit_reversed(p, bits)), j)
        away = lax.rem(z + nz - block, nz)
        to = keep_all.at[p] if p < nz // 2 else send_all.at[p - nz // 2]
        for dz in range(nz):

            @pl.when(away == dz)
            def _(dz=dz):
                to[...] = projected[dz] if dz in dzs else done[before.index(dz)]


def diagonal(rows):
    shape = (rows, 128)
    return lax.broadcasted_iota(I32, shape, 0) == lax.broadcasted_iota(I32, shape, 1)


def rows_kernel(s, keep, received, gain, router_t, sign, spare, out):
    width = gain.shape[1]
    rows = keep[...] + received[...].astype(F32)
    square = jnp.sum(rows * rows, axis=1, keepdims=True)
    scaled = rows * gain[...]
    logits = mm(scaled, router_t[...], NT, precision=HIGHEST)
    gap = jnp.sum(logits * sign[...], axis=1, keepdims=True)
    if out.shape[1] == width:
        lines = []
        for value in (square, gap):
            for piece in pieces(value)[:2]:
                spread = jnp.where(diagonal(rows.shape[0]), piece.astype(F32), 0.0)
                lines.append(jnp.sum(spread, axis=0, keepdims=True))
        lines.append(jnp.zeros((1, width - 128 * len(lines)), F32))
        line = jnp.concatenate(lines, axis=1)
        out[...] = jnp.where(spare[:, 0:1] > 0.0, line, scaled).astype(BF16)
        return
    out[:, :width] = scaled.astype(BF16)
    lane = lax.broadcasted_iota(I32, (rows.shape[0], 128), 1)
    stats = jnp.zeros((rows.shape[0], 128), F32)
    for at, value in ((0, square), (3, gap)):
        for k, piece in enumerate(pieces(value)):
            stats = jnp.where(lane == at + k, piece.astype(F32), stats)
    out[:, width:] = stats.astype(BF16)


def source_of(s, nz, ny, place):
    z = lax.rem(s[0] + nz - place[0], nz)
    return z * ny + lax.rem(s[1] + ny - place[1], ny)


def throttled(copies, n, depth):
    if n < 0:
        for c in copies[:depth]:
            c.start()
        return
    copies[n].wait()
    if n + depth < len(copies):
        copies[n + depth].start()


def up_kernel(nz, ny, places, first, last, features, s, *refs):
    count = len(places)
    blocks = refs[:count]
    refs = refs[count:]
    before = () if first else refs[:3]
    refs = refs[0 if first else 3 :]
    weights, spare = refs[:2], refs[2]
    outs, buffers, sem = refs[3:-3], refs[-3:-1], refs[-1]
    slots, width = blocks[0].shape
    is_spare = spare[:, 0:1] > 0.0
    copies = []
    for n, p in enumerate(places):
        lanes = pl.ds(pl.multiple_of(source_of(s, nz, ny, p) * width, 128), width)
        for m in range(2):
            source = weights[m].at[0, :, lanes]
            copies.append(pltpu.make_async_copy(source, buffers[m].at[n], sem.at[len(copies)]))
    throttled(copies, -1, 6)
    gate, up, stats = (None, None, None) if first else (b[...] for b in before)
    for n in range(count):
        rows = blocks[n][...].astype(F32)
        part = jnp.sum(jnp.where(is_spare, rows, 0.0), axis=0, keepdims=True)
        stats = part if stats is None else stats + part
        rows = jnp.where(is_spare, 0.0, rows).astype(BF16)
        throttled(copies, 2 * n, 6)
        part = mm(rows, buffers[0][n], NT)
        gate = part if gate is None else gate + part
        throttled(copies, 2 * n + 1, 6)
        part = mm(rows, buffers[1][n], NT)
        up = part if up is None else up + part
    if not last:
        outs[0][...] = gate
        outs[1][...] = up
        outs[2][...] = stats
        return
    sums = [stats[:, at : at + 128] + stats[:, at + 128 : at + 256] for at in (0, 256)]
    sums = [jnp.where(diagonal(slots), line, 0.0) for line in sums]
    square, gap = [jnp.sum(line, axis=1, keepdims=True) for line in sums]
    inverse = lax.rsqrt(square / features + EPS)
    gate = gate * inverse
    outs[0][...] = (gate * sigmoid(gate) * (up * inverse)).astype(BF16)
    outs[1][...] = jnp.broadcast_to(sigmoid(gap * inverse), outs[1].shape)


def down_kernel(nz, ny, cap, places, ahead, first, last, s, *refs):
    j = s[2]
    count = len(places)
    blocks = refs[:count]
    refs = refs[count:]
    before = None if first else refs[0]
    refs = refs[0 if first else 1 :]
    w_down = refs[0]
    refs = refs[1:]
    depth = blocks[0].shape[1]
    copies = []
    if last:
        weight, out_base, row_base = refs[:3]
        outs, buf = refs[3:], w_down
    else:
        outs = refs[:1]
        kept = refs[1] if ahead else None
        buf, sem = refs[-2:]
        jobs = [(p, buf, n) for n, p in enumerate(places)]
        jobs += [(p, kept, n) for n, p in enumerate(ahead)]
        for p, to, n in jobs:
            at = pl.ds(pl.multiple_of(source_of(s, nz, ny, p) * depth, depth), depth)
            source = w_down.at[0, at, :]
            copies.append(pltpu.make_async_copy(source, to.at[n], sem.at[len(copies)]))
        throttled(copies, -1, 5)
    total = None if first else before[...]
    for n in range(count):
        if not last:
            throttled(copies, n, 5)
        part = mm(blocks[n][...], buf[n])
        total = part if total is None else total + part
    if not last:
        outs[0][...] = total
        for n in range(count, len(copies)):
            throttled(copies, n, 5)
        return
    result = (total * weight[:, 0:1]).astype(BF16)
    for r, out in enumerate(outs):
        wanted = out_base[...] + lax.bitwise_xor(j, r) * cap
        out[...] = mm(one_hot(wanted == row_base[...]), result).astype(BF16)


def stream_kernel(cap, s, keep, received, residual, codes, ret_r, ret_base, out, pick):
    nz = codes.shape[0]
    j = s[2]
    out[...] = residual[...].astype(F32) + (keep[...].astype(F32) + received[...].astype(F32))
    ids = (lax.bitwise_xor(ret_r[...], j) * nz + j) * cap + ret_base[...]
    pick[...] = one_hot((ids == codes[j, 0:1, :]) | (ids == codes[j, 1:2, :]))


def combine_kernel(nz, s, *refs):
    returned = refs[:nz]
    before, pick, out, stacked = refs[nz:]
    rows = returned[0].shape[0]
    for n in range(nz):
        stacked[n * rows : (n + 1) * rows, :] = returned[n][...]
    out[...] = (before[...] + mm(pick[...], stacked[...], TN)).astype(BF16)


def local(
    residual,
    query,
    key_in,
    value_in,
    gate_in,
    log_decay,
    state_in,
    attn_gain,
    w_out,
    moe_gain,
    router,
    w_gate,
    w_up,
    w_down,
    expert_ids,
    keep_counts,
):
    nz = lax.axis_size("exp")
    ny = lax.axis_size("seq") // nz
    bits = nz.bit_length() - 1
    i = lax.axis_index("seq").astype(I32)
    j = lax.axis_index("exp").astype(I32)
    z, y = i // ny, i % ny
    place = jnp.stack([z, y, j])

    tok, head_width = query.shape
    head_count, hd = state_in.shape[0], state_in.shape[2]
    heads = head_count // ny
    width = heads * hd
    block, cols = residual.shape
    features = w_gate.shape[2]
    units = w_gate.shape[1]
    experts = router.shape[1]
    cap = 5 * block * nz // (2 * nz * experts)
    slots = nz * cap

    def z_turn(a, d):
        pairs = [(p * ny + q, (p + d) % nz * ny + q) for p in range(nz) for q in range(ny)]
        return lax.ppermute(a, "seq", pairs)

    def y_turn(a, d):
        pairs = [(p * ny + q, p * ny + (q + d) % ny) for p in range(nz) for q in range(ny)]
        return lax.ppermute(a, "seq", pairs)

    def swap(a, r):
        return lax.ppermute(a, "exp", [(p, p ^ r) for p in range(nz)])

    z_order = sorted(range(1, nz), key=lambda d: (min(d, nz - d), d))
    near = [d for d in z_order if min(d, nz - d) == 1]
    distant = [d for d in z_order if d not in near]
    places = [(dz, dy) for dy in range(ny) for dz in range(nz)]

    def behind(values, events):
        return list(lax.optimization_barrier((tuple(values), tuple(events)))[0])

    def gather_z(a):
        held = {(0, 0): a}
        for d in range(1, ny):
            held[0, d] = y_turn(a, d)
        for d in z_order:
            held[d, 0] = z_turn(a, d)
        return held

    def gather_y(held, events):
        for d in z_order:
            x = held[d, 0]
            if d == z_order[-1] and events:
                x = held[d, 0] = behind([x], events)[0]
            for e in range(1, ny):
                held[d, e] = y_turn(x, e)

    def stages(run, a, groups):
        arrived = gather_z(a)
        state = []
        if len(groups) == 2:
            gather_y(arrived, [])
        for n, group in enumerate(groups):
            blocks = [arrived[p] for p in group]
            state = run(group, blocks, state, n == 0, n == len(groups) - 1)
            if n == 0 and len(groups) == 3:
                gather_y(arrived, state)
        return state

    groups = [[(0, 0)], [(0, d) for d in range(1, ny)] + [(d, 0) for d in z_order]]
    groups.append([(d, e) for d in z_order for e in range(1, ny)])

    slot = np.arange(cap)
    row_r = np.repeat([bit_reversed(p, bits) for p in range(nz)], slots).astype(np.int32)[:, None]
    row_base = np.tile((np.arange(nz)[:, None] * cap + slot).reshape(slots), nz)
    row_base = row_base.astype(np.int32)[:, None]
    own_base = row_base[:slots]
    ret_rows = cap + -cap % 16
    padded = np.where(np.arange(ret_rows) < cap, np.arange(ret_rows), -(10**8)).astype(np.int32)
    ret_r = np.repeat(np.arange(nz), ret_rows).astype(np.int32)[:, None]
    ret_base = np.tile(padded, nz)[:, None]

    logs_t = jnp.transpose(log_decay)
    logs, kvs, qgs = [logs_t], [], []
    for d in range(1, ny):
        pack = pl.pallas_call(
            functools.partial(pack_kernel, d, ny),
            out_shape=sds((2, tok, width), BF16),
            in_specs=[pl.BlockSpec(memory_space=pltpu.HBM)] * 2,
            out_specs=pl.BlockSpec(memory_space=pltpu.VMEM),
            scratch_shapes=[pltpu.SemaphoreType.DMA((2 * CUTS,))],
            compiler_params=pltpu.CompilerParams(vmem_limit_bytes=60 * 1024 * 1024),
        )
        kvs.append(y_turn(pack(key_in, value_in), d))
        logs.append(y_turn(logs_t, d))
        qgs.append(pack(query, gate_in))
    ids = jnp.transpose(expert_ids)
    share = hd // nz
    codes, sign, spare, start = call(
        functools.partial(routing_kernel, nz, cap, slots),
        place,
        [(keep_counts, pl.BlockSpec(memory_space=pltpu.SMEM))]
        + [ids]
        + [swap(ids, r) for r in range(1, nz)]
        + [own_base, hbm(state_in)],
        [
            sds((nz, 2, block), I32),
            sds((slots, experts), F32),
            sds((slots, 128), F32),
            sds((heads, share, hd), F32),
        ],
        [pltpu.VMEM((nz, 2, block), I32), pltpu.SemaphoreType.DMA],
    )
    attn_gain_2, moe_gain_2, router_t = attn_gain[None], moe_gain[None], jnp.transpose(router)
    prepared = [codes, sign, spare, start, attn_gain_2, moe_gain_2]
    qgs = [y_turn(qg, d + 1) for d, qg in enumerate(behind(qgs, kvs + logs + prepared))]
    share = hd // nz
    long = tok * ny
    *parts, c_row, c_col = call(
        functools.partial(update_kernel, nz, ny, heads, hd),
        place,
        [hbm(key_in), hbm(value_in), *kvs, *logs],
        [sds((heads * share + 16, hd), BF16)] * nz
        + [sds((heads, long), F32), sds((long, heads), F32)],
        [
            pltpu.VMEM((heads, long), F32),
            pltpu.VMEM((heads, hd, hd), BF16),
            pltpu.VMEM((16, hd), F32),
            pltpu.VMEM((2, tok, width), BF16),
            pltpu.SemaphoreType.DMA((2 * CUTS,)),
        ],
        limit=40,
            flops=2 * long * hd * hd * heads,
    )
    parts = [parts[0]] + [z_turn(parts[d], d) for d in range(1, nz)]
    *entering, last_rows = call(
        functools.partial(prefix_kernel, nz, heads, hd),
        place,
        [*parts, start],
        [sds((heads * share, hd), BF16)] * nz + [sds((heads, share, hd), F32)],
        [
            pltpu.VMEM((nz, heads * share + 16, hd), BF16),
            pltpu.VMEM((nz, heads * share, hd), BF16),
            pltpu.VMEM((heads, share, hd), F32),
        ],
    )
    entering = [entering[0]] + [z_turn(entering[d], d) for d in range(1, nz)]
    (mixed,) = call(
        functools.partial(attention_kernel, nz, ny, heads, hd),
        place,
        [
            hbm(key_in),
            hbm(value_in),
            hbm(query),
            hbm(gate_in),
            *[anywhere(x) for x in kvs],
            *[anywhere(x) for x in qgs],
            *entering,
            c_row,
            c_col,
            (attn_gain_2, pl.BlockSpec((1, width), lambda n, s: (0, s[1]))),
        ],
        [sds((long, width), BF16)],
        [pltpu.VMEM((long, width), BF16)] * 4
        + [pltpu.VMEM((heads, hd, hd), BF16), pltpu.SemaphoreType.DMA((4 * ny,))],
        limit=40,
            flops=4 * long * long * width,
    )

    def across(blocks):
        return [[y_turn(x, e) for x in blocks] for e in range(1, ny)]

    held = {0: [[mixed]] + across([mixed])}
    for d in near:
        held[d] = [[z_turn(mixed, d)]]
    free = behind([mixed], [held[near[0]][0][0]])[0]
    for d in near:
        held[d] += across(held[d][0])
    halves = [free[: long // 2], free[long // 2 :]]
    for d in distant:
        held[d] = [[z_turn(x, d) for x in halves]]
    for d in distant:
        held[d] += across(held[d][0])
    w_parts = [
        (w_out, pl.BlockSpec((width, cols), lambda n, s, d=d: (lax.rem(s[1] + ny - d, ny), 0)))
        for d in range(ny)
    ]
    given = []
    for group in ([0] + near, distant):
        last = group is distant
        dzs = {d: held[d][0] for d in group}
        blocks = [x for dy in range(ny) for d in group for x in held[d][dy]]
        half = nz * slots // 2
        outs = [sds((len(group), block, cols), BF16), sds((nz * slots, cols), F32)]
        if last:
            outs = [sds((half, cols), F32), sds((half, cols), BF16)]
            outs += [sds((nz // 2, block, cols), BF16)] * 2
        given = call(
            functools.partial(project_kernel, nz, ny, cap, dzs, last),
            place,
            [anywhere(x) for x in blocks]
            + w_parts
            + [row_r, row_base, codes]
            + list(given)
            + ([hbm(residual)] if last else []),
            outs,
            [pltpu.VMEM((ny, len(group), long, width), BF16)]
            + ([pltpu.VMEM((block, cols), BF16)] if last else [])
            + [pltpu.SemaphoreType.DMA((len(blocks) + 1,))],
            limit=40,
            flops=2 * len(group) * long * head_width * cols,
        )
    keep, send, keep_all, send_all = given
    for b in range(bits):
        received = swap(send, 1 << b)
        if b < bits - 1:
            part = keep.shape[0] // 2
            send = (keep[part:] + received[part:].astype(F32)).astype(BF16)
            keep = keep[:part] + received[:part].astype(F32)
    fits = cols % 128 == 0 and cols >= 512 and slots <= 128
    (rows_out,) = call(
        rows_kernel,
        place,
        [keep, received, moe_gain_2, router_t, sign, spare],
        [sds((slots, cols if fits else cols + 128), BF16)],
    )
    send_all = behind([send_all], [rows_out])[0]
    for b in range(bits):
        received_all = swap(send_all, 1 << b)
        if b < bits - 1:
            n = keep_all.shape[0] // 2
            both = keep_all.astype(F32) + received_all.astype(F32)
            send_all, keep_all = both[n:].astype(BF16), both[:n].astype(BF16)
    rows = share // ny
    last_rows = behind([last_rows], [rows_out])[0]
    final_rows = jnp.zeros((head_count, rows, hd), F32)
    for d in range(ny):
        sent = lax.dynamic_slice_in_dim(last_rows, (y + d) % ny * rows, rows, 1)
        got = sent if d == 0 else y_turn(sent, d)
        final_rows = lax.dynamic_update_slice_in_dim(
            final_rows, got, (y - d) % ny * heads, 0
        )

    in_vmem = pl.BlockSpec(memory_space=pltpu.VMEM)

    def up(group, blocks, state, first, last):
        outs = [sds((slots, units), F32)] * 2 + [sds((1, cols), F32)]
        if last:
            outs = [sds((slots, units), BF16), sds((slots, 128), F32)]
        return call(
            functools.partial(up_kernel, nz, ny, group, first, last, features),
            place,
            blocks + list(state) + [anywhere(w_gate), anywhere(w_up), spare],
            outs,
            [pltpu.VMEM((len(group), units, cols), BF16)] * 2
            + [pltpu.SemaphoreType.DMA((2 * len(group),))],
            limit=40,
            flops=4 * len(group) * slots * units * cols,
        )

    def down(group, blocks, state, first, last):
        ahead = groups[-1] if first else []
        outs = [sds((slots, cols), F32)]
        outs += [sds((len(ahead), units, cols), BF16)] if ahead else []
        weights = [anywhere(w_down)]
        if last:
            outs = [sds((ret_rows, cols), BF16)] * nz
            weights = [(fetched["down"], in_vmem), weight, padded[:, None], own_base.T]
        state = call(
            functools.partial(down_kernel, nz, ny, cap, group, ahead, first, last),
            place,
            blocks + list(state) + weights,
            outs,
            []
            if last
            else [
                pltpu.VMEM((len(group), units, cols), BF16),
                pltpu.SemaphoreType.DMA((len(group) + len(ahead),)),
            ],
            limit=40,
            flops=2 * len(group) * slots * units * cols,
            held=1 if ahead else 0,
        )
        if ahead:
            fetched["down"] = state[1]
        return state if last else state[:1]

    fetched = {}
    if not fits:
        arrived = gather_z(rows_out)
        gather_y(arrived, [])
        order = jnp.stack([(z - dz) % nz * ny + (y - dy) % ny for dz, dy in places])
        at = jnp.argsort(order)
        rows_all = jnp.take(jnp.stack([arrived[p] for p in places]), at, axis=0)
        stats = jnp.sum(rows_all[:, :, cols:].astype(F32), axis=0)
        rows_all = jnp.swapaxes(rows_all[:, :, :cols], 0, 1).reshape(slots, features)
        inverse = lax.rsqrt(jnp.sum(stats[:, :3], axis=1) / features + EPS)[:, None]
        gate = mm(rows_all, w_gate[0], NT) * inverse
        hidden = (gate * sigmoid(gate) * (mm(rows_all, w_up[0], NT) * inverse)).astype(BF16)
        weight = sigmoid(jnp.sum(stats[:, 3:6], axis=1)[:, None] * inverse)
        weight = jnp.broadcast_to(weight, (slots, 128))
    else:
        hidden, weight = stages(up, rows_out, groups)
    state = stages(down, hidden, [groups[0] + groups[1], groups[2]])
    stream, picks = call(
        functools.partial(stream_kernel, cap),
        place,
        [keep_all[0], received_all[0], residual, codes, ret_r, ret_base],
        [sds((block, cols), F32), sds((nz * ret_rows, block), BF16)],
    )
    returned = [state[0]] + [swap(state[r], r) for r in range(1, nz)]
    (layer_out,) = call(
        functools.partial(combine_kernel, nz),
        place,
        returned + [stream, picks],
        [sds((block, cols), BF16)],
        [pltpu.VMEM((nz * ret_rows, cols), BF16)],
    )
    return layer_out, final_rows


def solution(mesh):
    in_specs = (
        P("exp", "seq"),
        P("seq", "exp"),
        P("seq", "exp"),
        P("seq", "exp"),
        P("seq", "exp"),
        P("seq", "exp"),
        P("exp", None, None),
        P("exp"),
        P("exp", "seq"),
        P("seq"),
        P("seq", None),
        P("exp", "seq", None),
        P("exp", "seq", None),
        P("exp", None, "seq"),
        P("exp", None),
        P(),
    )
    out_specs = (P("exp", "seq"), P("exp", "seq", None))
    return jax.shard_map(local, mesh=mesh, in_specs=in_specs, out_specs=out_specs, check_vma=False)
```
